32 devices in a mesh: ctx: 8 (over z, y), wt: 4 (over x, core).
Axes of the slice: x: 2, y: 2, z: 4, core: 2. Of those that a mesh axis runs over, the one named last changes fastest.
Arguments:
- tokens: bfloat16 [4, 1024, 1536], P('wt', 'ctx'), may hold values from -6 to 6
- cotangent: bfloat16 [4, 1024, 1536], P('wt', 'ctx'), may hold values from -6 to 6
- seq_lengths: int32 [4, 1], P('wt'), may hold values from 1024 to 1024, as said below
- block_deal: int32 [4, 8, 1], P('wt'), may hold values from 0 to 7, as said below
- routes: int32 [2, 4, 1024, 2], P(None, 'wt', 'ctx'), may hold values from 0 to 7, all different within a row; in each aligned block of 128 rows (0 to 127, 128 to 255, ..., all dimensions but the last counted through in order) at most 48 rows name the same one
- attention_gain: bfloat16 [2, 1536], P(None, 'wt'), may hold values from 0.5 to 1.5
- query_weight: bfloat16 [2, 1536, 1536], P(None, 'wt'), may hold values from -0.15625 to 0.15625
- key_weight: bfloat16 [2, 1536, 512], P(None, 'wt'), may hold values from -0.15625 to 0.15625
- value_weight: bfloat16 [2, 1536, 512], P(None, 'wt'), may hold values from -0.15625 to 0.15625
- out_weight: bfloat16 [2, 1536, 1536], P(None, 'wt'), may hold values from -1.25 to 1.25
- mixture_gain: bfloat16 [2, 1536], P(None, 'wt'), may hold values from 0.5 to 1.5
- router_weight: bfloat16 [2, 1536, 8], P(None, 'wt'), may hold values from -0.099609375 to 0.099609375
- gate_weight: bfloat16 [2, 8, 1536, 1024], P(None, 'ctx', None, 'wt'), may hold values from -0.15625 to 0.15625
- up_weight: bfloat16 [2, 8, 1536, 1024], P(None, 'ctx', None, 'wt'), may hold values from -0.15625 to 0.15625
- down_weight: bfloat16 [2, 8, 1024, 1536], P(None, 'ctx', 'wt'), may hold values from -0.375 to 0.375
Outputs:
- block_output: bfloat16 [4, 1024, 1536], P('wt', 'ctx')
- input_grad: float32 [4, 1024, 1536], P('wt', 'ctx')
- attention_gain_grad: float32 [2, 1536], P(None, 'wt')
- query_grad: float32 [2, 1536, 1536], P(None, 'wt')
- key_grad: float32 [2, 1536, 512], P(None, 'wt')
- value_grad: float32 [2, 1536, 512], P(None, 'wt')
- out_grad: float32 [2, 1536, 1536], P(None, 'wt')
- mixture_gain_grad: float32 [2, 1536], P(None, 'wt')
- router_grad: float32 [2, 1536, 8], P(None, 'wt')
- gate_grad: float32 [2, 8, 1536, 1024], P(None, 'ctx', None, 'wt')
- up_grad: float32 [2, 8, 1536, 1024], P(None, 'ctx', None, 'wt')
- down_grad: float32 [2, 8, 1024, 1536], P(None, 'ctx', 'wt')
The draws below stay inside these ranges and needn't reach their ends.
Inputs may be any that keep to these rules, and one draw needn't show every extreme that they name: `seq_lengths`: a group's lengths sum to 1024, each is at least 1024, and one is exactly 1024. `block_deal`: each group's table is a permutation of the 8 stream blocks; devices 0, 4 and 7 hold blocks 0, 2 and 1 in their first slot. `routes`: each row names two different experts; among the rows of one device no expert is named more than 48 times, a bound that some block reaches.
All inputs are finite; a program needn't handle non-finite values.
Results may differ from the reference program's by a relative error of at most 0.03.
Values may be sent and summed in bfloat16 or wider, within the bound.
No kernel may reach another device: no remote copies, remote signals or barrier semaphores. Data moves between devices by JAX's collectives and lax.ppermute only.
A program may use at most 256 MiB of HBM per device.

```python
import math
import jax
import jax.numpy as jnp
import numpy as np
from jax import lax

HEADS = 24
KV_HEADS = 8
HEAD = 64
D = 1536
KVW = 512
FF = 1024
LAYERS = 2
TOK_DEV = 128
BLK = 128
MINLEN = 1024
MAXLEN = 4096
EXPERTS = 8
CAP = 48
BPD = 1
GTOK = 1024
GROUPS = 4
SEQS = 1
LONGEST = 1024
SPARE = 0
N_CTX = 8


def draw_seq_lengths(key, part):
    key = jax.random.fold_in(key, 11)
    others_count = SEQS - 1

    def one(group_key):
        first_key, second_key = jax.random.split(group_key)
        weights = jax.random.randint(first_key, (max(others_count, 1),), 1, 5)
        adds = SPARE * weights // jnp.sum(weights)
        adds = adds.at[0].add(SPARE - jnp.sum(adds))
        others = (MINLEN + adds)[:others_count].astype(jnp.int32)
        joined = jnp.concatenate([jnp.full((1,), LONGEST, jnp.int32), others])
        order = jax.random.permutation(second_key, SEQS)
        return joined[order].astype(jnp.int32)
    return jax.vmap(one)(jax.random.split(key, GROUPS))


def draw_block_deal(key, part):
    key = jax.random.fold_in(key, 23)
    count = N_CTX * BPD
    middle = N_CTX // 2 * BPD
    last = (N_CTX - 1) * BPD

    def one(group_key):
        others = (3 + jax.random.permutation(group_key, count - 3)).astype(jnp.int32)
        flat = jnp.concatenate([jnp.zeros((1,), jnp.int32), others[:middle - 1], jnp.full((1,), 2, jnp.int32), others[middle - 1:last - 2], jnp.ones((1,), jnp.int32), others[last - 2:]])
        return flat.reshape(N_CTX, BPD)
    return jax.vmap(one)(jax.random.split(key, GROUPS))


def steps_of(stream_key, extent, shards, smallest, high):
    def one(axis_at, shards_of):
        draws = jax.random.uniform(jax.random.fold_in(jax.random.fold_in(stream_key, 6), axis_at), (shards_of,), jnp.float32, smallest / len(shards), high / len(shards))
        return jnp.repeat(jnp.exp(draws), extent[axis_at] // shards_of).reshape((-1,) + (1,) * (len(extent) - axis_at - 1))

    loudness = one(*shards[0])
    for cut in shards[1:]:
        loudness = loudness * one(*cut)
    return loudness


def shared_out(rng, own, number, rows, count, top, limit, skew):
    ranking = jax.random.permutation(rng, count)
    crowded, ordinary = load_shares(count, rows * top, limit, skew, True), load_shares(count, rows * top, limit, skew, False)
    places = jnp.arange(count)

    def named(sizes, rotation):
        used = int((sizes > 0).sum())
        fixed = max(1, used // 4)
        passed = fixed + (places - fixed + rotation * (used - fixed)) % max(1, count - fixed)
        return jnp.zeros((count,), jnp.int32).at[ranking[jnp.where(places < fixed, places, passed)]].set(jnp.asarray(sizes, jnp.int32))

    sizes = jnp.where(number % 4 == 0, named(crowded, number // 4), named(ordinary, number - number // 4 - 1))
    mixed = jax.random.permutation(jax.random.fold_in(own, 3), count)
    source_of, sink = mixed[0:count // 2 * 2:2], mixed[1:count // 2 * 2:2]
    room = jnp.minimum(sizes[source_of] - 1, limit - sizes[sink]) // 2
    room = jnp.where((source_of == ranking[0]) | (sink == ranking[0]) | (sizes[sink] == 0), 0, jnp.maximum(room, 0))
    passed = jax.random.randint(jax.random.fold_in(own, 4), (count // 2,), 0, 1 << 20) % (room + 1)
    sizes = sizes.at[source_of].add(-passed).at[sink].add(passed)
    members = jnp.searchsorted(jnp.cumsum(sizes), jnp.arange(rows * top), side="right").astype(jnp.int32)
    listing = members.reshape(top, rows).T
    listing = listing[jax.random.permutation(jax.random.fold_in(own, 1), rows)]
    rotation = jax.random.randint(jax.random.fold_in(own, 2), (rows, 1), 0, top)
    return jnp.take_along_axis(listing, (jnp.arange(top)[None, :] + rotation) % top, axis=1)


def load_shares(count, total, limit, slope, full):
    weights = [(1 << 20) // math.isqrt(standing ** slope) + 1 for standing in range(1, count + 1)]
    largest = limit if full else min(limit, max(-(-total // count), total * weights[0] // sum(weights)))
    least = 1 if total - largest >= count - 1 else 0
    given, surplus = [largest] + [least] * (count - 1), total - largest - least * (count - 1)
    while surplus > 0:
        movable = [i for i in range(1, count) if given[i] < largest] or [i for i in range(1, count) if given[i] < limit]
        mass, budget = sum([weights[i] for i in movable]), surplus
        for i in movable:
            addition = min(limit - given[i], max(1, budget * weights[i] // mass), surplus)
            given[i] = given[i] + addition
            surplus = surplus - addition
    return np.array(given)


def gaussian(rng, shape, spread, limit, pieces=(), kind=jnp.bfloat16):
    factor_of = steps_of(rng, shape, pieces, -0.22, 0.18) if pieces else 1.0
    drawn = jax.random.normal(rng, shape, jnp.float32) * spread * factor_of
    return jnp.minimum(jnp.maximum(drawn, -limit), limit).astype(kind)


def setup_inputs(seed: int = 0) -> dict:
    streams_of = jax.random.split(jax.random.key(seed), 16)
    tokens = gaussian(streams_of[0], (GROUPS, GTOK, D), 1.0, 6.0, ((0, 4), (1, 8)))
    cotangent = gaussian(streams_of[1], (GROUPS, GTOK, D), 1.0, 6.0, ((0, 4), (1, 8)))
    seq_lengths = draw_seq_lengths(jax.random.fold_in(streams_of[15], 71), 0)
    block_deal = draw_block_deal(jax.random.fold_in(streams_of[15], 71), 0)
    routes_keys = jax.random.split(jax.random.fold_in(streams_of[4], 1), LAYERS * GROUPS * GTOK // TOK_DEV)
    routes_turns = jax.random.permutation(jax.random.fold_in(streams_of[4], 3), LAYERS * GROUPS * GTOK // TOK_DEV)
    routes = jax.vmap(lambda own, number: shared_out(jax.random.fold_in(streams_of[4], 2), own, number, TOK_DEV, EXPERTS, 2, CAP, 1))(routes_keys, routes_turns).reshape((LAYERS, GROUPS, GTOK, 2))
    attention_gain = jnp.clip(1.0 + 0.1 * jax.random.normal(streams_of[5], (LAYERS, D), jnp.float32), 0.5, 1.5).astype(jnp.bfloat16)
    query_weight = gaussian(streams_of[6], (LAYERS, D, D), D ** -0.5, 0.15625, ((1, 4),))
    key_weight = gaussian(streams_of[7], (LAYERS, D, KVW), D ** -0.5, 0.15625, ((1, 4),))
    value_weight = gaussian(streams_of[8], (LAYERS, D, KVW), D ** -0.5, 0.15625, ((1, 4),))
    out_weight = gaussian(streams_of[9], (LAYERS, D, D), (max(4, D // 64)) ** -0.5, 1.25, ((1, 4),))
    mixture_gain = jnp.clip(1.0 + 0.1 * jax.random.normal(streams_of[10], (LAYERS, D), jnp.float32), 0.5, 1.5).astype(jnp.bfloat16)
    router_weight = gaussian(streams_of[11], (LAYERS, D, EXPERTS), 0.018, 0.099609375, ((1, 4),))
    gate_weight = gaussian(streams_of[12], (LAYERS, EXPERTS, D, FF), D ** -0.5, 0.15625, ((1, 8), (3, 4)))
    up_weight = gaussian(streams_of[13], (LAYERS, EXPERTS, D, FF), D ** -0.5, 0.15625, ((1, 8), (3, 4)))
    down_weight = gaussian(streams_of[14], (LAYERS, EXPERTS, FF, D), (FF // 4) ** -0.5, 0.375, ((1, 8), (2, 4)))
    return {"tokens": tokens, "cotangent": cotangent, "seq_lengths": seq_lengths, "block_deal": block_deal, "routes": routes, "attention_gain": attention_gain, "query_weight": query_weight, "key_weight": key_weight, "value_weight": value_weight, "out_weight": out_weight, "mixture_gain": mixture_gain, "router_weight": router_weight, "gate_weight": gate_weight, "up_weight": up_weight, "down_weight": down_weight}


EPS = 1e-05
NEG = -1e+30

@jax.custom_vjp
def low(v):
    return lax.optimization_barrier(v.astype(jnp.bfloat16)).astype(jnp.float32)

@jax.custom_vjp
def low_back(v):
    return v

def low_keep(v):
    return (low(v), None)

def low_pass(kept, grad):
    return (grad,)

def back_keep(v):
    return (v, None)

def back_low(kept, grad):
    return (low(grad),)
low.defvjp(low_keep, low_pass)
low_back.defvjp(back_keep, back_low)

def highest(left, right):
    return jnp.dot(left, right, precision=lax.Precision.HIGHEST, preferred_element_type=jnp.float32)

def rms_scale(rows, gain):
    return rows * lax.rsqrt(lax.optimization_barrier(jnp.mean(rows * rows, axis=-1, keepdims=True)) + EPS) * gain

def stream_positions(table):
    offsets = jnp.arange(BLK, dtype=jnp.int32)
    return (table[:, :, None] * BLK + offsets[None, None, :]).reshape(-1).astype(jnp.int32)

def sequence_ids(positions, seq_row):
    ends = jnp.cumsum(seq_row).astype(jnp.int32)
    return lax.optimization_barrier(jnp.sum((positions[:, None] >= ends[None, :]).astype(jnp.int32), axis=1)).astype(jnp.int32)

def expert_slots(route):
    flat = route.reshape(N_CTX, 2 * TOK_DEV).astype(jnp.int32)
    onehot = (flat[:, :, None] == jnp.arange(EXPERTS, dtype=jnp.int32)[None, None, :]).astype(jnp.int32)
    rank = lax.optimization_barrier(jnp.sum((jnp.cumsum(onehot, axis=1) - onehot) * onehot, axis=2)).astype(jnp.int32)
    source = jnp.arange(N_CTX, dtype=jnp.int32)[:, None]
    return (flat * (N_CTX * CAP) + source * CAP + rank).reshape(-1).astype(jnp.int32)

def attend(queries, keys, values, stream_seq):
    block = min(512, GTOK)
    span = min(GTOK, MAXLEN + block)
    ratio = HEADS // KV_HEADS
    scale = HEAD ** (-0.5)

    def one(index):
        first = (index * block).astype(jnp.int32)
        kstart = jnp.clip(first + block - span, 0, GTOK - span).astype(jnp.int32)
        query_rows = lax.dynamic_slice_in_dim(queries, first, block, 0).reshape(block, KV_HEADS, ratio, HEAD)
        key_rows = lax.dynamic_slice_in_dim(keys, kstart, span, 0).reshape(span, KV_HEADS, HEAD)
        value_rows = lax.dynamic_slice_in_dim(values, kstart, span, 0).reshape(span, KV_HEADS, HEAD)
        query_pos = first + jnp.arange(block, dtype=jnp.int32)
        key_pos = kstart + jnp.arange(span, dtype=jnp.int32)
        query_seq = lax.dynamic_slice_in_dim(stream_seq, first, block, 0)
        key_seq = lax.dynamic_slice_in_dim(stream_seq, kstart, span, 0)
        allowed = (query_seq[:, None] == key_seq[None, :]) & (key_pos[None, :] <= query_pos[:, None])
        scores = low_back(jnp.einsum('tgrd,kgd->grtk', query_rows, key_rows, precision=lax.Precision.HIGHEST) * scale)
        scores = jnp.where(allowed[None, None], scores, NEG)
        top = lax.optimization_barrier(jnp.max(scores, axis=-1, keepdims=True))
        weights = jnp.where(allowed[None, None], jnp.exp(scores - top), 0.0)
        total = lax.optimization_barrier(jnp.sum(weights, axis=-1, keepdims=True))
        result = jnp.einsum('grtk,kgd->grtd', low(weights), value_rows, precision=lax.Precision.HIGHEST) / total
        return result.transpose(2, 0, 1, 3).reshape(block, D)
    return lax.map(jax.checkpoint(one), jnp.arange(GTOK // block, dtype=jnp.int32)).reshape(GTOK, D)

def block_step(state, layout, route, slots, weights):
    dealt, order, stream_seq = layout
    gain_one, query_matrix, key_matrix, value_matrix, out_matrix, gain_two, router_matrix, gate_stack, up_stack, down_stack = weights
    normed = low(rms_scale(state, gain_one))
    queries = low_back(low(highest(normed, query_matrix)))
    keys = low_back(low(highest(normed, key_matrix)))
    values = low_back(low(highest(normed, value_matrix)))
    attended = attend(queries[order], keys[order], values[order], stream_seq)[dealt]
    attended = low_back(low(attended))
    middle = state + low_back(highest(attended, out_matrix))
    mixed = low(rms_scale(middle, gain_two))
    probs = jax.nn.softmax(highest(mixed, router_matrix), axis=-1)
    picked = jnp.take_along_axis(probs, route, axis=1)
    gates = picked / lax.optimization_barrier(jnp.sum(picked, axis=1, keepdims=True))
    rows = jnp.arange(2 * GTOK, dtype=jnp.int32) // 2
    buffer = jnp.zeros((EXPERTS * N_CTX * CAP, D), jnp.float32).at[slots].set(mixed[rows])
    buffer = low_back(buffer).reshape(EXPERTS, N_CTX * CAP, D)
    gate_value = low_back(jnp.einsum('erd,edf->erf', buffer, gate_stack, precision=lax.Precision.HIGHEST))
    up_value = low_back(jnp.einsum('erd,edf->erf', buffer, up_stack, precision=lax.Precision.HIGHEST))
    inner = low(jax.nn.silu(gate_value) * up_value)
    produced = low_back(low(jnp.einsum('erf,efd->erd', inner, down_stack, precision=lax.Precision.HIGHEST))).reshape(-1, D)
    expert_out = produced[slots].reshape(GTOK, 2, D)
    return middle + lax.optimization_barrier(jnp.sum(gates[:, :, None] * expert_out, axis=1))

def reference(tokens, cotangent, seq_lengths, block_deal, routes, attention_gain, query_weight, key_weight, value_weight, out_weight, mixture_gain, router_weight, gate_weight, up_weight, down_weight):
    params = tuple((weight.astype(jnp.float32) for weight in (attention_gain, query_weight, key_weight, value_weight, out_weight, mixture_gain, router_weight, gate_weight, up_weight, down_weight)))
    layouts = []
    for group in range(GROUPS):
        dealt = stream_positions(block_deal[group])
        order = jnp.zeros((GTOK,), jnp.int32).at[dealt].set(jnp.arange(GTOK, dtype=jnp.int32))
        stream_seq = sequence_ids(jnp.arange(GTOK, dtype=jnp.int32), seq_lengths[group])
        layouts.append((dealt, order, stream_seq))
    slot_table = [[expert_slots(routes[layer, group]) for group in range(GROUPS)] for layer in range(LAYERS)]

    def forward(inputs, weights):
        results = []
        for group in range(GROUPS):
            state = inputs[group]
            for layer in range(LAYERS):
                state = block_step(state, layouts[group], routes[layer, group].astype(jnp.int32), slot_table[layer][group], tuple((weight[layer] for weight in weights)))
            results.append(state)
        return jnp.stack(results)
    output, pull = jax.vjp(forward, tokens.astype(jnp.float32), params)
    grad_input, grads = pull(cotangent.astype(jnp.float32))
    return (output.astype(jnp.bfloat16), grad_input, grads[0], grads[1], grads[2], grads[3], grads[4], grads[5], grads[6], grads[7], grads[8], grads[9])
```

```python
import functools

import jax
import jax.numpy as jnp
from jax import lax
from jax.experimental import pallas as pl
from jax.experimental.pallas import tpu as pltpu
from jax.sharding import PartitionSpec as P

HEADS = 24
KV_HEADS = 8
HEAD = 64
BLK = 128


EPS = 1e-05
NEG = -1e30


def rms_scale(rows, gain):
    return rows * lax.rsqrt(jnp.mean(rows * rows, axis=-1, keepdims=True) + EPS) * gain


def stream_positions(table, width):
    offsets = jnp.arange(width, dtype=jnp.int32)
    return (table[:, :, None] * width + offsets[None, None, :]).reshape(-1)


def sequence_ids(positions, seq_row):
    ends = jnp.cumsum(seq_row)
    return jnp.sum((positions[:, None] >= ends[None, :]).astype(jnp.int32), axis=1)


def outer_rows(left, right):
    return lax.dot_general(
        left, right, (((0,), (0,)), ((), ())), preferred_element_type=jnp.float32
    )


def times_transposed(left, right):
    return lax.dot_general(
        left, right, (((1,), (1,)), ((), ())), preferred_element_type=jnp.float32
    )


def unchanged(state):
    return state


def times(left, right, a, b):
    return lax.dot_general(left, right, (((a,), (b,)), ((), ())), preferred_element_type=jnp.float32)


def causal_mask(keys_count, span):
    key_at = lax.broadcasted_iota(jnp.int32, (span, span), 0)
    query_at = lax.broadcasted_iota(jnp.int32, (span, span), 1)
    return key_at <= query_at


def attend_kernel(rep, head, span, owner_ref, qkv_ref, sent_ref, exact_ref, log_ref):
    tokens = qkv_ref.shape[1]
    width = rep * head
    blocks = span // BLK
    scale = head ** (-0.5)
    mask = causal_mask(span, span)
    for part in range(tokens // span):
        lanes = pl.ds(part * span, span)
        seen = (part + 1) * span
        keys = qkv_ref[width : width + head, :seen]
        values = qkv_ref[width + head :, :seen]
        for h in range(rep):
            rows = slice(h * head, (h + 1) * head)
            scores = times(keys, qkv_ref[rows, lanes], 0, 0) * scale
            last = jnp.where(mask, scores[seen - span :], NEG)
            top = jnp.max(last, axis=0, keepdims=True)
            if part:
                top = jnp.maximum(top, jnp.max(scores[: seen - span], axis=0, keepdims=True))
            last = jnp.exp(last - top)
            weights = last if part == 0 else jnp.concatenate([jnp.exp(scores[: seen - span] - top), last], axis=0)
            total = jnp.sum(weights, axis=0, keepdims=True)
            result = times(values, weights.astype(jnp.bfloat16), 1, 0) / total
            exact_ref[rows, lanes] = result
            log_ref[h : h + 1, lanes] = top + jnp.log(total)
            for b in range(blocks):
                sent_ref[owner_ref[part * blocks + b], rows, :] = result[:, b * BLK : (b + 1) * BLK].astype(jnp.bfloat16)


def attend_back_kernel(rep, head, span, owner_ref, qkv_ref, exact_ref, log_ref, grad_ref, whole_ref, sent_ref, grad_all, keys_sum, values_sum):
    tokens = qkv_ref.shape[1]
    width = rep * head
    blocks = span // BLK
    scale = head ** (-0.5)
    mask = causal_mask(span, span)
    for block in range(tokens // BLK):
        grad_all[:, block * BLK : (block + 1) * BLK] = grad_ref[owner_ref[block]]
    keys_sum[...] = jnp.zeros_like(keys_sum)
    values_sum[...] = jnp.zeros_like(values_sum)
    for part in range(tokens // span):
        lanes = pl.ds(part * span, span)
        seen = (part + 1) * span
        keys = qkv_ref[width : width + head, :seen]
        values = qkv_ref[width + head :, :seen]
        for h in range(rep):
            rows = slice(h * head, (h + 1) * head)
            queries = qkv_ref[rows, lanes]
            grads = grad_all[rows, lanes]
            delta = jnp.sum(grads.astype(jnp.float32) * exact_ref[rows, lanes], axis=0, keepdims=True)
            scores = times(keys, queries, 0, 0) * scale
            probs = jnp.exp(scores - log_ref[h : h + 1, lanes])
            last = jnp.where(mask, probs[seen - span :], 0.0)
            probs = last if part == 0 else jnp.concatenate([probs[: seen - span], last], axis=0)
            pulled = times(values, grads, 0, 0)
            slopes = (probs * (pulled - delta)).astype(jnp.bfloat16)
            back = (times(keys, slopes, 1, 0) * scale).astype(jnp.bfloat16)
            whole_ref[rows, lanes] = back
            for b in range(blocks):
                sent_ref[owner_ref[part * blocks + b], rows, :] = back[:, b * BLK : (b + 1) * BLK]
            keys_sum[:, :seen] += times(queries, slopes, 1, 1)
            values_sum[:, :seen] += times(grads, probs.astype(jnp.bfloat16), 1, 1)
    keys_low = (keys_sum[...] * scale).astype(jnp.bfloat16)
    values_low = values_sum[...].astype(jnp.bfloat16)
    whole_ref[width : width + head, :] = keys_low
    whole_ref[width + head :, :] = values_low
    for block in range(tokens // BLK):
        cut = slice(block * BLK, (block + 1) * BLK)
        sent_ref[owner_ref[block], width : width + head, :] = keys_low[:, cut]
        sent_ref[owner_ref[block], width + head :, :] = values_low[:, cut]


def attend(owner_of, qkv, rep, head, count):
    tokens = qkv.shape[1]
    span = min(256, tokens)
    pairs = rep * tokens * (tokens + span) // 2
    return pl.pallas_call(
        functools.partial(attend_kernel, rep, head, span),
        out_shape=(
            jax.ShapeDtypeStruct((count, rep * head, BLK), jnp.bfloat16),
            jax.ShapeDtypeStruct((rep * head, tokens), jnp.float32),
            jax.ShapeDtypeStruct((rep, tokens), jnp.float32),
        ),
        in_specs=[pl.BlockSpec(memory_space=pltpu.SMEM), pl.BlockSpec(memory_space=pltpu.VMEM)],
        out_specs=(pl.BlockSpec(memory_space=pltpu.VMEM),) * 3,
        compiler_params=pltpu.CompilerParams(vmem_limit_bytes=40 * 2**20),
        cost_estimate=pl.CostEstimate(flops=4 * head * pairs, bytes_accessed=4 * 2**20, transcendentals=pairs),
        name="attend",
    )(owner_of, qkv)


def attend_back(owner_of, qkv, exact, log_total, grads, rep, head, count):
    tokens = qkv.shape[1]
    span = min(256, tokens)
    pairs = rep * tokens * (tokens + span) // 2
    rows = qkv.shape[0]
    return pl.pallas_call(
        functools.partial(attend_back_kernel, rep, head, span),
        out_shape=(
            jax.ShapeDtypeStruct((rows, tokens), jnp.bfloat16),
            jax.ShapeDtypeStruct((count, rows, BLK), jnp.bfloat16),
        ),
        in_specs=[pl.BlockSpec(memory_space=pltpu.SMEM)] + [pl.BlockSpec(memory_space=pltpu.VMEM)] * 4,
        out_specs=(pl.BlockSpec(memory_space=pltpu.VMEM),) * 2,
        scratch_shapes=[
            pltpu.VMEM((rep * head, tokens), jnp.bfloat16),
            pltpu.VMEM((head, tokens), jnp.float32),
            pltpu.VMEM((head, tokens), jnp.float32),
        ],
        compiler_params=pltpu.CompilerParams(vmem_limit_bytes=40 * 2**20),
        cost_estimate=pl.CostEstimate(flops=10 * head * pairs, bytes_accessed=6 * 2**20, transcendentals=pairs),
        name="attend_back",
    )(owner_of, qkv, exact, log_total, grads)


def swap(x, axis, count, mask):
    return lax.ppermute(x, axis, [(i, i ^ mask) for i in range(count)])


def wt_gather(own):
    far = swap(own, "wt", 4, 2)
    near = swap(own, "wt", 4, 1)
    return (own, near, far, swap(far, "wt", 4, 1))


def wt_scatter_sum(pieces):
    got = swap(jnp.stack([pieces[1], pieces[3]]).astype(jnp.bfloat16), "wt", 4, 1).astype(jnp.float32)
    kept = pieces[0] + got[0]
    far = swap((pieces[2] + got[1]).astype(jnp.bfloat16), "wt", 4, 2)
    return kept + far.astype(jnp.float32)


def wt_exchange(slices, me):
    def cut(m):
        return lax.dynamic_index_in_dim(slices, me ^ m, 0, keepdims=False)

    far = swap(jnp.stack([cut(2), cut(3)]), "wt", 4, 2)
    near = swap(jnp.stack([cut(1), far[1]]), "wt", 4, 1)
    return (cut(0), near[0], far[0], near[1])


def in_order(pieces, me, axis):
    own, near, far, last = pieces
    odd, high = me % 2 == 1, me >= 2
    low = (jnp.where(odd, near, own), jnp.where(odd, own, near))
    up = (jnp.where(odd, last, far), jnp.where(odd, far, last))
    first = [jnp.where(high, b, a) for a, b in zip(low, up)]
    second = [jnp.where(high, a, b) for a, b in zip(low, up)]
    return jnp.concatenate(first + second, axis=axis)


def tie(*arrays):
    return lax.optimization_barrier(arrays)


def ring_gather(x, me, count, place):
    ring = list(range(0, count, 2)) + list(range(count - 1, 0, -2))
    around = jnp.asarray([[ring[(ring.index(i) + k) % count] for k in range(count)] for i in range(count)], jnp.int32)
    spots = place[lax.dynamic_index_in_dim(around, me, 0, keepdims=False)].astype(jnp.uint32)
    right = [(ring[i], ring[(i + 1) % count]) for i in range(count)]
    left = [(b, a) for a, b in right]
    full = jnp.zeros((count,) + x.shape, x.dtype)

    def put(full, block, offset):
        return lax.dynamic_update_index_in_dim(full, block, spots[offset % count], 0)

    full = put(full, x, 0)
    ahead = behind = x
    for step in range(1, count // 2):
        ahead, behind = lax.ppermute(ahead, "ctx", right), lax.ppermute(behind, "ctx", left)
        full = put(put(full, ahead, -step), behind, step)
    half = x.shape[0] // 2
    last = jnp.concatenate([lax.ppermute(ahead[:half], "ctx", right), lax.ppermute(behind[half:], "ctx", left)])
    return put(full, last, count // 2)


def all_to_all(x):
    return lax.all_to_all(x, "ctx", split_axis=0, concat_axis=0, tiled=True)


def rms_back(rows, gain, grad):
    scale = lax.rsqrt(jnp.mean(rows * rows, axis=-1, keepdims=True) + EPS)
    unit = rows * scale
    pulled = grad * gain
    return scale * (pulled - unit * jnp.mean(pulled * unit, axis=-1, keepdims=True)), grad * unit


def by_heads(mesh, tokens, cotangent, seq_lengths, block_deal, *rest):
    return (
        mesh.shape["ctx"] == KV_HEADS
        and mesh.shape["wt"] == 4
        and seq_lengths.shape[1] == 1
        and block_deal.shape[2] == 1
        and tokens.shape[1] == BLK
    )


def local_heads(
    mesh,
    tokens,
    cotangent,
    seq_lengths,
    block_deal,
    routes,
    attention_gain,
    query_weight,
    key_weight,
    value_weight,
    out_weight,
    mixture_gain,
    router_weight,
    gate_weight,
    up_weight,
    down_weight,
):
    n_ctx = mesh.shape["ctx"]
    rows = tokens.shape[1]
    width = tokens.shape[2]
    layers = query_weight.shape[0]
    experts = router_weight.shape[2]
    capacity = 3 * rows // experts
    rep = HEADS // KV_HEADS
    wide = rep * HEAD
    part = width // 4
    hidden = gate_weight.shape[3]
    ctx = lax.axis_index("ctx")
    wt = lax.axis_index("wt").astype(jnp.uint32)
    table = block_deal[0, :, 0]
    devices = jnp.arange(n_ctx, dtype=jnp.int32)
    owner_of = jnp.sum(jnp.where(table[None, :] == devices[:, None], devices[None, :], 0), axis=1)

    expert_ids = jnp.arange(experts, dtype=jnp.int32)
    chosen = routes[:, 0]
    flat = chosen.reshape(layers, 2 * rows)
    onehot = flat[:, :, None] == expert_ids
    earlier = jnp.tril(jnp.ones((2 * rows, 2 * rows), jnp.bfloat16), -1)
    rank = jnp.einsum("ij,lje->lie", earlier, onehot.astype(jnp.bfloat16), preferred_element_type=jnp.float32)
    rank = jnp.sum(jnp.where(onehot, rank, 0.0), axis=2).astype(jnp.int32)
    slots = (flat * capacity + rank).reshape(layers, rows, 2).transpose(0, 2, 1)
    place = (slots[..., None] == jnp.arange(experts * capacity, dtype=jnp.int32)).astype(jnp.bfloat16)
    named = (chosen.transpose(0, 2, 1)[..., None] == expert_ids).astype(jnp.float32)

    def head_rows(layer):
        return [
            lax.dynamic_slice_in_dim(query_weight[layer], ctx * wide, wide, 1).T,
            lax.dynamic_slice_in_dim(key_weight[layer], ctx * HEAD, HEAD, 1).T,
            lax.dynamic_slice_in_dim(value_weight[layer], ctx * HEAD, HEAD, 1).T,
            router_weight[layer].T,
            attention_gain[layer][None],
            mixture_gain[layer][None],
            jnp.zeros((14 - experts, part), jnp.bfloat16),
        ]

    lanes = wide + 2 * HEAD
    deep = lanes + 16
    head_own = jnp.concatenate(sum([head_rows(layer) for layer in range(layers)], []), axis=0)
    head_all = in_order(wt_gather(head_own), wt, 1).reshape(layers, deep, width)
    token_all = ring_gather(tokens[0], ctx, n_ctx, table).reshape(n_ctx * rows, width)

    def far_start(own):
        return swap(own, "wt", 4, 2), own

    def near_finish(far, own):
        return (own, swap(own, "wt", 4, 1), far, swap(far, "wt", 4, 1))

    far_pair = [
        far_start(jnp.concatenate([gate_weight[layer, 0], up_weight[layer, 0]], axis=1)) for layer in range(layers)
    ]
    far_down = [far_start(down_weight[layer, 0]) for layer in range(layers)]
    far_project = [
        far_start(jnp.concatenate([query_weight[layer], key_weight[layer], value_weight[layer]], axis=1))
        for layer in range(layers)
    ]

    state = tokens[0].astype(jnp.float32)
    saved = []
    for layer in range(layers):
        head_weight = head_all[layer, :lanes]
        router = head_all[layer, lanes : lanes + experts]
        gain_one = head_all[layer, lanes + experts : lanes + experts + 1].astype(jnp.float32)
        gain_two = head_all[layer, lanes + experts + 1 : lanes + experts + 2].astype(jnp.float32)
        out_pieces = wt_gather(out_weight[layer])
        pair_far, pair_own = far_pair[layer]
        down_far, down_own = far_down[layer]
        if layer == 0:
            normed = rms_scale(token_all.astype(jnp.float32), gain_one).astype(jnp.bfloat16)
        else:
            normed = rms_scale(state, gain_one).astype(jnp.bfloat16)
            normed = ring_gather(normed, ctx, n_ctx, table).reshape(n_ctx * rows, width)
        qkv = times(head_weight, normed, 1, 1).astype(jnp.bfloat16)
        sent, exact, log_total = attend(owner_of, qkv, rep, HEAD, n_ctx)
        sent, pair_far = tie(sent, pair_far)
        pair_pieces = near_finish(pair_far, pair_own)
        attended = all_to_all(sent).reshape(4, part, rows)
        middle = state
        for m in range(4):
            middle = middle + times(lax.dynamic_index_in_dim(attended, wt ^ m, 0, keepdims=False), out_pieces[m], 0, 0)
        mixed = rms_scale(middle, gain_two).astype(jnp.bfloat16)
        probs = jax.nn.softmax(times(mixed, router, 1, 1), axis=-1)
        picked = jnp.sum(named[layer] * probs[None], axis=-1, keepdims=True)
        pair_total = picked[0] + picked[1]
        gates = picked / pair_total
        both = place[layer, 0] + place[layer, 1]
        outgoing = times(both, mixed, 0, 0).astype(jnp.bfloat16).reshape(experts, capacity, width)
        if layer == 0:
            outgoing, down_far = tie(outgoing, down_far)
        else:
            outgoing, down_far = tie(outgoing, down_far)
        down_pieces = near_finish(down_far, down_own)
        arrived = all_to_all(outgoing).reshape(experts * capacity, width)
        pairs = [times(arrived, piece, 1, 0) for piece in pair_pieces]
        inner = [(jax.nn.silu(p[:, :hidden]) * p[:, hidden:]).astype(jnp.bfloat16) for p in pairs]
        produced = sum(times(z, piece, 1, 0) for z, piece in zip(inner, down_pieces)).astype(jnp.bfloat16)
        returned = all_to_all(produced.reshape(experts, capacity, width)).reshape(experts * capacity, width)
        results = [times(place[layer, choice], returned, 1, 0) for choice in range(2)]
        saved.append(
            dict(
                state=state,
                normed=normed,
                qkv=qkv,
                exact=exact,
                log_total=log_total,
                attended=attended,
                middle=middle,
                mixed=mixed,
                probs=probs,
                pair_total=pair_total,
                gates=gates,
                both=both,
                arrived=arrived,
                pairs=pairs,
                inner=inner,
                results=results,
                gain_one=gain_one,
                gain_two=gain_two,
                router=router,
                out_pieces=out_pieces,
                pair_pieces=pair_pieces,
                down_pieces=down_pieces,
            )
        )
        state = middle + gates[0] * results[0] + gates[1] * results[1]
    block_output = state.astype(jnp.bfloat16)[None]

    upstream = cotangent[0].astype(jnp.float32)
    grads = [None] * layers
    for layer in reversed(range(layers)):
        k = saved[layer]
        gates = k["gates"]
        back_rows = (gates * upstream[None]).astype(jnp.bfloat16).reshape(2 * rows, width)
        outgoing = times(place[layer].reshape(2 * rows, -1), back_rows, 0, 0).astype(jnp.bfloat16)
        arrived_grad = all_to_all(outgoing.reshape(experts, capacity, width)).reshape(experts * capacity, width)
        grad_rows = 0.0
        pair_grads, down_grads = [], []
        for m in range(4):
            gate_value, up_value = k["pairs"][m][:, :hidden], k["pairs"][m][:, hidden:]
            grad_inner = times(arrived_grad, k["down_pieces"][m], 1, 1)
            sigma = jax.nn.sigmoid(gate_value)
            grad_pair = jnp.concatenate(
                [
                    (grad_inner * up_value * sigma * (1.0 + gate_value * (1.0 - sigma))).astype(jnp.bfloat16),
                    (grad_inner * gate_value * sigma).astype(jnp.bfloat16),
                ],
                axis=1,
            )
            grad_rows = grad_rows + times(grad_pair, k["pair_pieces"][m], 1, 1)
            pair_grads.append(times(k["arrived"], grad_pair, 0, 0))
            down_grads.append(times(k["inner"][m], arrived_grad, 0, 0))
        pair_sum = wt_scatter_sum(pair_grads)
        down_sum = wt_scatter_sum(down_grads)
        back = all_to_all(grad_rows.astype(jnp.bfloat16).reshape(experts, capacity, width))
        grad_mixed = times(k["both"], back.reshape(experts * capacity, width), 1, 0)
        signal = jnp.stack([jnp.sum(upstream * r, axis=-1, keepdims=True) for r in k["results"]])
        grad_picked = (signal - jnp.sum(gates * signal, axis=0, keepdims=True)) / k["pair_total"][None]
        grad_probs = jnp.sum(grad_picked * named[layer], axis=0)
        grad_logits = k["probs"] * (grad_probs - jnp.sum(k["probs"] * grad_probs, axis=1, keepdims=True))
        router_part = lax.dot_general(
            k["mixed"].astype(jnp.float32),
            grad_logits,
            (((0,), (0,)), ((), ())),
            precision=lax.Precision.HIGHEST,
            preferred_element_type=jnp.float32,
        )
        grad_mixed = grad_mixed + lax.dot_general(
            grad_logits,
            k["router"].astype(jnp.float32),
            (((1,), (0,)), ((), ())),
            precision=lax.Precision.HIGHEST,
            preferred_element_type=jnp.float32,
        )
        pulled, gain_two_rows = rms_back(k["middle"], k["gain_two"], grad_mixed)
        grad_middle = upstream + pulled
        middle_low = grad_middle.astype(jnp.bfloat16)
        grad_attended = jnp.zeros((4, part, rows), jnp.bfloat16)
        for m in range(4):
            grad_attended = lax.dynamic_update_index_in_dim(
                grad_attended, times(k["out_pieces"][m], middle_low, 1, 1).astype(jnp.bfloat16), wt ^ m, 0
            )
        grad_heads = all_to_all(grad_attended.reshape(n_ctx, wide, rows))
        grad_whole, grad_sent = attend_back(
            owner_of, k["qkv"], k["exact"], k["log_total"], grad_heads, rep, HEAD, n_ctx
        )
        grad_own = all_to_all(grad_sent)
        small = jnp.concatenate([jnp.sum(gain_two_rows, axis=0)[:, None], router_part], axis=1)
        head_part = jnp.concatenate([times(k["normed"], grad_whole, 0, 1), small], axis=1)
        head_part = head_part.reshape(4, part, lanes + 1 + experts)
        head_sum = wt_scatter_sum(
            [lax.dynamic_index_in_dim(head_part, wt ^ m, 0, keepdims=False) for m in range(4)]
        ).astype(jnp.bfloat16)
        if layer == 0:
            head_grads = ring_gather(head_sum, ctx, n_ctx, devices)
        else:
            head_grads = lax.all_gather(head_sum, "ctx", axis=0)
        middle_pieces = wt_gather(middle_low)
        attended_pieces = wt_exchange(k["attended"], wt)
        out_part = times(jnp.concatenate(attended_pieces, axis=1), jnp.concatenate(middle_pieces, axis=0), 1, 0)
        out_sum = lax.psum(out_part.astype(jnp.bfloat16), "ctx").astype(jnp.float32)
        own = jnp.concatenate(
            [
                grad_own[:, :wide].reshape(width, rows),
                grad_own[:, wide : wide + HEAD].reshape(n_ctx * HEAD, rows),
                grad_own[:, wide + HEAD :].reshape(n_ctx * HEAD, rows),
            ],
            axis=0,
        )
        project = near_finish(*far_project[layer])
        grad_normed = jnp.zeros((rows, width), jnp.float32)
        for m in range(4):
            grad_normed = lax.dynamic_update_slice_in_dim(
                grad_normed, times(own, project[m], 0, 1), (wt ^ m) * part, 1
            )
        pulled, _ = rms_back(k["state"], k["gain_one"], grad_normed)
        upstream = grad_middle + pulled
        head_grads = head_grads.astype(jnp.float32)
        small_sum = jnp.sum(head_grads[:, :, lanes:], axis=0)
        columns = head_grads.transpose(1, 0, 2)
        projected = [
            columns[:, :, :wide].reshape(part, width),
            columns[:, :, wide : wide + HEAD].reshape(part, n_ctx * HEAD),
            columns[:, :, wide + HEAD : lanes].reshape(part, n_ctx * HEAD),
        ]
        gain_one_sum = sum(
            jnp.sum(weight[layer].astype(jnp.float32) * grad, axis=1)
            for weight, grad in zip((query_weight, key_weight, value_weight), projected)
        ) / attention_gain[layer].astype(jnp.float32)
        grads[layer] = (
            gain_one_sum,
            *projected,
            out_sum,
            small_sum[:, 0],
            small_sum[:, 1:],
            pair_sum[None, :, :hidden],
            pair_sum[None, :, hidden:],
            down_sum[None],
        )
    return (block_output, upstream[None], *[jnp.stack(items) for items in zip(*grads)])


def local_rows(
    tokens,
    cotangent,
    seq_lengths,
    block_deal,
    routes,
    attention_gain,
    query_weight,
    key_weight,
    value_weight,
    out_weight,
    mixture_gain,
    router_weight,
    gate_weight,
    up_weight,
    down_weight,
):
    rows_here = tokens.shape[1]
    width = tokens.shape[2]
    layers = query_weight.shape[0]
    experts = router_weight.shape[2]
    capacity = 3 * rows_here // experts
    kv_groups = KV_HEADS
    per_group = HEADS // KV_HEADS
    head_size = HEAD
    kv_width = kv_groups * head_size
    scale = head_size ** (-0.5)
    device = lax.axis_index("ctx")
    everywhere = stream_positions(block_deal[0], BLK)
    every_seq = sequence_ids(everywhere, seq_lengths[0])
    own_pos = lax.dynamic_slice_in_dim(everywhere, device * rows_here, rows_here, 0)
    own_seq = lax.dynamic_slice_in_dim(every_seq, device * rows_here, rows_here, 0)
    choice_rows = jnp.arange(2 * rows_here, dtype=jnp.int32) // 2
    expert_ids = jnp.arange(experts, dtype=jnp.int32)

    def block_mask(start, count):
        key_pos = lax.dynamic_slice_in_dim(everywhere, start, count, 0)
        key_seq = lax.dynamic_slice_in_dim(every_seq, start, count, 0)
        return (own_seq[:, None] == key_seq[None, :]) & (key_pos[None, :] <= own_pos[:, None])

    hidden_state = tokens[0].astype(jnp.float32)
    saved = []
    for layer in range(layers):
        shared = (
            lax.all_gather(attention_gain[layer], "wt", axis=0, tiled=True),
            lax.all_gather(query_weight[layer], "wt", axis=0, tiled=True),
            lax.all_gather(key_weight[layer], "wt", axis=0, tiled=True),
            lax.all_gather(value_weight[layer], "wt", axis=0, tiled=True),
            lax.all_gather(out_weight[layer], "wt", axis=0, tiled=True),
            lax.all_gather(mixture_gain[layer], "wt", axis=0, tiled=True),
            lax.all_gather(router_weight[layer], "wt", axis=0, tiled=True),
        )
        gain_one, full_query, full_key, full_value, full_out, gain_two, full_router = shared
        normed = rms_scale(hidden_state, gain_one.astype(jnp.float32)).astype(jnp.bfloat16)
        queries = jnp.dot(normed, full_query, preferred_element_type=jnp.float32).astype(
            jnp.bfloat16
        )
        keys = jnp.dot(normed, full_key, preferred_element_type=jnp.float32).astype(jnp.bfloat16)
        values = jnp.dot(normed, full_value, preferred_element_type=jnp.float32).astype(
            jnp.bfloat16
        )
        query_heads = queries.reshape(rows_here, kv_groups, per_group, head_size)
        start_state = (
            jnp.full((kv_groups, per_group, rows_here), NEG, jnp.float32),
            jnp.zeros((kv_groups, per_group, rows_here), jnp.float32),
            jnp.zeros((kv_groups, per_group, rows_here, head_size), jnp.float32),
        )
        gathered = None
        key_piece = lax.all_gather(keys, "ctx", axis=0, tiled=True)
        value_piece = lax.all_gather(values, "ctx", axis=0, tiled=True)
        absorb_count = key_piece.shape[0]
        absorb_span = 512

        def turn(index, state):
            first = index * absorb_span
            key_block = lax.dynamic_slice_in_dim(key_piece, first, absorb_span, 0).reshape(
                absorb_span, kv_groups, head_size
            )
            value_block = lax.dynamic_slice_in_dim(value_piece, first, absorb_span, 0).reshape(
                absorb_span, kv_groups, head_size
            )
            allowed = block_mask(first, absorb_span)

            def work(state):
                top, total, summed = state
                scores = (
                    jnp.einsum(
                        "tgrd,kgd->grtk", query_heads, key_block, preferred_element_type=jnp.float32
                    )
                    * scale
                )
                scores = jnp.where(allowed[None, None], scores, NEG)
                top_new = jnp.maximum(top, jnp.max(scores, axis=-1))
                fade = jnp.exp(top - top_new)
                weights = jnp.where(allowed[None, None], jnp.exp(scores - top_new[..., None]), 0.0)
                total = total * fade + jnp.sum(weights, axis=-1)
                summed = summed * fade[..., None] + jnp.einsum(
                    "grtk,kgd->grtd",
                    weights.astype(jnp.bfloat16),
                    value_block,
                    preferred_element_type=jnp.float32,
                )
                return (top_new, total, summed)

            return lax.cond(jnp.any(allowed), work, unchanged, state)

        top, total, summed = lax.fori_loop(0, absorb_count // absorb_span, turn, start_state)
        attended = (summed / total[..., None]).transpose(2, 0, 1, 3).reshape(rows_here, width)
        log_total = top + jnp.log(total)
        attended_low = attended.astype(jnp.bfloat16)
        middle = hidden_state + jnp.dot(attended_low, full_out, preferred_element_type=jnp.float32)
        mixed_low = rms_scale(middle, gain_two.astype(jnp.float32)).astype(jnp.bfloat16)
        probs = jax.nn.softmax(
            jnp.dot(mixed_low, full_router, preferred_element_type=jnp.float32), axis=-1
        )
        chosen = routes[layer, 0]
        picked = jnp.take_along_axis(probs, chosen, axis=1)
        gates = picked / jnp.sum(picked, axis=1, keepdims=True)
        flat_choice = chosen.reshape(-1)
        onehot = (flat_choice[:, None] == expert_ids[None, :]).astype(jnp.int32)
        rank = jnp.sum((jnp.cumsum(onehot, axis=0) - onehot) * onehot, axis=1)
        slots = flat_choice * capacity + rank
        outgoing = (
            jnp.zeros((experts * capacity, width), jnp.bfloat16)
            .at[slots]
            .set(mixed_low[choice_rows])
            .reshape(experts, capacity, width)
        )
        arrived = lax.all_to_all(outgoing, "ctx", split_axis=0, concat_axis=0, tiled=True)
        expert_full = (
            lax.all_gather(gate_weight[layer, 0], "wt", axis=1, tiled=True),
            lax.all_gather(up_weight[layer, 0], "wt", axis=1, tiled=True),
            lax.all_gather(down_weight[layer, 0], "wt", axis=0, tiled=True),
        )
        gate_full, up_full, down_full = expert_full
        expert_rows = arrived.reshape(-1, width)
        gate_value = jnp.dot(expert_rows, gate_full, preferred_element_type=jnp.float32)
        up_value = jnp.dot(expert_rows, up_full, preferred_element_type=jnp.float32)
        inner = (jax.nn.silu(gate_value) * up_value).astype(jnp.bfloat16)
        produced = (
            jnp.dot(inner, down_full, preferred_element_type=jnp.float32)
            .astype(jnp.bfloat16)
            .reshape(experts, capacity, width)
        )
        returned = lax.all_to_all(produced, "ctx", split_axis=0, concat_axis=0, tiled=True)
        expert_out = (
            returned.reshape(-1, width)[slots].reshape(rows_here, 2, width).astype(jnp.float32)
        )
        saved.append(
            (
                hidden_state,
                shared,
                normed,
                query_heads,
                keys,
                values,
                gathered,
                attended,
                attended_low,
                log_total,
                middle,
                mixed_low,
                probs,
                chosen,
                picked,
                gates,
                slots,
                expert_full,
                expert_rows,
                gate_value,
                up_value,
                inner,
                expert_out,
            )
        )
        hidden_state = middle + jnp.sum(gates[:, :, None] * expert_out, axis=1)
    block_output = hidden_state.astype(jnp.bfloat16)[None]
    upstream = cotangent[0].astype(jnp.float32)
    collected = []
    for layer in reversed(range(layers)):
        (
            layer_input,
            shared,
            normed,
            query_heads,
            keys,
            values,
            gathered,
            attended,
            attended_low,
            log_total,
            middle,
            mixed_low,
            probs,
            chosen,
            picked,
            gates,
            slots,
            expert_full,
            expert_rows,
            gate_value,
            up_value,
            inner,
            expert_out,
        ) = saved[layer]
        gain_one, full_query, full_key, full_value, full_out, gain_two, full_router = shared
        gate_full, up_full, down_full = expert_full
        gate_signal = jnp.sum(upstream[:, None, :] * expert_out, axis=-1)
        back_rows = (
            (gates[:, :, None] * upstream[:, None, :]).astype(jnp.bfloat16).reshape(-1, width)
        )
        outgoing_grad = (
            jnp.zeros((experts * capacity, width), jnp.bfloat16)
            .at[slots]
            .set(back_rows)
            .reshape(experts, capacity, width)
        )
        arrived_grad = lax.all_to_all(
            outgoing_grad, "ctx", split_axis=0, concat_axis=0, tiled=True
        ).reshape(-1, width)
        grad_down = outer_rows(inner, arrived_grad)
        grad_inner = times_transposed(arrived_grad, down_full)
        sigma = jax.nn.sigmoid(gate_value)
        grad_gate_value = (
            grad_inner * up_value * sigma * (1.0 + gate_value * (1.0 - sigma))
        ).astype(jnp.bfloat16)
        grad_up_value = (grad_inner * gate_value * sigma).astype(jnp.bfloat16)
        grad_gate = outer_rows(expert_rows, grad_gate_value)
        grad_up = outer_rows(expert_rows, grad_up_value)
        grad_rows = (
            (
                times_transposed(grad_gate_value, gate_full)
                + times_transposed(grad_up_value, up_full)
            )
            .astype(jnp.bfloat16)
            .reshape(experts, capacity, width)
        )
        back_grad = lax.all_to_all(grad_rows, "ctx", split_axis=0, concat_axis=0, tiled=True)
        grad_mixed = jnp.sum(
            back_grad.reshape(-1, width)[slots].reshape(rows_here, 2, width).astype(jnp.float32),
            axis=1,
        )
        pair_total = jnp.sum(picked, axis=1, keepdims=True)
        grad_picked = (
            gate_signal - jnp.sum(gates * gate_signal, axis=1, keepdims=True)
        ) / pair_total
        grad_probs = jnp.sum(
            grad_picked[:, :, None]
            * (chosen[:, :, None] == expert_ids[None, None, :]).astype(jnp.float32),
            axis=1,
        )
        grad_logits = probs * (grad_probs - jnp.sum(probs * grad_probs, axis=1, keepdims=True))
        grad_router = lax.dot_general(
            mixed_low.astype(jnp.float32),
            grad_logits,
            (((0,), (0,)), ((), ())),
            precision=lax.Precision.HIGHEST,
            preferred_element_type=jnp.float32,
        )
        grad_mixed = grad_mixed + lax.dot_general(
            grad_logits,
            full_router.astype(jnp.float32),
            (((1,), (1,)), ((), ())),
            precision=lax.Precision.HIGHEST,
            preferred_element_type=jnp.float32,
        )
        norm_value, pull_two = jax.vjp(rms_scale, middle, gain_two.astype(jnp.float32))
        grad_middle_norm, grad_gain_two = pull_two(grad_mixed)
        grad_middle = upstream + grad_middle_norm
        middle_low = grad_middle.astype(jnp.bfloat16)
        grad_out = outer_rows(attended_low, middle_low)
        grad_attended = times_transposed(middle_low, full_out).astype(jnp.bfloat16)
        grad_heads = grad_attended.reshape(rows_here, kv_groups, per_group, head_size)
        attended_heads = attended.reshape(rows_here, kv_groups, per_group, head_size)
        delta = jnp.sum(grad_heads.astype(jnp.float32) * attended_heads, axis=-1).transpose(1, 2, 0)
        whole = (
            lax.all_gather(keys, "ctx", axis=0, tiled=True),
            lax.all_gather(values, "ctx", axis=0, tiled=True),
        )
        key_all, value_all = whole
        total_rows = key_all.shape[0]
        span = 512

        def score_block(first, count, allowed):
            key_block = lax.dynamic_slice_in_dim(key_all, first, count, 0).reshape(
                count, kv_groups, head_size
            )
            value_block = lax.dynamic_slice_in_dim(value_all, first, count, 0).reshape(
                count, kv_groups, head_size
            )
            scores = (
                jnp.einsum(
                    "tgrd,kgd->grtk", query_heads, key_block, preferred_element_type=jnp.float32
                )
                * scale
            )
            probs_block = jnp.where(
                allowed[None, None], jnp.exp(scores - log_total[..., None]), 0.0
            )
            grad_probs_block = jnp.einsum(
                "tgrd,kgd->grtk", grad_heads, value_block, preferred_element_type=jnp.float32
            )
            grad_scores = (probs_block * (grad_probs_block - delta[..., None])).astype(jnp.bfloat16)
            return (key_block, probs_block, grad_scores)

        def key_terms(probs_block, grad_scores, count):
            key_part = (
                jnp.einsum(
                    "grtk,tgrd->kgd", grad_scores, query_heads, preferred_element_type=jnp.float32
                )
                * scale
            ).reshape(count, kv_width)
            value_part = jnp.einsum(
                "grtk,tgrd->kgd",
                probs_block.astype(jnp.bfloat16),
                grad_heads,
                preferred_element_type=jnp.float32,
            ).reshape(count, kv_width)
            return (key_part, value_part)

        query_start = jnp.zeros((rows_here, kv_groups, per_group, head_size), jnp.float32)

        def turn_back(index, state):
            first = index * span
            allowed = block_mask(first, span)

            def work(state):
                grad_query, grad_keys, grad_values = state
                key_block, probs_block, grad_scores = score_block(first, span, allowed)
                grad_query = (
                    grad_query
                    + jnp.einsum(
                        "grtk,kgd->tgrd", grad_scores, key_block, preferred_element_type=jnp.float32
                    )
                    * scale
                )
                key_part, value_part = key_terms(probs_block, grad_scores, span)
                grad_keys = lax.dynamic_update_slice_in_dim(grad_keys, key_part, first, 0)
                grad_values = lax.dynamic_update_slice_in_dim(grad_values, value_part, first, 0)
                return (grad_query, grad_keys, grad_values)

            return lax.cond(jnp.any(allowed), work, unchanged, state)

        back_start = (
            query_start,
            jnp.zeros((total_rows, kv_width), jnp.float32),
            jnp.zeros((total_rows, kv_width), jnp.float32),
        )
        grad_query, grad_keys, grad_values = lax.fori_loop(
            0, total_rows // span, turn_back, back_start
        )
        grad_keys, grad_values = (
            lax.psum_scatter(
                grad_keys.astype(jnp.bfloat16), "ctx", scatter_dimension=0, tiled=True
            ).astype(jnp.float32),
            lax.psum_scatter(
                grad_values.astype(jnp.bfloat16), "ctx", scatter_dimension=0, tiled=True
            ).astype(jnp.float32),
        )
        query_low = grad_query.reshape(rows_here, width).astype(jnp.bfloat16)
        key_low = grad_keys.astype(jnp.bfloat16)
        value_low = grad_values.astype(jnp.bfloat16)
        grad_query_weight = outer_rows(normed, query_low)
        grad_key_weight = outer_rows(normed, key_low)
        grad_value_weight = outer_rows(normed, value_low)
        grad_normed = (
            times_transposed(query_low, full_query)
            + times_transposed(key_low, full_key)
            + times_transposed(value_low, full_value)
        )
        norm_value, pull_one = jax.vjp(rms_scale, layer_input, gain_one.astype(jnp.float32))
        grad_input_norm, grad_gain_one = pull_one(grad_normed)
        upstream = grad_middle + grad_input_norm
        part_one, part_query, part_key, part_value, part_out, part_two, part_router = (
            lax.psum_scatter(
                grad_gain_one.astype(jnp.bfloat16), "wt", scatter_dimension=0, tiled=True
            ).astype(jnp.float32),
            lax.psum_scatter(
                grad_query_weight.astype(jnp.bfloat16), "wt", scatter_dimension=0, tiled=True
            ).astype(jnp.float32),
            lax.psum_scatter(
                grad_key_weight.astype(jnp.bfloat16), "wt", scatter_dimension=0, tiled=True
            ).astype(jnp.float32),
            lax.psum_scatter(
                grad_value_weight.astype(jnp.bfloat16), "wt", scatter_dimension=0, tiled=True
            ).astype(jnp.float32),
            lax.psum_scatter(
                grad_out.astype(jnp.bfloat16), "wt", scatter_dimension=0, tiled=True
            ).astype(jnp.float32),
            lax.psum_scatter(
                grad_gain_two.astype(jnp.bfloat16), "wt", scatter_dimension=0, tiled=True
            ).astype(jnp.float32),
            lax.psum_scatter(
                grad_router.astype(jnp.bfloat16), "wt", scatter_dimension=0, tiled=True
            ).astype(jnp.float32),
        )
        summed_parts = (
            lax.psum(part_one.astype(jnp.bfloat16), "ctx").astype(jnp.float32),
            lax.psum(part_query.astype(jnp.bfloat16), "ctx").astype(jnp.float32),
            lax.psum(part_key.astype(jnp.bfloat16), "ctx").astype(jnp.float32),
            lax.psum(part_value.astype(jnp.bfloat16), "ctx").astype(jnp.float32),
            lax.psum(part_out.astype(jnp.bfloat16), "ctx").astype(jnp.float32),
            lax.psum(part_two.astype(jnp.bfloat16), "ctx").astype(jnp.float32),
            lax.psum(part_router.astype(jnp.bfloat16), "ctx").astype(jnp.float32),
        )
        expert_parts = (
            lax.psum_scatter(
                grad_gate.astype(jnp.bfloat16), "wt", scatter_dimension=1, tiled=True
            ).astype(jnp.float32),
            lax.psum_scatter(
                grad_up.astype(jnp.bfloat16), "wt", scatter_dimension=1, tiled=True
            ).astype(jnp.float32),
            lax.psum_scatter(
                grad_down.astype(jnp.bfloat16), "wt", scatter_dimension=0, tiled=True
            ).astype(jnp.float32),
        )
        collected.append((summed_parts, expert_parts))
    ordered = collected[::-1]
    attention_gain_grad = jnp.stack([item[0][0] for item in ordered])
    query_grad = jnp.stack([item[0][1] for item in ordered])
    key_grad = jnp.stack([item[0][2] for item in ordered])
    value_grad = jnp.stack([item[0][3] for item in ordered])
    out_grad = jnp.stack([item[0][4] for item in ordered])
    mixture_gain_grad = jnp.stack([item[0][5] for item in ordered])
    router_grad = jnp.stack([item[0][6] for item in ordered])
    gate_grad = jnp.stack([item[1][0] for item in ordered])[:, None]
    up_grad = jnp.stack([item[1][1] for item in ordered])[:, None]
    down_grad = jnp.stack([item[1][2] for item in ordered])[:, None]
    return (
        block_output,
        upstream[None],
        attention_gain_grad,
        query_grad,
        key_grad,
        value_grad,
        out_grad,
        mixture_gain_grad,
        router_grad,
        gate_grad,
        up_grad,
        down_grad,
    )


def solution(mesh):
    placed = (
        P("wt", "ctx", None),
        P("wt", "ctx", None),
        P("wt", None),
        P("wt", None, None),
        P(None, "wt", "ctx", None),
        P(None, "wt"),
        P(None, "wt", None),
        P(None, "wt", None),
        P(None, "wt", None),
        P(None, "wt", None),
        P(None, "wt"),
        P(None, "wt", None),
        P(None, "ctx", None, "wt"),
        P(None, "ctx", None, "wt"),
        P(None, "ctx", "wt", None),
    )
    def local(*arrays):
        if by_heads(mesh, *arrays):
            return local_heads(mesh, *arrays)
        return local_rows(*arrays)

    return jax.shard_map(
        local,
        mesh=mesh,
        in_specs=placed,
        out_specs=(
            P("wt", "ctx", None),
            P("wt", "ctx", None),
            P(None, "wt"),
            P(None, "wt", None),
            P(None, "wt", None),
            P(None, "wt", None),
            P(None, "wt", None),
            P(None, "wt"),
            P(None, "wt", None),
            P(None, "ctx", None, "wt"),
            P(None, "ctx", None, "wt"),
            P(None, "ctx", "wt", None),
        ),
        check_vma=False,
    )
```

```python
import functools

import jax
import jax.numpy as jnp
from jax import lax
from jax.experimental import pallas as pl
from jax.experimental.pallas import tpu as pltpu
from jax.sharding import PartitionSpec as P

HEADS = 24
KV_HEADS = 8
HEAD = 64
BLK = 128


EPS = 1e-05
NEG = -1e30


def rms_scale(rows, gain):
    return rows * lax.rsqrt(jnp.mean(rows * rows, axis=-1, keepdims=True) + EPS) * gain


def stream_positions(table, width):
    offsets = jnp.arange(width, dtype=jnp.int32)
    return (table[:, :, None] * width + offsets[None, None, :]).reshape(-1)


def sequence_ids(positions, seq_row):
    ends = jnp.cumsum(seq_row)
    return jnp.sum((positions[:, None] >= ends[None, :]).astype(jnp.int32), axis=1)


def outer_rows(left, right):
    return lax.dot_general(
        left, right, (((0,), (0,)), ((), ())), preferred_element_type=jnp.float32
    )


def times_transposed(left, right):
    return lax.dot_general(
        left, right, (((1,), (1,)), ((), ())), preferred_element_type=jnp.float32
    )


def unchanged(state):
    return state


def times(left, right, a, b):
    return lax.dot_general(left, right, (((a,), (b,)), ((), ())), preferred_element_type=jnp.float32)


def vmem(count):
    return [pl.BlockSpec(memory_space=pltpu.VMEM)] * count


def kernel_params():
    return pltpu.CompilerParams(vmem_limit_bytes=56 * 2**20)


def cost(flops, nbytes, transcendentals=0):
    return pl.CostEstimate(flops=int(flops), bytes_accessed=int(nbytes), transcendentals=int(transcendentals))


def causal_mask(span):
    key_at = lax.broadcasted_iota(jnp.int32, (span, span), 0)
    query_at = lax.broadcasted_iota(jnp.int32, (span, span), 1)
    return key_at <= query_at


def front_kernel(raw, rep, head, span, spot_ref, owner_ref, *refs):
    *blocks, weight_ref, gain_ref, normed_ref, qkv_ref, sent_ref, exact_ref, log_ref = refs
    rows = blocks[0].shape[0]
    count = len(blocks) - 1
    tokens = count * rows
    width = rep * head
    scale = head ** (-0.5)
    gain = gain_ref[...]
    for k in range(count):
        low, high = (blocks[k],) * 2 if k < count - 1 else blocks[k:]
        half = low.shape[0] if k == count - 1 else rows
        for start, ref in ((0, low), (half, high)) if k == count - 1 else ((0, low),):
            block = ref[...]
            if raw:
                block = rms_scale(block.astype(jnp.float32), gain).astype(jnp.bfloat16)
            normed_ref[spot_ref[k], start : start + ref.shape[0], :] = block
    lanes_all = weight_ref.shape[0]
    for part in range(tokens // span):
        take = span // rows
        piece = normed_ref[part * take : (part + 1) * take].reshape(span, normed_ref.shape[2])
        qkv_ref[:, part * span : (part + 1) * span] = times(weight_ref[...], piece, 1, 1).astype(jnp.bfloat16)
    mask = causal_mask(span)
    per = span // rows
    for part in range(tokens // span):
        lanes = pl.ds(part * span, span)
        seen = (part + 1) * span
        keys = qkv_ref[width : width + head, :seen]
        values = qkv_ref[width + head : lanes_all, :seen]
        for h in range(rep):
            at = slice(h * head, (h + 1) * head)
            scores = times(keys, qkv_ref[at, lanes], 0, 0) * scale
            last = jnp.where(mask, scores[seen - span :], NEG)
            top = jnp.max(last, axis=0, keepdims=True)
            if part:
                top = jnp.maximum(top, jnp.max(scores[: seen - span], axis=0, keepdims=True))
            weights = jnp.exp(last - top)
            if part:
                weights = jnp.concatenate([jnp.exp(scores[: seen - span] - top), weights], axis=0)
            total = jnp.sum(weights, axis=0, keepdims=True)
            result = times(values, weights.astype(jnp.bfloat16), 1, 0) / total
            exact_ref[at, lanes] = result
            log_ref[h : h + 1, lanes] = top + jnp.log(total)
            for b in range(per):
                sent_ref[owner_ref[part * per + b], at, :] = result[:, b * rows : (b + 1) * rows].astype(jnp.bfloat16)


def front(raw, spots, owner_of, blocks, weight, gain, rep, head):
    rows, width = blocks[0].shape
    count = len(blocks) - 1
    tokens = count * rows
    span = min(256, tokens)
    deep = weight.shape[0]
    pairs = rep * tokens * (tokens + span) // 2
    return pl.pallas_call(
        functools.partial(front_kernel, raw, rep, head, span),
        out_shape=(
            jax.ShapeDtypeStruct((count, rows, width), jnp.bfloat16),
            jax.ShapeDtypeStruct((deep, tokens), jnp.bfloat16),
            jax.ShapeDtypeStruct((count, rep * head, rows), jnp.bfloat16),
            jax.ShapeDtypeStruct((rep * head, tokens), jnp.float32),
            jax.ShapeDtypeStruct((rep, tokens), jnp.float32),
        ),
        in_specs=[pl.BlockSpec(memory_space=pltpu.SMEM)] * 2 + vmem(len(blocks) + 2),
        out_specs=tuple(vmem(5)),
        compiler_params=kernel_params(),
        cost_estimate=cost(4 * head * pairs + 2 * deep * width * tokens, 9 * 2**20, pairs),
        name="front",
    )(spots, owner_of, *blocks, weight, gain)


def attend_back_kernel(rep, head, span, owner_ref, qkv_ref, exact_ref, log_ref, grad_ref, whole_ref, sent_ref, grad_all, keys_sum, values_sum):
    tokens = qkv_ref.shape[1]
    rows = grad_ref.shape[2]
    width = rep * head
    per = span // rows
    scale = head ** (-0.5)
    mask = causal_mask(span)
    for block in range(tokens // rows):
        grad_all[:, block * rows : (block + 1) * rows] = grad_ref[owner_ref[block]]
    keys_sum[...] = jnp.zeros_like(keys_sum)
    values_sum[...] = jnp.zeros_like(values_sum)
    for part in range(tokens // span):
        lanes = pl.ds(part * span, span)
        seen = (part + 1) * span
        keys = qkv_ref[width : width + head, :seen]
        values = qkv_ref[width + head :, :seen]
        for h in range(rep):
            at = slice(h * head, (h + 1) * head)
            queries = qkv_ref[at, lanes]
            grads = grad_all[at, lanes]
            delta = jnp.sum(grads.astype(jnp.float32) * exact_ref[at, lanes], axis=0, keepdims=True)
            scores = times(keys, queries, 0, 0) * scale
            probs = jnp.exp(scores - log_ref[h : h + 1, lanes])
            last = jnp.where(mask, probs[seen - span :], 0.0)
            probs = last if part == 0 else jnp.concatenate([probs[: seen - span], last], axis=0)
            pulled = times(values, grads, 0, 0)
            slopes = (probs * (pulled - delta)).astype(jnp.bfloat16)
            back = (times(keys, slopes, 1, 0) * scale).astype(jnp.bfloat16)
            whole_ref[at, lanes] = back
            for b in range(per):
                sent_ref[owner_ref[part * per + b], at, :] = back[:, b * rows : (b + 1) * rows]
            keys_sum[:, :seen] += times(queries, slopes, 1, 1)
            values_sum[:, :seen] += times(grads, probs.astype(jnp.bfloat16), 1, 1)
    keys_low = (keys_sum[...] * scale).astype(jnp.bfloat16)
    values_low = values_sum[...].astype(jnp.bfloat16)
    whole_ref[width : width + head, :] = keys_low
    whole_ref[width + head :, :] = values_low
    for block in range(tokens // rows):
        cut = slice(block * rows, (block + 1) * rows)
        sent_ref[owner_ref[block], width : width + head, :] = keys_low[:, cut]
        sent_ref[owner_ref[block], width + head :, :] = values_low[:, cut]


def attend_back(owner_of, qkv, exact, log_total, grads, rep, head):
    deep, tokens = qkv.shape
    count, _, rows = grads.shape
    span = min(256, tokens)
    pairs = rep * tokens * (tokens + span) // 2
    return pl.pallas_call(
        functools.partial(attend_back_kernel, rep, head, span),
        out_shape=(
            jax.ShapeDtypeStruct((deep, tokens), jnp.bfloat16),
            jax.ShapeDtypeStruct((count, deep, rows), jnp.bfloat16),
        ),
        in_specs=[pl.BlockSpec(memory_space=pltpu.SMEM)] + vmem(4),
        out_specs=tuple(vmem(2)),
        scratch_shapes=[
            pltpu.VMEM((rep * head, tokens), jnp.bfloat16),
            pltpu.VMEM((head, tokens), jnp.float32),
            pltpu.VMEM((head, tokens), jnp.float32),
        ],
        compiler_params=kernel_params(),
        cost_estimate=cost(10 * head * pairs, 6 * 2**20, pairs),
        name="attend_back",
    )(owner_of, qkv, exact, log_total, grads)


def silu_pair(gate_value, up_value):
    return (gate_value * jax.nn.sigmoid(gate_value) * up_value).astype(jnp.bfloat16)


def pair_back(grad_inner, gate_value, up_value):
    sigma = jax.nn.sigmoid(gate_value)
    grad_gate = grad_inner * up_value * sigma * (1.0 + gate_value * (1.0 - sigma))
    return grad_gate.astype(jnp.bfloat16), (grad_inner * gate_value * sigma).astype(jnp.bfloat16)


def expert_forward_kernel(rows_ref, *refs):
    gate, up, down = refs[:4], refs[4:8], refs[8:12]
    made_ref, gates_ref, ups_ref, inner_ref, total = refs[12:]
    rows = rows_ref[...]
    for m in range(4):
        gate_value = times(rows, gate[m][...], 1, 0)
        up_value = times(rows, up[m][...], 1, 0)
        gates_ref[m] = gate_value
        ups_ref[m] = up_value
        inner = silu_pair(gate_value, up_value)
        inner_ref[m] = inner
        part = times(inner, down[m][...], 1, 0)
        if m == 0:
            total[...] = part
        elif m < 3:
            total[...] += part
        else:
            made_ref[...] = (total[...] + part).astype(jnp.bfloat16)


def expert_forward(rows, gate, up, down):
    count, width = rows.shape
    hidden = gate[0].shape[1]
    return pl.pallas_call(
        expert_forward_kernel,
        out_shape=(
            jax.ShapeDtypeStruct((count, width), jnp.bfloat16),
            jax.ShapeDtypeStruct((4, count, hidden), jnp.float32),
            jax.ShapeDtypeStruct((4, count, hidden), jnp.float32),
            jax.ShapeDtypeStruct((4, count, hidden), jnp.bfloat16),
        ),
        in_specs=vmem(13),
        out_specs=tuple(vmem(4)),
        scratch_shapes=[pltpu.VMEM((count, width), jnp.float32)],
        compiler_params=kernel_params(),
        cost_estimate=cost(24 * count * width * hidden, 16 * 2**20, 4 * count * hidden),
        name="expert_forward",
    )(rows, *gate, *up, *down)


def expert_backward_kernel(grad_ref, *refs):
    gate, up, down = refs[:4], refs[4:8], refs[8:12]
    gates_ref, ups_ref, back_ref, grad_gate_ref, grad_up_ref, total = refs[12:]
    grads = grad_ref[...]
    for m in range(4):
        grad_gate, grad_up = pair_back(times(grads, down[m][...], 1, 1), gates_ref[m], ups_ref[m])
        grad_gate_ref[m] = grad_gate
        grad_up_ref[m] = grad_up
        part = times(grad_gate, gate[m][...], 1, 1) + times(grad_up, up[m][...], 1, 1)
        if m == 0:
            total[...] = part
        elif m < 3:
            total[...] += part
        else:
            back_ref[...] = (total[...] + part).astype(jnp.bfloat16)


def expert_backward(grads, gate, up, down, gates, ups):
    count, width = grads.shape
    hidden = gate[0].shape[1]
    return pl.pallas_call(
        expert_backward_kernel,
        out_shape=(
            jax.ShapeDtypeStruct((count, width), jnp.bfloat16),
            jax.ShapeDtypeStruct((4, count, hidden), jnp.bfloat16),
            jax.ShapeDtypeStruct((4, count, hidden), jnp.bfloat16),
        ),
        in_specs=vmem(15),
        out_specs=tuple(vmem(3)),
        scratch_shapes=[pltpu.VMEM((count, width), jnp.float32)],
        compiler_params=kernel_params(),
        cost_estimate=cost(24 * count * width * hidden, 16 * 2**20, 4 * count * hidden),
        name="expert_backward",
    )(grads, *gate, *up, *down, gates, ups)


def expert_both_kernel(experts, mine_ref, rows_ref, cot_ref, router_ref, *refs):
    gate, up, down = refs[:4], refs[4:8], refs[8:12]
    made_ref, back_ref, grad_ref, inner_ref, grad_gate_ref, grad_up_ref, total, total_back = refs[12:]
    rows = rows_ref[...]
    count, width = rows.shape
    cot = cot_ref[:, :width].astype(jnp.float32)
    logits = times(rows, router_ref[...], 1, 1)
    ids = lax.broadcasted_iota(jnp.int32, logits.shape, 1)
    logits = jnp.where(ids < experts, logits, NEG)
    odds = jnp.exp(logits - jnp.max(logits, axis=1, keepdims=True))
    other = cot_ref[:, width : width + 1].astype(jnp.float32).astype(jnp.int32)
    own_odds = jnp.sum(jnp.where(ids == mine_ref[0], odds, 0.0), axis=1, keepdims=True)
    other_odds = jnp.sum(jnp.where(ids == other, odds, 0.0), axis=1, keepdims=True)
    grad_ref[...] = (own_odds / (own_odds + other_odds) * cot).astype(jnp.bfloat16)
    grads = grad_ref[...]
    for m in range(4):
        gate_value = times(rows, gate[m][...], 1, 0)
        up_value = times(rows, up[m][...], 1, 0)
        inner = silu_pair(gate_value, up_value)
        inner_ref[m] = inner
        grad_gate, grad_up = pair_back(times(grads, down[m][...], 1, 1), gate_value, up_value)
        grad_gate_ref[m] = grad_gate
        grad_up_ref[m] = grad_up
        part = times(inner, down[m][...], 1, 0)
        part_back = times(grad_gate, gate[m][...], 1, 1) + times(grad_up, up[m][...], 1, 1)
        total[...] = part if m == 0 else total[...] + part
        total_back[...] = part_back if m == 0 else total_back[...] + part_back
    made = total[...].astype(jnp.bfloat16)
    made_ref[...] = made
    back_ref[:, :width] = total_back[...].astype(jnp.bfloat16)
    signal = jnp.sum(cot * made.astype(jnp.float32), axis=1, keepdims=True)
    high = signal.astype(jnp.bfloat16)
    low = (signal - high.astype(jnp.float32)).astype(jnp.bfloat16)
    at = lax.broadcasted_iota(jnp.int32, (count, back_ref.shape[1] - width), 1)
    back_ref[:, width:] = jnp.where(
        at == 0, high.astype(jnp.float32), jnp.where(at == 1, low.astype(jnp.float32), 0.0)
    ).astype(jnp.bfloat16)


def expert_both(experts, mine, rows, cot, router, gate, up, down):
    count, width = rows.shape
    hidden = gate[0].shape[1]
    return pl.pallas_call(
        functools.partial(expert_both_kernel, experts),
        out_shape=(
            jax.ShapeDtypeStruct((count, width), jnp.bfloat16),
            jax.ShapeDtypeStruct(cot.shape, jnp.bfloat16),
            jax.ShapeDtypeStruct((count, width), jnp.bfloat16),
            jax.ShapeDtypeStruct((4, count, hidden), jnp.bfloat16),
            jax.ShapeDtypeStruct((4, count, hidden), jnp.bfloat16),
            jax.ShapeDtypeStruct((4, count, hidden), jnp.bfloat16),
        ),
        in_specs=[pl.BlockSpec(memory_space=pltpu.SMEM)] + vmem(15),
        out_specs=tuple(vmem(6)),
        scratch_shapes=[pltpu.VMEM((count, width), jnp.float32)] * 2,
        compiler_params=kernel_params(),
        cost_estimate=cost(48 * count * width * hidden, 18 * 2**20, 8 * count * hidden),
        name="expert_both",
    )(mine, rows, cot, router, *gate, *up, *down)


def expert_grads_kernel(rows_ref, grad_ref, inner_ref, grad_gate_ref, grad_up_ref, pair_give, pair_own, pair_far, down_give, down_own, down_far):
    for m, (pairs, at, downs, down_at) in enumerate(
        (
            (pair_own, 0, down_own, 0),
            (pair_give, 0, down_give, 0),
            (pair_far, 0, down_far, 0),
            (pair_give, 2, down_give, 1),
        )
    ):
        pairs[at] = times(rows_ref[...], grad_gate_ref[m], 0, 0).astype(jnp.bfloat16)
        pairs[at + 1] = times(rows_ref[...], grad_up_ref[m], 0, 0).astype(jnp.bfloat16)
        downs[down_at] = times(inner_ref[m], grad_ref[...], 0, 0).astype(jnp.bfloat16)


def expert_grads(rows, grads, inner, grad_gate, grad_up):
    count, width = rows.shape
    hidden = inner.shape[2]
    shapes = [(4, width, hidden), (2, width, hidden), (2, width, hidden)]
    shapes += [(2, hidden, width), (1, hidden, width), (1, hidden, width)]
    return pl.pallas_call(
        expert_grads_kernel,
        out_shape=tuple(jax.ShapeDtypeStruct(shape, jnp.bfloat16) for shape in shapes),
        in_specs=vmem(5),
        out_specs=tuple(vmem(6)),
        compiler_params=kernel_params(),
        cost_estimate=cost(24 * count * width * hidden, 14 * 2**20),
        name="expert_grads",
    )(rows, grads, inner, grad_gate, grad_up)


def head_grads_kernel(part, at_ref, normed_ref, whole_ref, small_ref, give_ref, own_ref, far_ref):
    tokens = whole_ref.shape[1]
    deep = whole_ref.shape[0]
    for m, (ref, slot) in enumerate(((own_ref, 0), (give_ref, 0), (far_ref, 0), (give_ref, 1))):
        lanes = pl.ds(pl.multiple_of(at_ref[m] * part, 128), part)
        rows = normed_ref[:, :, lanes].reshape(tokens, part)
        ref[slot, :deep, :] = times(whole_ref[...], rows, 1, 0).astype(jnp.bfloat16)
        ref[slot, deep:, :] = small_ref[:, lanes].astype(jnp.bfloat16)


def head_grads(at, normed, whole, small):
    deep, tokens = whole.shape
    width = normed.shape[2]
    part = width // 4
    full = deep + small.shape[0]
    return pl.pallas_call(
        functools.partial(head_grads_kernel, part),
        out_shape=tuple(jax.ShapeDtypeStruct((n, full, part), jnp.bfloat16) for n in (2, 1, 1)),
        in_specs=[pl.BlockSpec(memory_space=pltpu.SMEM)] + vmem(3),
        out_specs=tuple(vmem(3)),
        compiler_params=kernel_params(),
        cost_estimate=cost(2 * deep * width * tokens, 6 * 2**20),
        name="head_grads",
    )(at, normed, whole, small)


def spread_kernel(wide, head, ringed, *refs):
    if ringed:
        spot_ref, *blocks, query_ref, key_ref, value_ref = refs[: ringed + 4]
        gathered_ref = refs[-1]
        outs = refs[-7:-1]
        for k, block in enumerate(blocks[:-2]):
            gathered_ref[spot_ref[k]] = block[...]
        half = blocks[-2].shape[0]
        gathered_ref[spot_ref[ringed - 2], :half, :] = blocks[-2][...]
        gathered_ref[spot_ref[ringed - 2], half:, :] = blocks[-1][...]
    else:
        gathered_ref, out_ref, query_ref, key_ref, value_ref = refs[:5]
        outs = refs[-6:]
    query_out, key_out, value_out, out_out, small_out, sum_ref = outs
    count, _, part = gathered_ref.shape
    deep = wide + 2 * head
    small = small_out.shape[0]
    sums = jnp.zeros((part, 1), jnp.float32)
    for i in range(count // 2):
        block = gathered_ref[2 * i : 2 * i + 2, :wide, :].astype(jnp.float32).reshape(2 * wide, part).T
        lanes = slice(2 * i * wide, 2 * (i + 1) * wide)
        query_out[0, :, lanes] = block
        sums += jnp.sum(block * query_ref[:, lanes].astype(jnp.float32), axis=1, keepdims=True)
    for start, weight_ref, out in ((wide, key_ref, key_out), (wide + head, value_ref, value_out)):
        block = gathered_ref[:, start : start + head, :].astype(jnp.float32).reshape(count * head, part).T
        out[0] = block
        sums += jnp.sum(block * weight_ref[...].astype(jnp.float32), axis=1, keepdims=True)
    sum_ref[...] = sums
    total = gathered_ref[0, deep : deep + small, :].astype(jnp.float32)
    for c in range(1, count):
        total += gathered_ref[c, deep : deep + small, :].astype(jnp.float32)
    small_out[...] = total
    if ringed:
        rows = part // count
        for c in range(count):
            for j in range(out_out.shape[2] // part):
                piece = gathered_ref[c, deep + small + j * rows : deep + small + (j + 1) * rows, :]
                out_out[0, c * rows : (c + 1) * rows, j * part : (j + 1) * part] = piece.astype(jnp.float32)
    else:
        out_out[0] = out_ref[...].astype(jnp.float32)


def spread(layer, layers, spots, sources, weights, wide, head, small, before):
    ringed = len(sources) if spots is not None else 0
    part = weights[0].shape[0]
    width = weights[0].shape[1]
    count = width // wide
    shapes = [(layers,) + weight.shape for weight in weights] + [(layers, part, width)]
    aliased = [] if before is None else list(before)
    one = lambda shape: pl.BlockSpec((1,) + shape[1:], lambda i: (layer, 0, 0))
    whole = lambda shape: pl.BlockSpec(shape, lambda i: (0,) * len(shape))
    deep = sources[0].shape[-2]
    lead = [spots] if ringed else []
    return pl.pallas_call(
        functools.partial(spread_kernel, wide, head, ringed),
        grid=(1,),
        out_shape=tuple(jax.ShapeDtypeStruct(shape, jnp.float32) for shape in shapes)
        + (jax.ShapeDtypeStruct((small, part), jnp.float32), jax.ShapeDtypeStruct((part, 1), jnp.float32)),
        in_specs=[pl.BlockSpec(memory_space=pltpu.SMEM)] * len(lead)
        + [whole(source.shape) for source in sources]
        + [whole(weight.shape) for weight in weights]
        + [pl.BlockSpec(memory_space=pl.ANY)] * len(aliased),
        out_specs=tuple(one(shape) for shape in shapes) + (whole((small, part)), whole((part, 1))),
        scratch_shapes=[pltpu.VMEM((count, deep, part), jnp.bfloat16)] if ringed else [],
        input_output_aliases={len(lead) + len(sources) + 3 + i: i for i in range(len(aliased))},
        compiler_params=kernel_params(),
        cost_estimate=cost(4 * count * part * wide, 12 * 2**20),
        name="spread",
    )(*lead, *sources, *weights, *aliased)


def finish_kernel(*refs):
    own_ref, near_ref, far_ref = refs[:3]
    outs = refs[-own_ref.shape[0] :]
    for i, out in enumerate(outs):
        total = own_ref[i].astype(jnp.float32) + near_ref[i].astype(jnp.float32) + far_ref[i].astype(jnp.float32)
        out[0, 0] = total


def finish(layer, layers, own, near, far, before):
    count, rows, columns = own.shape
    steps = 2
    block = rows // steps
    aliased = [] if before is None else list(before)
    taken = pl.BlockSpec((count, block, columns), lambda i: (0, i, 0))
    made = pl.BlockSpec((1, 1, block, columns), lambda i: (layer, 0, i, 0))
    return pl.pallas_call(
        finish_kernel,
        grid=(steps,),
        out_shape=tuple(jax.ShapeDtypeStruct((layers, 1, rows, columns), jnp.float32) for _ in range(count)),
        in_specs=[taken] * 3 + [pl.BlockSpec(memory_space=pl.ANY)] * len(aliased),
        out_specs=(made,) * count,
        input_output_aliases={3 + i: i for i in range(len(aliased))},
        compiler_params=kernel_params(),
        cost_estimate=cost(2 * count * rows * columns, 10 * count * rows * columns),
        name="finish",
    )(own, near, far, *aliased)


def swap(x, mask):
    return lax.ppermute(x, "wt", [(i, i ^ mask) for i in range(4)])


def near_finish(far, own):
    return (own, swap(own, 1), far, swap(far, 1))


def wt_gather(own):
    return near_finish(swap(own, 2), own)


def wt_exchange(slices, me):
    def cut(m):
        return lax.dynamic_index_in_dim(slices, me ^ m, 0, keepdims=False)

    far = swap(jnp.stack([cut(2), cut(3)]), 2)
    near = swap(jnp.stack([cut(1), far[1]]), 1)
    return (cut(0), near[0], far[0], near[1])


def in_order(pieces, me, axis):
    own, near, far, last = pieces
    odd, high = me % 2 == 1, me >= 2
    low = (jnp.where(odd, near, own), jnp.where(odd, own, near))
    up = (jnp.where(odd, last, far), jnp.where(odd, far, last))
    first = [jnp.where(high, b, a) for a, b in zip(low, up)]
    second = [jnp.where(high, a, b) for a, b in zip(low, up)]
    return jnp.concatenate(first + second, axis=axis)


def tie(*arrays):
    return lax.optimization_barrier(arrays)


def ring_of(count):
    ring = list(range(0, count, 2)) + list(range(count - 1, 0, -2))
    offsets = [0] + [sign * step for step in range(1, count // 2) for sign in (-1, 1)] + [count // 2]
    table = [[ring[(ring.index(i) + k) % count] for k in offsets] for i in range(count)]
    return ring, jnp.asarray(table, jnp.int32)


def ring_start(x, ring):
    right = [(a, b) for a, b in zip(ring, ring[1:] + ring[:1])]
    left = [(b, a) for a, b in right]
    return lax.ppermute(x, "ctx", right), lax.ppermute(x, "ctx", left)


def ring_blocks(x, first, ring):
    count = len(ring)
    right = [(a, b) for a, b in zip(ring, ring[1:] + ring[:1])]
    left = [(b, a) for a, b in right]
    ahead, behind = first
    blocks = [x, ahead, behind]
    for _ in range(2, count // 2):
        ahead, behind = lax.ppermute(ahead, "ctx", right), lax.ppermute(behind, "ctx", left)
        blocks += [ahead, behind]
    half = x.shape[0] // 2
    return blocks + [lax.ppermute(ahead[:half], "ctx", right), lax.ppermute(behind[half:], "ctx", left)]


def all_to_all(x):
    return lax.all_to_all(x, "ctx", split_axis=0, concat_axis=0, tiled=True)


def rms_back(rows, gain, grad):
    scale = lax.rsqrt(jnp.mean(rows * rows, axis=-1, keepdims=True) + EPS)
    unit = rows * scale
    pulled = grad * gain
    return scale * (pulled - unit * jnp.mean(pulled * unit, axis=-1, keepdims=True)), grad * unit


def by_heads(mesh, tokens, cotangent, seq_lengths, block_deal, *rest):
    return (
        mesh.shape["ctx"] == KV_HEADS
        and mesh.shape["wt"] == 4
        and seq_lengths.shape[1] == 1
        and block_deal.shape[2] == 1
        and tokens.shape[1] == BLK
    )


def local_heads(
    mesh,
    tokens,
    cotangent,
    seq_lengths,
    block_deal,
    routes,
    attention_gain,
    query_weight,
    key_weight,
    value_weight,
    out_weight,
    mixture_gain,
    router_weight,
    gate_weight,
    up_weight,
    down_weight,
):
    n_ctx = mesh.shape["ctx"]
    rows = tokens.shape[1]
    width = tokens.shape[2]
    layers = query_weight.shape[0]
    experts = router_weight.shape[2]
    capacity = 3 * rows // experts
    slot_count = experts * capacity
    rep = HEADS // KV_HEADS
    wide = rep * HEAD
    lanes = wide + 2 * HEAD
    part = width // 4
    ctx = lax.axis_index("ctx")
    mine = ctx.astype(jnp.int32).reshape(1)
    wt = lax.axis_index("wt").astype(jnp.uint32)
    others = (wt ^ jnp.arange(4, dtype=jnp.uint32)).astype(jnp.int32)
    table = block_deal[0, :, 0]
    devices = jnp.arange(n_ctx, dtype=jnp.int32)
    owner_of = jnp.sum(jnp.where(table[None, :] == devices[:, None], devices[None, :], 0), axis=1)
    ring, ring_table = ring_of(n_ctx)
    ring_owners = lax.dynamic_index_in_dim(ring_table, ctx.astype(jnp.uint32), 0, keepdims=False)
    spots = jnp.sum(jnp.where(ring_owners[:, None] == devices[None, :], table[None, :], 0), axis=1)

    first = ring_start(tokens[0], ring)

    expert_ids = jnp.arange(experts, dtype=jnp.int32)
    chosen = routes[:, 0]
    flat = chosen.reshape(layers, 2 * rows)
    onehot = flat[:, :, None] == expert_ids
    earlier = jnp.tril(jnp.ones((2 * rows, 2 * rows), jnp.bfloat16), -1)
    rank = jnp.einsum("ij,lje->lie", earlier, onehot.astype(jnp.bfloat16), preferred_element_type=jnp.float32)
    rank = jnp.sum(jnp.where(onehot, rank, 0.0), axis=2).astype(jnp.int32)
    slots = (flat * capacity + rank).reshape(layers, rows, 2).transpose(0, 2, 1)
    place = (slots[..., None] == jnp.arange(slot_count, dtype=jnp.int32)).astype(jnp.bfloat16)
    named = (chosen.transpose(0, 2, 1)[..., None] == expert_ids).astype(jnp.float32)

    def head_rows(layer, query_weight, key_weight, value_weight):
        return [
            lax.dynamic_slice_in_dim(query_weight[layer], ctx * wide, wide, 1).T,
            lax.dynamic_slice_in_dim(key_weight[layer], ctx * HEAD, HEAD, 1).T,
            lax.dynamic_slice_in_dim(value_weight[layer], ctx * HEAD, HEAD, 1).T,
            router_weight[layer].T,
            attention_gain[layer][None],
            mixture_gain[layer][None],
            jnp.zeros((14 - experts, part), jnp.bfloat16),
        ]

    deep = lanes + 16
    first, *projections = tie(first, query_weight, key_weight, value_weight)
    head_own = jnp.concatenate(sum([head_rows(layer, *projections) for layer in range(layers)], []), axis=0)
    head_all = in_order(wt_gather(head_own), wt, 1).reshape(layers, deep, width)

    out_own = list(out_weight)
    gate_own = [gate_weight[layer, 0] for layer in range(layers)]
    up_own = [up_weight[layer, 0] for layer in range(layers)]
    down_own = [down_weight[layer, 0] for layer in range(layers)]
    project_own = [
        jnp.concatenate([query_weight[layer], key_weight[layer], value_weight[layer]], axis=1) for layer in range(layers)
    ]
    out_far, gate_far, up_far, down_far, project_far = [
        [swap(own, 2) for own in group] for group in (out_own, gate_own, up_own, down_own, project_own)
    ]

    state = tokens[0].astype(jnp.float32)
    saved = []
    last = layers - 1
    cot_slots = None
    for layer in range(layers):
        head_weight = head_all[layer, :lanes]
        router = head_all[layer, lanes : lanes + experts]
        gain_one = head_all[layer, lanes + experts : lanes + experts + 1].astype(jnp.float32)
        gain_two = head_all[layer, lanes + experts + 1 : lanes + experts + 2].astype(jnp.float32)
        if layer == 0:
            blocks = ring_blocks(tokens[0], first, ring)
        else:
            normed = rms_scale(state, gain_one).astype(jnp.bfloat16)
            normed, out_far[layer] = tie(normed, out_far[layer])
            blocks = ring_blocks(normed, ring_start(normed, ring), ring)
        normed_all, qkv, sent, exact, log_total = front(
            layer == 0, spots, owner_of, blocks, head_weight, gain_one, rep, HEAD
        )
        if layer == 0:
            other = chosen[last].transpose(1, 0)[::-1, :, None].astype(jnp.bfloat16)
            cot_rows = jnp.concatenate(
                [jnp.broadcast_to(cotangent[0][None], (2, rows, width)), jnp.broadcast_to(other, (2, rows, 128))], axis=2
            ).reshape(2 * rows, width + 128)
            cot_out = times(place[last].reshape(2 * rows, slot_count), cot_rows, 0, 0).astype(jnp.bfloat16)
            cot_out, blocks[1] = tie(cot_out, blocks[1])
            cot_slots = all_to_all(cot_out.reshape(experts, capacity, width + 128)).reshape(slot_count, width + 128)
            sent, out_far[layer] = tie(sent, out_far[layer])
        else:
            sent, gate_far[layer], up_far[layer] = tie(sent, gate_far[layer], up_far[layer])
        out_pieces = near_finish(out_far[layer], out_own[layer])
        attended = all_to_all(sent).reshape(4, part, rows)
        middle = state
        for m in range(4):
            middle = middle + times(lax.dynamic_index_in_dim(attended, wt ^ m, 0, keepdims=False), out_pieces[m], 0, 0)
        mixed = rms_scale(middle, gain_two).astype(jnp.bfloat16)
        both = place[layer, 0] + place[layer, 1]
        outgoing = times(both, mixed, 0, 0).astype(jnp.bfloat16).reshape(experts, capacity, width)
        if layer == 0:
            outgoing, gate_far[layer] = tie(outgoing, gate_far[layer])
        else:
            outgoing, down_far[layer] = tie(outgoing, down_far[layer])
        arrived = all_to_all(outgoing).reshape(slot_count, width)
        probs = jax.nn.softmax(times(mixed, router, 1, 1), axis=-1)
        picked = jnp.sum(named[layer] * probs[None], axis=-1, keepdims=True)
        pair_total = picked[0] + picked[1]
        gates = picked / pair_total
        kept = dict(
            state=state,
            normed_all=normed_all,
            qkv=qkv,
            exact=exact,
            log_total=log_total,
            attended=attended,
            middle=middle,
            mixed=mixed,
            probs=probs,
            pair_total=pair_total,
            gates=gates,
            both=both,
            arrived=arrived,
            gain_one=gain_one,
            gain_two=gain_two,
            router=router,
            out_pieces=out_pieces,
        )
        pieces = [near_finish(far[layer], own[layer]) for far, own in ((gate_far, gate_own), (up_far, up_own), (down_far, down_own))]
        kept["pieces"] = pieces
        saved.append(kept)
        if layer == last:
            break
        made, kept["gate_values"], kept["up_values"], kept["inner"] = expert_forward(arrived, *pieces)
        returned = all_to_all(made.reshape(experts, capacity, width)).reshape(slot_count, width)
        kept["results"] = [times(place[layer, choice], returned, 1, 0) for choice in range(2)]
        state = middle + gates[0] * kept["results"][0] + gates[1] * kept["results"][1]

    upstream = cotangent[0].astype(jnp.float32)
    expert_done = [None, None]
    head_done = None
    smalls, gain_sums = [None] * layers, [None] * layers
    block_output = None
    for layer in reversed(range(layers)):
        k = saved[layer]
        gates, both, pieces = k["gates"], k["both"], k["pieces"]
        if layer == last:
            router_rows = jnp.concatenate([k["router"], jnp.zeros((128 - experts, width), jnp.bfloat16)])
            arrived, project_far[layer] = tie(k["arrived"], project_far[layer])
            made, back, arrived_grad, inner, grad_gate, grad_up = expert_both(
                experts, mine, arrived, cot_slots, router_rows, *pieces
            )
            back = all_to_all(back.reshape(experts, capacity, width + 128)).reshape(slot_count, width + 128)
            signal = jnp.stack([jnp.sum(times(p, back[:, width:], 1, 0), axis=1, keepdims=True) for p in place[layer]])
            back = back[:, :width]
        else:
            arrived, inner = k["arrived"], k["inner"]
            back_rows = (gates * upstream[None]).astype(jnp.bfloat16).reshape(2 * rows, width)
            outgoing = times(place[layer].reshape(2 * rows, slot_count), back_rows, 0, 0).astype(jnp.bfloat16)
            arrived_grad = all_to_all(outgoing.reshape(experts, capacity, width)).reshape(slot_count, width)
            back, grad_gate, grad_up = expert_backward(arrived_grad, *pieces, k["gate_values"], k["up_values"])
            back = all_to_all(back.reshape(experts, capacity, width)).reshape(slot_count, width)
            signal = jnp.stack([jnp.sum(upstream * r, axis=-1, keepdims=True) for r in k["results"]])
        pair_give, pair_own, pair_far, down_give, down_kept, down_far_part = expert_grads(
            arrived, arrived_grad, inner, grad_gate, grad_up
        )
        pair_near, down_near = swap(pair_give, 1), swap(down_give, 1)
        add = lambda a, b: (a.astype(jnp.float32) + b.astype(jnp.float32)).astype(jnp.bfloat16)
        pair_last = swap(add(pair_far, pair_near[2:]), 2)
        down_last = swap(add(down_far_part, down_near[1:]), 2)
        grad_mixed = times(both, back, 1, 0)
        grad_picked = (signal - jnp.sum(gates * signal, axis=0, keepdims=True)) / k["pair_total"][None]
        grad_probs = jnp.sum(grad_picked * named[layer], axis=0)
        grad_logits = k["probs"] * (grad_probs - jnp.sum(k["probs"] * grad_probs, axis=1, keepdims=True))
        router_part = lax.dot_general(
            grad_logits,
            k["mixed"].astype(jnp.float32),
            (((0,), (0,)), ((), ())),
            precision=lax.Precision.HIGHEST,
            preferred_element_type=jnp.float32,
        )
        grad_mixed = grad_mixed + lax.dot_general(
            grad_logits,
            k["router"].astype(jnp.float32),
            (((1,), (0,)), ((), ())),
            precision=lax.Precision.HIGHEST,
            preferred_element_type=jnp.float32,
        )
        pulled, gain_two_rows = rms_back(k["middle"], k["gain_two"], grad_mixed)
        grad_middle = upstream + pulled
        if layer == last:
            grad_middle, project_far[0] = tie(grad_middle, project_far[0])
        middle_low = grad_middle.astype(jnp.bfloat16)
        grad_attended = jnp.zeros((4, part, rows), jnp.bfloat16)
        for m in range(4):
            grad_attended = lax.dynamic_update_index_in_dim(
                grad_attended, times(k["out_pieces"][m], middle_low, 1, 1).astype(jnp.bfloat16), wt ^ m, 0
            )
        if layer == last:
            made, back = tie(made, grad_attended)[0], back
            returned = all_to_all(made.reshape(experts, capacity, width)).reshape(slot_count, width)
            state = k["middle"] + sum(gates[i] * times(place[layer, i], returned, 1, 0) for i in range(2))
            block_output = state.astype(jnp.bfloat16)[None]
        grad_heads = all_to_all(grad_attended.reshape(n_ctx, wide, rows))
        grad_whole, grad_sent = attend_back(owner_of, k["qkv"], k["exact"], k["log_total"], grad_heads, rep, HEAD)
        grad_sent, grad_whole, pair_last, down_last = tie(grad_sent, grad_whole, pair_last, down_last)
        pair_done = finish(layer, layers, pair_own, pair_near, pair_last, expert_done[0])
        down_done = finish(layer, layers, down_kept, down_near, down_last, expert_done[1])
        expert_done = [pair_done, down_done]
        grad_own = all_to_all(grad_sent)
        small = jnp.concatenate(
            [router_part, jnp.sum(gain_two_rows, axis=0)[None], jnp.zeros((15 - experts, width), jnp.float32)]
        )
        head_give, head_kept, head_far = head_grads(others, k["normed_all"], grad_whole, small)
        head_near = swap(head_give, 1)
        head_last = swap(add(head_far[0], head_near[1]), 2)
        head_sum = (
            head_kept[0].astype(jnp.float32) + head_near[0].astype(jnp.float32) + head_last.astype(jnp.float32)
        ).astype(jnp.bfloat16)
        middle_pieces = wt_gather(middle_low)
        attended_pieces = wt_exchange(k["attended"], wt)
        out_part = times(jnp.concatenate(attended_pieces, axis=1), jnp.concatenate(middle_pieces, axis=0), 1, 0)
        out_part = out_part.astype(jnp.bfloat16)
        weights = (query_weight[layer], key_weight[layer], value_weight[layer])
        if layer == last:
            out_sum = lax.psum(out_part, "ctx")
            gathered = lax.all_gather(head_sum, "ctx", axis=0)
            sources, ring_spots = (gathered, out_sum), None
        else:
            out_rows = all_to_all(out_part.reshape(n_ctx, part // n_ctx, width))
            out_rows = jnp.sum(out_rows.astype(jnp.float32), axis=0).astype(jnp.bfloat16)
            merged = jnp.concatenate([head_sum] + [out_rows[:, i * part : (i + 1) * part] for i in range(4)], axis=0)
            sources, ring_spots = ring_blocks(merged, ring_start(merged, ring), ring), ring_owners
        *head_done, smalls[layer], gain_sums[layer] = spread(
            layer, layers, ring_spots, sources, weights, wide, HEAD, 16, head_done
        )
        own = jnp.concatenate(
            [
                grad_own[:, :wide].reshape(width, rows),
                grad_own[:, wide : wide + HEAD].reshape(n_ctx * HEAD, rows),
                grad_own[:, wide + HEAD :].reshape(n_ctx * HEAD, rows),
            ],
            axis=0,
        )
        project = near_finish(project_far[layer], project_own[layer])
        grad_normed = jnp.zeros((rows, width), jnp.float32)
        for m in range(4):
            grad_normed = lax.dynamic_update_slice_in_dim(
                grad_normed, times(own, project[m], 0, 1), (wt ^ m) * part, 1
            )
        pulled, _ = rms_back(k["state"], k["gain_one"], grad_normed)
        upstream = grad_middle + pulled
    gain_one_grad = jnp.stack([s[:, 0] for s in gain_sums]) / attention_gain.astype(jnp.float32)
    small_all = jnp.stack(smalls)
    query_grad, key_grad, value_grad, out_grad = head_done
    return (
        block_output,
        upstream[None],
        gain_one_grad,
        query_grad,
        key_grad,
        value_grad,
        out_grad,
        small_all[:, experts],
        small_all[:, :experts].transpose(0, 2, 1),
        *expert_done[0],
        *expert_done[1],
    )


def local_rows(
    tokens,
    cotangent,
    seq_lengths,
    block_deal,
    routes,
    attention_gain,
    query_weight,
    key_weight,
    value_weight,
    out_weight,
    mixture_gain,
    router_weight,
    gate_weight,
    up_weight,
    down_weight,
):
    rows_here = tokens.shape[1]
    width = tokens.shape[2]
    layers = query_weight.shape[0]
    experts = router_weight.shape[2]
    capacity = 3 * rows_here // experts
    kv_groups = KV_HEADS
    per_group = HEADS // KV_HEADS
    head_size = HEAD
    kv_width = kv_groups * head_size
    scale = head_size ** (-0.5)
    device = lax.axis_index("ctx")
    everywhere = stream_positions(block_deal[0], BLK)
    every_seq = sequence_ids(everywhere, seq_lengths[0])
    own_pos = lax.dynamic_slice_in_dim(everywhere, device * rows_here, rows_here, 0)
    own_seq = lax.dynamic_slice_in_dim(every_seq, device * rows_here, rows_here, 0)
    choice_rows = jnp.arange(2 * rows_here, dtype=jnp.int32) // 2
    expert_ids = jnp.arange(experts, dtype=jnp.int32)

    def block_mask(start, count):
        key_pos = lax.dynamic_slice_in_dim(everywhere, start, count, 0)
        key_seq = lax.dynamic_slice_in_dim(every_seq, start, count, 0)
        return (own_seq[:, None] == key_seq[None, :]) & (key_pos[None, :] <= own_pos[:, None])

    hidden_state = tokens[0].astype(jnp.float32)
    saved = []
    for layer in range(layers):
        shared = (
            lax.all_gather(attention_gain[layer], "wt", axis=0, tiled=True),
            lax.all_gather(query_weight[layer], "wt", axis=0, tiled=True),
            lax.all_gather(key_weight[layer], "wt", axis=0, tiled=True),
            lax.all_gather(value_weight[layer], "wt", axis=0, tiled=True),
            lax.all_gather(out_weight[layer], "wt", axis=0, tiled=True),
            lax.all_gather(mixture_gain[layer], "wt", axis=0, tiled=True),
            lax.all_gather(router_weight[layer], "wt", axis=0, tiled=True),
        )
        gain_one, full_query, full_key, full_value, full_out, gain_two, full_router = shared
        normed = rms_scale(hidden_state, gain_one.astype(jnp.float32)).astype(jnp.bfloat16)
        queries = jnp.dot(normed, full_query, preferred_element_type=jnp.float32).astype(
            jnp.bfloat16
        )
        keys = jnp.dot(normed, full_key, preferred_element_type=jnp.float32).astype(jnp.bfloat16)
        values = jnp.dot(normed, full_value, preferred_element_type=jnp.float32).astype(
            jnp.bfloat16
        )
        query_heads = queries.reshape(rows_here, kv_groups, per_group, head_size)
        start_state = (
            jnp.full((kv_groups, per_group, rows_here), NEG, jnp.float32),
            jnp.zeros((kv_groups, per_group, rows_here), jnp.float32),
            jnp.zeros((kv_groups, per_group, rows_here, head_size), jnp.float32),
        )
        gathered = None
        key_piece = lax.all_gather(keys, "ctx", axis=0, tiled=True)
        value_piece = lax.all_gather(values, "ctx", axis=0, tiled=True)
        absorb_count = key_piece.shape[0]
        absorb_span = 512

        def turn(index, state):
            first = index * absorb_span
            key_block = lax.dynamic_slice_in_dim(key_piece, first, absorb_span, 0).reshape(
                absorb_span, kv_groups, head_size
            )
            value_block = lax.dynamic_slice_in_dim(value_piece, first, absorb_span, 0).reshape(
                absorb_span, kv_groups, head_size
            )
            allowed = block_mask(first, absorb_span)

            def work(state):
                top, total, summed = state
                scores = (
                    jnp.einsum(
                        "tgrd,kgd->grtk", query_heads, key_block, preferred_element_type=jnp.float32
                    )
                    * scale
                )
                scores = jnp.where(allowed[None, None], scores, NEG)
                top_new = jnp.maximum(top, jnp.max(scores, axis=-1))
                fade = jnp.exp(top - top_new)
                weights = jnp.where(allowed[None, None], jnp.exp(scores - top_new[..., None]), 0.0)
                total = total * fade + jnp.sum(weights, axis=-1)
                summed = summed * fade[..., None] + jnp.einsum(
                    "grtk,kgd->grtd",
                    weights.astype(jnp.bfloat16),
                    value_block,
                    preferred_element_type=jnp.float32,
                )
                return (top_new, total, summed)

            return lax.cond(jnp.any(allowed), work, unchanged, state)

        top, total, summed = lax.fori_loop(0, absorb_count // absorb_span, turn, start_state)
        attended = (summed / total[..., None]).transpose(2, 0, 1, 3).reshape(rows_here, width)
        log_total = top + jnp.log(total)
        attended_low = attended.astype(jnp.bfloat16)
        middle = hidden_state + jnp.dot(attended_low, full_out, preferred_element_type=jnp.float32)
        mixed_low = rms_scale(middle, gain_two.astype(jnp.float32)).astype(jnp.bfloat16)
        probs = jax.nn.softmax(
            jnp.dot(mixed_low, full_router, preferred_element_type=jnp.float32), axis=-1
        )
        chosen = routes[layer, 0]
        picked = jnp.take_along_axis(probs, chosen, axis=1)
        gates = picked / jnp.sum(picked, axis=1, keepdims=True)
        flat_choice = chosen.reshape(-1)
        onehot = (flat_choice[:, None] == expert_ids[None, :]).astype(jnp.int32)
        rank = jnp.sum((jnp.cumsum(onehot, axis=0) - onehot) * onehot, axis=1)
        slots = flat_choice * capacity + rank
        outgoing = (
            jnp.zeros((experts * capacity, width), jnp.bfloat16)
            .at[slots]
            .set(mixed_low[choice_rows])
            .reshape(experts, capacity, width)
        )
        arrived = lax.all_to_all(outgoing, "ctx", split_axis=0, concat_axis=0, tiled=True)
        expert_full = (
            lax.all_gather(gate_weight[layer, 0], "wt", axis=1, tiled=True),
            lax.all_gather(up_weight[layer, 0], "wt", axis=1, tiled=True),
            lax.all_gather(down_weight[layer, 0], "wt", axis=0, tiled=True),
        )
        gate_full, up_full, down_full = expert_full
        expert_rows = arrived.reshape(-1, width)
        gate_value = jnp.dot(expert_rows, gate_full, preferred_element_type=jnp.float32)
        up_value = jnp.dot(expert_rows, up_full, preferred_element_type=jnp.float32)
        inner = (jax.nn.silu(gate_value) * up_value).astype(jnp.bfloat16)
        produced = (
            jnp.dot(inner, down_full, preferred_element_type=jnp.float32)
            .astype(jnp.bfloat16)
            .reshape(experts, capacity, width)
        )
        returned = lax.all_to_all(produced, "ctx", split_axis=0, concat_axis=0, tiled=True)
        expert_out = (
            returned.reshape(-1, width)[slots].reshape(rows_here, 2, width).astype(jnp.float32)
        )
        saved.append(
            (
                hidden_state,
                shared,
                normed,
                query_heads,
                keys,
                values,
                gathered,
                attended,
                attended_low,
                log_total,
                middle,
                mixed_low,
                probs,
                chosen,
                picked,
                gates,
                slots,
                expert_full,
                expert_rows,
                gate_value,
                up_value,
                inner,
                expert_out,
            )
        )
        hidden_state = middle + jnp.sum(gates[:, :, None] * expert_out, axis=1)
    block_output = hidden_state.astype(jnp.bfloat16)[None]
    upstream = cotangent[0].astype(jnp.float32)
    collected = []
    for layer in reversed(range(layers)):
        (
            layer_input,
            shared,
            normed,
            query_heads,
            keys,
            values,
            gathered,
            attended,
            attended_low,
            log_total,
            middle,
            mixed_low,
            probs,
            chosen,
            picked,
            gates,
            slots,
            expert_full,
            expert_rows,
            gate_value,
            up_value,
            inner,
            expert_out,
        ) = saved[layer]
        gain_one, full_query, full_key, full_value, full_out, gain_two, full_router = shared
        gate_full, up_full, down_full = expert_full
        gate_signal = jnp.sum(upstream[:, None, :] * expert_out, axis=-1)
        back_rows = (
            (gates[:, :, None] * upstream[:, None, :]).astype(jnp.bfloat16).reshape(-1, width)
        )
        outgoing_grad = (
            jnp.zeros((experts * capacity, width), jnp.bfloat16)
            .at[slots]
            .set(back_rows)
            .reshape(experts, capacity, width)
        )
        arrived_grad = lax.all_to_all(
            outgoing_grad, "ctx", split_axis=0, concat_axis=0, tiled=True
        ).reshape(-1, width)
        grad_down = outer_rows(inner, arrived_grad)
        grad_inner = times_transposed(arrived_grad, down_full)
        sigma = jax.nn.sigmoid(gate_value)
        grad_gate_value = (
            grad_inner * up_value * sigma * (1.0 + gate_value * (1.0 - sigma))
        ).astype(jnp.bfloat16)
        grad_up_value = (grad_inner * gate_value * sigma).astype(jnp.bfloat16)
        grad_gate = outer_rows(expert_rows, grad_gate_value)
        grad_up = outer_rows(expert_rows, grad_up_value)
        grad_rows = (
            (
                times_transposed(grad_gate_value, gate_full)
                + times_transposed(grad_up_value, up_full)
            )
            .astype(jnp.bfloat16)
            .reshape(experts, capacity, width)
        )
        back_grad = lax.all_to_all(grad_rows, "ctx", split_axis=0, concat_axis=0, tiled=True)
        grad_mixed = jnp.sum(
            back_grad.reshape(-1, width)[slots].reshape(rows_here, 2, width).astype(jnp.float32),
            axis=1,
        )
        pair_total = jnp.sum(picked, axis=1, keepdims=True)
        grad_picked = (
            gate_signal - jnp.sum(gates * gate_signal, axis=1, keepdims=True)
        ) / pair_total
        grad_probs = jnp.sum(
            grad_picked[:, :, None]
            * (chosen[:, :, None] == expert_ids[None, None, :]).astype(jnp.float32),
            axis=1,
        )
        grad_logits = probs * (grad_probs - jnp.sum(probs * grad_probs, axis=1, keepdims=True))
        grad_router = lax.dot_general(
            mixed_low.astype(jnp.float32),
            grad_logits,
            (((0,), (0,)), ((), ())),
            precision=lax.Precision.HIGHEST,
            preferred_element_type=jnp.float32,
        )
        grad_mixed = grad_mixed + lax.dot_general(
            grad_logits,
            full_router.astype(jnp.float32),
            (((1,), (1,)), ((), ())),
            precision=lax.Precision.HIGHEST,
            preferred_element_type=jnp.float32,
        )
        norm_value, pull_two = jax.vjp(rms_scale, middle, gain_two.astype(jnp.float32))
        grad_middle_norm, grad_gain_two = pull_two(grad_mixed)
        grad_middle = upstream + grad_middle_norm
        middle_low = grad_middle.astype(jnp.bfloat16)
        grad_out = outer_rows(attended_low, middle_low)
        grad_attended = times_transposed(middle_low, full_out).astype(jnp.bfloat16)
        grad_heads = grad_attended.reshape(rows_here, kv_groups, per_group, head_size)
        attended_heads = attended.reshape(rows_here, kv_groups, per_group, head_size)
        delta = jnp.sum(grad_heads.astype(jnp.float32) * attended_heads, axis=-1).transpose(1, 2, 0)
        whole = (
            lax.all_gather(keys, "ctx", axis=0, tiled=True),
            lax.all_gather(values, "ctx", axis=0, tiled=True),
        )
        key_all, value_all = whole
        total_rows = key_all.shape[0]
        span = 512

        def score_block(first, count, allowed):
            key_block = lax.dynamic_slice_in_dim(key_all, first, count, 0).reshape(
                count, kv_groups, head_size
            )
            value_block = lax.dynamic_slice_in_dim(value_all, first, count, 0).reshape(
                count, kv_groups, head_size
            )
            scores = (
                jnp.einsum(
                    "tgrd,kgd->grtk", query_heads, key_block, preferred_element_type=jnp.float32
                )
                * scale
            )
            probs_block = jnp.where(
                allowed[None, None], jnp.exp(scores - log_total[..., None]), 0.0
            )
            grad_probs_block = jnp.einsum(
                "tgrd,kgd->grtk", grad_heads, value_block, preferred_element_type=jnp.float32
            )
            grad_scores = (probs_block * (grad_probs_block - delta[..., None])).astype(jnp.bfloat16)
            return (key_block, probs_block, grad_scores)

        def key_terms(probs_block, grad_scores, count):
            key_part = (
                jnp.einsum(
                    "grtk,tgrd->kgd", grad_scores, query_heads, preferred_element_type=jnp.float32
                )
                * scale
            ).reshape(count, kv_width)
            value_part = jnp.einsum(
                "grtk,tgrd->kgd",
                probs_block.astype(jnp.bfloat16),
                grad_heads,
                preferred_element_type=jnp.float32,
            ).reshape(count, kv_width)
            return (key_part, value_part)

        query_start = jnp.zeros((rows_here, kv_groups, per_group, head_size), jnp.float32)

        def turn_back(index, state):
            first = index * span
            allowed = block_mask(first, span)

            def work(state):
                grad_query, grad_keys, grad_values = state
                key_block, probs_block, grad_scores = score_block(first, span, allowed)
                grad_query = (
                    grad_query
                    + jnp.einsum(
                        "grtk,kgd->tgrd", grad_scores, key_block, preferred_element_type=jnp.float32
                    )
                    * scale
                )
                key_part, value_part = key_terms(probs_block, grad_scores, span)
                grad_keys = lax.dynamic_update_slice_in_dim(grad_keys, key_part, first, 0)
                grad_values = lax.dynamic_update_slice_in_dim(grad_values, value_part, first, 0)
                return (grad_query, grad_keys, grad_values)

            return lax.cond(jnp.any(allowed), work, unchanged, state)

        back_start = (
            query_start,
            jnp.zeros((total_rows, kv_width), jnp.float32),
            jnp.zeros((total_rows, kv_width), jnp.float32),
        )
        grad_query, grad_keys, grad_values = lax.fori_loop(
            0, total_rows // span, turn_back, back_start
        )
        grad_keys, grad_values = (
            lax.psum_scatter(
                grad_keys.astype(jnp.bfloat16), "ctx", scatter_dimension=0, tiled=True
            ).astype(jnp.float32),
            lax.psum_scatter(
                grad_values.astype(jnp.bfloat16), "ctx", scatter_dimension=0, tiled=True
            ).astype(jnp.float32),
        )
        query_low = grad_query.reshape(rows_here, width).astype(jnp.bfloat16)
        key_low = grad_keys.astype(jnp.bfloat16)
        value_low = grad_values.astype(jnp.bfloat16)
        grad_query_weight = outer_rows(normed, query_low)
        grad_key_weight = outer_rows(normed, key_low)
        grad_value_weight = outer_rows(normed, value_low)
        grad_normed = (
            times_transposed(query_low, full_query)
            + times_transposed(key_low, full_key)
            + times_transposed(value_low, full_value)
        )
        norm_value, pull_one = jax.vjp(rms_scale, layer_input, gain_one.astype(jnp.float32))
        grad_input_norm, grad_gain_one = pull_one(grad_normed)
        upstream = grad_middle + grad_input_norm
        part_one, part_query, part_key, part_value, part_out, part_two, part_router = (
            lax.psum_scatter(
                grad_gain_one.astype(jnp.bfloat16), "wt", scatter_dimension=0, tiled=True
            ).astype(jnp.float32),
            lax.psum_scatter(
                grad_query_weight.astype(jnp.bfloat16), "wt", scatter_dimension=0, tiled=True
            ).astype(jnp.float32),
            lax.psum_scatter(
                grad_key_weight.astype(jnp.bfloat16), "wt", scatter_dimension=0, tiled=True
            ).astype(jnp.float32),
            lax.psum_scatter(
                grad_value_weight.astype(jnp.bfloat16), "wt", scatter_dimension=0, tiled=True
            ).astype(jnp.float32),
            lax.psum_scatter(
                grad_out.astype(jnp.bfloat16), "wt", scatter_dimension=0, tiled=True
            ).astype(jnp.float32),
            lax.psum_scatter(
                grad_gain_two.astype(jnp.bfloat16), "wt", scatter_dimension=0, tiled=True
            ).astype(jnp.float32),
            lax.psum_scatter(
                grad_router.astype(jnp.bfloat16), "wt", scatter_dimension=0, tiled=True
            ).astype(jnp.float32),
        )
        summed_parts = (
            lax.psum(part_one.astype(jnp.bfloat16), "ctx").astype(jnp.float32),
            lax.psum(part_query.astype(jnp.bfloat16), "ctx").astype(jnp.float32),
            lax.psum(part_key.astype(jnp.bfloat16), "ctx").astype(jnp.float32),
            lax.psum(part_value.astype(jnp.bfloat16), "ctx").astype(jnp.float32),
            lax.psum(part_out.astype(jnp.bfloat16), "ctx").astype(jnp.float32),
            lax.psum(part_two.astype(jnp.bfloat16), "ctx").astype(jnp.float32),
            lax.psum(part_router.astype(jnp.bfloat16), "ctx").astype(jnp.float32),
        )
        expert_parts = (
            lax.psum_scatter(
                grad_gate.astype(jnp.bfloat16), "wt", scatter_dimension=1, tiled=True
            ).astype(jnp.float32),
            lax.psum_scatter(
                grad_up.astype(jnp.bfloat16), "wt", scatter_dimension=1, tiled=True
            ).astype(jnp.float32),
            lax.psum_scatter(
                grad_down.astype(jnp.bfloat16), "wt", scatter_dimension=0, tiled=True
            ).astype(jnp.float32),
        )
        collected.append((summed_parts, expert_parts))
    ordered = collected[::-1]
    attention_gain_grad = jnp.stack([item[0][0] for item in ordered])
    query_grad = jnp.stack([item[0][1] for item in ordered])
    key_grad = jnp.stack([item[0][2] for item in ordered])
    value_grad = jnp.stack([item[0][3] for item in ordered])
    out_grad = jnp.stack([item[0][4] for item in ordered])
    mixture_gain_grad = jnp.stack([item[0][5] for item in ordered])
    router_grad = jnp.stack([item[0][6] for item in ordered])
    gate_grad = jnp.stack([item[1][0] for item in ordered])[:, None]
    up_grad = jnp.stack([item[1][1] for item in ordered])[:, None]
    down_grad = jnp.stack([item[1][2] for item in ordered])[:, None]
    return (
        block_output,
        upstream[None],
        attention_gain_grad,
        query_grad,
        key_grad,
        value_grad,
        out_grad,
        mixture_gain_grad,
        router_grad,
        gate_grad,
        up_grad,
        down_grad,
    )


def solution(mesh):
    placed = (
        P("wt", "ctx", None),
        P("wt", "ctx", None),
        P("wt", None),
        P("wt", None, None),
        P(None, "wt", "ctx", None),
        P(None, "wt"),
        P(None, "wt", None),
        P(None, "wt", None),
        P(None, "wt", None),
        P(None, "wt", None),
        P(None, "wt"),
        P(None, "wt", None),
        P(None, "ctx", None, "wt"),
        P(None, "ctx", None, "wt"),
        P(None, "ctx", "wt", None),
    )
    def local(*arrays):
        if by_heads(mesh, *arrays):
            return local_heads(mesh, *arrays)
        return local_rows(*arrays)

    return jax.shard_map(
        local,
        mesh=mesh,
        in_specs=placed,
        out_specs=(
            P("wt", "ctx", None),
            P("wt", "ctx", None),
            P(None, "wt"),
            P(None, "wt", None),
            P(None, "wt", None),
            P(None, "wt", None),
            P(None, "wt", None),
            P(None, "wt"),
            P(None, "wt", None),
            P(None, "ctx", None, "wt"),
            P(None, "ctx", None, "wt"),
            P(None, "ctx", "wt", None),
        ),
        check_vma=False,
    )
```

```python
import functools

import jax
import jax.numpy as jnp
from jax import lax
from jax.experimental import pallas as pl
from jax.experimental.pallas import tpu as pltpu
from jax.sharding import PartitionSpec as P

HEADS = 24
KV_HEADS = 8
HEAD = 64
BLK = 128


EPS = 1e-05
NEG = -1e30


def rms_scale(rows, gain):
    return rows * lax.rsqrt(jnp.mean(rows * rows, axis=-1, keepdims=True) + EPS) * gain


def stream_positions(table, width):
    offsets = jnp.arange(width, dtype=jnp.int32)
    return (table[:, :, None] * width + offsets[None, None, :]).reshape(-1)


def sequence_ids(positions, seq_row):
    ends = jnp.cumsum(seq_row)
    return jnp.sum((positions[:, None] >= ends[None, :]).astype(jnp.int32), axis=1)


def outer_rows(left, right):
    return lax.dot_general(
        left, right, (((0,), (0,)), ((), ())), preferred_element_type=jnp.float32
    )


def times_transposed(left, right):
    return lax.dot_general(
        left, right, (((1,), (1,)), ((), ())), preferred_element_type=jnp.float32
    )


def unchanged(state):
    return state


def times(left, right, a, b):
    return lax.dot_general(left, right, (((a,), (b,)), ((), ())), preferred_element_type=jnp.float32)


def vmem(count):
    return [pl.BlockSpec(memory_space=pltpu.VMEM)] * count


def kernel_params():
    return pltpu.CompilerParams(vmem_limit_bytes=56 * 2**20)


def cost(flops, nbytes, transcendentals=0):
    return pl.CostEstimate(flops=int(flops), bytes_accessed=int(nbytes), transcendentals=int(transcendentals))


def causal_mask(span):
    key_at = lax.broadcasted_iota(jnp.int32, (span, span), 0)
    query_at = lax.broadcasted_iota(jnp.int32, (span, span), 1)
    return key_at <= query_at


def front_kernel(raw, rep, head, span, base, spot_ref, owner_ref, at_ref, *refs):
    *blocks, gain_ref, w0, w1, w2, w3, normed_ref, qkv_ref, sent_ref, exact_ref, log_ref = refs
    rows = blocks[0].shape[0]
    count = len(blocks) - 1
    tokens = count * rows
    width = rep * head
    scale = head ** (-0.5)
    gain = gain_ref[...]
    for k in range(count):
        low, high = (blocks[k],) * 2 if k < count - 1 else blocks[k:]
        half = low.shape[0] if k == count - 1 else rows
        for start, ref in ((0, low), (half, high)) if k == count - 1 else ((0, low),):
            block = ref[...]
            if raw:
                block = rms_scale(block.astype(jnp.float32), gain).astype(jnp.bfloat16)
            normed_ref[spot_ref[k], start : start + ref.shape[0], :] = block
    lanes_all = qkv_ref.shape[0]
    slice_width = w0.shape[1]
    for part in range(tokens // span):
        take = span // rows
        total = 0.0
        for m, weight_ref in enumerate((w0, w1, w2, w3)):
            lanes = pl.ds(pl.multiple_of(at_ref[m] * slice_width, 128), slice_width)
            piece = normed_ref[part * take : (part + 1) * take, :, lanes].reshape(span, slice_width)
            total = total + times(weight_ref[base : base + lanes_all, :], piece, 1, 1)
        qkv_ref[:, part * span : (part + 1) * span] = total.astype(jnp.bfloat16)
    mask = causal_mask(span)
    per = span // rows
    for part in range(tokens // span):
        lanes = pl.ds(part * span, span)
        seen = (part + 1) * span
        keys = qkv_ref[width : width + head, :seen]
        values = qkv_ref[width + head : lanes_all, :seen]
        for h in range(rep):
            at = slice(h * head, (h + 1) * head)
            scores = times(keys, qkv_ref[at, lanes], 0, 0) * scale
            last = jnp.where(mask, scores[seen - span :], NEG)
            top = jnp.max(last, axis=0, keepdims=True)
            if part:
                top = jnp.maximum(top, jnp.max(scores[: seen - span], axis=0, keepdims=True))
            weights = jnp.exp(last - top)
            if part:
                weights = jnp.concatenate([jnp.exp(scores[: seen - span] - top), weights], axis=0)
            total = jnp.sum(weights, axis=0, keepdims=True)
            result = times(values, weights.astype(jnp.bfloat16), 1, 0) / total
            exact_ref[at, lanes] = result
            log_ref[h : h + 1, lanes] = top + jnp.log(total)
            for b in range(per):
                sent_ref[owner_ref[part * per + b], at, :] = result[:, b * rows : (b + 1) * rows].astype(jnp.bfloat16)


def front(raw, spots, owner_of, at, blocks, gain, pieces, base, rep, head):
    rows, width = blocks[0].shape
    count = len(blocks) - 1
    tokens = count * rows
    span = min(256, tokens)
    deep = (rep + 2) * head
    pairs = rep * tokens * (tokens + span) // 2
    return pl.pallas_call(
        functools.partial(front_kernel, raw, rep, head, span, base),
        out_shape=(
            jax.ShapeDtypeStruct((count, rows, width), jnp.bfloat16),
            jax.ShapeDtypeStruct((deep, tokens), jnp.bfloat16),
            jax.ShapeDtypeStruct((count, rep * head, rows), jnp.bfloat16),
            jax.ShapeDtypeStruct((rep * head, tokens), jnp.float32),
            jax.ShapeDtypeStruct((rep, tokens), jnp.float32),
        ),
        in_specs=[pl.BlockSpec(memory_space=pltpu.SMEM)] * 3 + vmem(len(blocks) + 5),
        out_specs=tuple(vmem(5)),
        compiler_params=kernel_params(),
        cost_estimate=cost(4 * head * pairs + 2 * deep * width * tokens, 9 * 2**20, pairs),
        name="front",
    )(spots, owner_of, at, *blocks, gain, *pieces)


def attend_back_kernel(rep, head, span, owner_ref, qkv_ref, exact_ref, log_ref, grad_ref, whole_ref, sent_ref, grad_all, keys_sum, values_sum):
    tokens = qkv_ref.shape[1]
    rows = grad_ref.shape[2]
    width = rep * head
    per = span // rows
    scale = head ** (-0.5)
    mask = causal_mask(span)
    for block in range(tokens // rows):
        grad_all[:, block * rows : (block + 1) * rows] = grad_ref[owner_ref[block]]
    keys_sum[...] = jnp.zeros_like(keys_sum)
    values_sum[...] = jnp.zeros_like(values_sum)
    for part in range(tokens // span):
        lanes = pl.ds(part * span, span)
        seen = (part + 1) * span
        keys = qkv_ref[width : width + head, :seen]
        values = qkv_ref[width + head :, :seen]
        for h in range(rep):
            at = slice(h * head, (h + 1) * head)
            queries = qkv_ref[at, lanes]
            grads = grad_all[at, lanes]
            delta = jnp.sum(grads.astype(jnp.float32) * exact_ref[at, lanes], axis=0, keepdims=True)
            scores = times(keys, queries, 0, 0) * scale
            probs = jnp.exp(scores - log_ref[h : h + 1, lanes])
            last = jnp.where(mask, probs[seen - span :], 0.0)
            probs = last if part == 0 else jnp.concatenate([probs[: seen - span], last], axis=0)
            pulled = times(values, grads, 0, 0)
            slopes = (probs * (pulled - delta)).astype(jnp.bfloat16)
            back = (times(keys, slopes, 1, 0) * scale).astype(jnp.bfloat16)
            whole_ref[at, lanes] = back
            for b in range(per):
                sent_ref[owner_ref[part * per + b], at, :] = back[:, b * rows : (b + 1) * rows]
            keys_sum[:, :seen] += times(queries, slopes, 1, 1)
            values_sum[:, :seen] += times(grads, probs.astype(jnp.bfloat16), 1, 1)
    keys_low = (keys_sum[...] * scale).astype(jnp.bfloat16)
    values_low = values_sum[...].astype(jnp.bfloat16)
    whole_ref[width : width + head, :] = keys_low
    whole_ref[width + head :, :] = values_low
    for block in range(tokens // rows):
        cut = slice(block * rows, (block + 1) * rows)
        sent_ref[owner_ref[block], width : width + head, :] = keys_low[:, cut]
        sent_ref[owner_ref[block], width + head :, :] = values_low[:, cut]


def attend_back(owner_of, qkv, exact, log_total, grads, rep, head):
    deep, tokens = qkv.shape
    count, _, rows = grads.shape
    span = min(256, tokens)
    pairs = rep * tokens * (tokens + span) // 2
    return pl.pallas_call(
        functools.partial(attend_back_kernel, rep, head, span),
        out_shape=(
            jax.ShapeDtypeStruct((deep, tokens), jnp.bfloat16),
            jax.ShapeDtypeStruct((count, deep, rows), jnp.bfloat16),
        ),
        in_specs=[pl.BlockSpec(memory_space=pltpu.SMEM)] + vmem(4),
        out_specs=tuple(vmem(2)),
        scratch_shapes=[
            pltpu.VMEM((rep * head, tokens), jnp.bfloat16),
            pltpu.VMEM((head, tokens), jnp.float32),
            pltpu.VMEM((head, tokens), jnp.float32),
        ],
        compiler_params=kernel_params(),
        cost_estimate=cost(10 * head * pairs, 6 * 2**20, pairs),
        name="attend_back",
    )(owner_of, qkv, exact, log_total, grads)


def silu_pair(gate_value, up_value):
    return (gate_value * jax.nn.sigmoid(gate_value) * up_value).astype(jnp.bfloat16)


def pair_back(grad_inner, gate_value, up_value):
    sigma = jax.nn.sigmoid(gate_value)
    grad_gate = grad_inner * up_value * sigma * (1.0 + gate_value * (1.0 - sigma))
    return grad_gate.astype(jnp.bfloat16), (grad_inner * gate_value * sigma).astype(jnp.bfloat16)


def by_piece(gate, up, down):
    return [piece for pieces in zip(gate, up, down) for piece in pieces]


def expert_forward_kernel(rows_ref, *refs):
    weights, (made_ref, gates_ref, ups_ref, inner_ref, total) = refs[:12], refs[12:]
    rows = rows_ref[...]
    for m in range(4):
        gate_value = times(rows, weights[3 * m][...], 1, 0)
        up_value = times(rows, weights[3 * m + 1][...], 1, 0)
        gates_ref[m] = gate_value
        ups_ref[m] = up_value
        inner = silu_pair(gate_value, up_value)
        inner_ref[m] = inner
        part = times(inner, weights[3 * m + 2][...], 1, 0)
        if m == 0:
            total[...] = part
        elif m < 3:
            total[...] += part
        else:
            made_ref[...] = (total[...] + part).astype(jnp.bfloat16)


def expert_forward(rows, gate, up, down):
    count, width = rows.shape
    hidden = gate[0].shape[1]
    weights = by_piece(gate, up, down)
    return pl.pallas_call(
        expert_forward_kernel,
        out_shape=(
            jax.ShapeDtypeStruct((count, width), jnp.bfloat16),
            jax.ShapeDtypeStruct((4, count, hidden), jnp.float32),
            jax.ShapeDtypeStruct((4, count, hidden), jnp.float32),
            jax.ShapeDtypeStruct((4, count, hidden), jnp.bfloat16),
        ),
        in_specs=vmem(1) + vmem(12),
        out_specs=tuple(vmem(4)),
        scratch_shapes=[pltpu.VMEM((count, width), jnp.float32)],
        compiler_params=kernel_params(),
        cost_estimate=cost(24 * count * width * hidden, 16 * 2**20, 4 * count * hidden),
        name="expert_forward",
    )(rows, *weights)


def expert_backward_kernel(grad_ref, *refs):
    weights, (gates, ups, back_ref, grad_gate_ref, grad_up_ref, total) = refs[2:14], refs[:2] + refs[14:]
    grads = grad_ref[...]
    for m in range(4):
        grad_inner = times(grads, weights[3 * m + 2][...], 1, 1)
        grad_gate, grad_up = pair_back(grad_inner, gates[m], ups[m])
        grad_gate_ref[m] = grad_gate
        grad_up_ref[m] = grad_up
        part = times(grad_gate, weights[3 * m][...], 1, 1) + times(grad_up, weights[3 * m + 1][...], 1, 1)
        if m == 0:
            total[...] = part
        elif m < 3:
            total[...] += part
        else:
            back_ref[...] = (total[...] + part).astype(jnp.bfloat16)


def expert_backward(grads, gate, up, down, gates, ups):
    count, width = grads.shape
    hidden = gate[0].shape[1]
    weights = [gates, ups] + by_piece(gate, up, down)
    return pl.pallas_call(
        expert_backward_kernel,
        out_shape=(
            jax.ShapeDtypeStruct((count, width), jnp.bfloat16),
            jax.ShapeDtypeStruct((4, count, hidden), jnp.bfloat16),
            jax.ShapeDtypeStruct((4, count, hidden), jnp.bfloat16),
        ),
        in_specs=vmem(1) + vmem(14),
        out_specs=tuple(vmem(3)),
        scratch_shapes=[pltpu.VMEM((count, width), jnp.float32)],
        compiler_params=kernel_params(),
        cost_estimate=cost(24 * count * width * hidden, 16 * 2**20, 4 * count * hidden),
        name="expert_backward",
    )(grads, *weights)


def expert_both_kernel(experts, mine_ref, rows_ref, cot_ref, router_ref, *refs):
    weights, outs = refs[:12], refs[12:]
    made_ref, back_ref, grad_ref, inner_ref, grad_gate_ref, grad_up_ref, total, total_back = outs
    rows = rows_ref[...]
    count, width = rows.shape
    cot = cot_ref[:, :width].astype(jnp.float32)
    logits = times(rows, router_ref[...], 1, 1)
    ids = lax.broadcasted_iota(jnp.int32, logits.shape, 1)
    logits = jnp.where(ids < experts, logits, NEG)
    odds = jnp.exp(logits - jnp.max(logits, axis=1, keepdims=True))
    other = cot_ref[:, width : width + 1].astype(jnp.float32).astype(jnp.int32)
    own_odds = jnp.sum(jnp.where(ids == mine_ref[0], odds, 0.0), axis=1, keepdims=True)
    other_odds = jnp.sum(jnp.where(ids == other, odds, 0.0), axis=1, keepdims=True)
    grad_ref[...] = (own_odds / (own_odds + other_odds) * cot).astype(jnp.bfloat16)
    grads = grad_ref[...]
    for m in range(4):
        gate, up = weights[3 * m], weights[3 * m + 1]
        gate_value = times(rows, gate[...], 1, 0)
        up_value = times(rows, up[...], 1, 0)
        inner = silu_pair(gate_value, up_value)
        inner_ref[m] = inner
        down = weights[3 * m + 2]
        grad_gate, grad_up = pair_back(times(grads, down[...], 1, 1), gate_value, up_value)
        grad_gate_ref[m] = grad_gate
        grad_up_ref[m] = grad_up
        part = times(inner, down[...], 1, 0)
        part_back = times(grad_gate, gate[...], 1, 1) + times(grad_up, up[...], 1, 1)
        total[...] = part if m == 0 else total[...] + part
        total_back[...] = part_back if m == 0 else total_back[...] + part_back
    made = total[...].astype(jnp.bfloat16)
    made_ref[...] = made
    back_ref[:, :width] = total_back[...].astype(jnp.bfloat16)
    signal = jnp.sum(cot * made.astype(jnp.float32), axis=1, keepdims=True)
    high = signal.astype(jnp.bfloat16)
    low = (signal - high.astype(jnp.float32)).astype(jnp.bfloat16)
    at = lax.broadcasted_iota(jnp.int32, (count, back_ref.shape[1] - width), 1)
    back_ref[:, width:] = jnp.where(
        at == 0, high.astype(jnp.float32), jnp.where(at == 1, low.astype(jnp.float32), 0.0)
    ).astype(jnp.bfloat16)


def expert_both(experts, mine, rows, cot, router, gate, up, down):
    count, width = rows.shape
    hidden = gate[0].shape[1]
    weights = by_piece(gate, up, down)
    return pl.pallas_call(
        functools.partial(expert_both_kernel, experts),
        out_shape=(
            jax.ShapeDtypeStruct((count, width), jnp.bfloat16),
            jax.ShapeDtypeStruct(cot.shape, jnp.bfloat16),
            jax.ShapeDtypeStruct((count, width), jnp.bfloat16),
            jax.ShapeDtypeStruct((4, count, hidden), jnp.bfloat16),
            jax.ShapeDtypeStruct((4, count, hidden), jnp.bfloat16),
            jax.ShapeDtypeStruct((4, count, hidden), jnp.bfloat16),
        ),
        in_specs=[pl.BlockSpec(memory_space=pltpu.SMEM)] + vmem(3) + vmem(12),
        out_specs=tuple(vmem(6)),
        scratch_shapes=[pltpu.VMEM((count, width), jnp.float32)] * 2,
        compiler_params=kernel_params(),
        cost_estimate=cost(48 * count * width * hidden, 18 * 2**20, 8 * count * hidden),
        name="expert_both",
    )(mine, rows, cot, router, *weights)


def expert_grads_kernel(rows_ref, grad_ref, inner_ref, grad_gate_ref, grad_up_ref, pair_give, far_give, pair_own, pair_far, down_give, down_own, down_far):
    for m, (pairs, at, downs, down_at) in enumerate(
        (
            (pair_own, 0, down_own, 0),
            (pair_give, 0, down_give, 0),
            (pair_far, 0, down_far, 0),
            (far_give, 0, down_give, 1),
        )
    ):
        pairs[at] = times(rows_ref[...], grad_gate_ref[m], 0, 0).astype(jnp.bfloat16)
        pairs[at + 1] = times(rows_ref[...], grad_up_ref[m], 0, 0).astype(jnp.bfloat16)
        downs[down_at] = times(inner_ref[m], grad_ref[...], 0, 0).astype(jnp.bfloat16)


def expert_grads(rows, grads, inner, grad_gate, grad_up):
    count, width = rows.shape
    hidden = inner.shape[2]
    shapes = [(2, width, hidden)] * 4
    shapes += [(2, hidden, width), (1, hidden, width), (1, hidden, width)]
    return pl.pallas_call(
        expert_grads_kernel,
        out_shape=tuple(jax.ShapeDtypeStruct(shape, jnp.bfloat16) for shape in shapes),
        in_specs=vmem(5),
        out_specs=tuple(vmem(7)),
        compiler_params=kernel_params(),
        cost_estimate=cost(24 * count * width * hidden, 14 * 2**20),
        name="expert_grads",
    )(rows, grads, inner, grad_gate, grad_up)


def head_grads_kernel(part, at_ref, normed_ref, whole_ref, small_ref, give_ref, own_ref, far_ref):
    tokens = whole_ref.shape[1]
    deep = whole_ref.shape[0]
    for m, (ref, slot) in enumerate(((own_ref, 0), (give_ref, 0), (far_ref, 0), (give_ref, 1))):
        lanes = pl.ds(pl.multiple_of(at_ref[m] * part, 128), part)
        rows = normed_ref[:, :, lanes].reshape(tokens, part)
        ref[slot, :deep, :] = times(whole_ref[...], rows, 1, 0).astype(jnp.bfloat16)
        ref[slot, deep:, :] = small_ref[:, lanes].astype(jnp.bfloat16)


def head_grads(at, normed, whole, small):
    deep, tokens = whole.shape
    width = normed.shape[2]
    part = width // 4
    full = deep + small.shape[0]
    return pl.pallas_call(
        functools.partial(head_grads_kernel, part),
        out_shape=tuple(jax.ShapeDtypeStruct((n, full, part), jnp.bfloat16) for n in (2, 1, 1)),
        in_specs=[pl.BlockSpec(memory_space=pltpu.SMEM)] + vmem(3),
        out_specs=tuple(vmem(3)),
        compiler_params=kernel_params(),
        cost_estimate=cost(2**20, 2**16),
        name="head_grads",
    )(at, normed, whole, small)


def spread_kernel(wide, head, ringed, *refs):
    if ringed:
        spot_ref, *blocks, query_ref, key_ref, value_ref = refs[: ringed + 4]
        gathered_ref = refs[-1]
        outs = refs[-7:-1]
        for k, block in enumerate(blocks[:-2]):
            gathered_ref[spot_ref[k]] = block[...]
        half = blocks[-2].shape[0]
        gathered_ref[spot_ref[ringed - 2], :half, :] = blocks[-2][...]
        gathered_ref[spot_ref[ringed - 2], half:, :] = blocks[-1][...]
    else:
        gathered_ref, query_ref, key_ref, value_ref = refs[:4]
        outs = refs[-6:]
    query_out, key_out, value_out, out_out, small_out, sum_ref = outs
    count, _, part = gathered_ref.shape
    deep = wide + 2 * head
    small = small_out.shape[0]
    sums = jnp.zeros((part, 1), jnp.float32)
    for i in range(count // 2):
        block = gathered_ref[2 * i : 2 * i + 2, :wide, :].astype(jnp.float32).reshape(2 * wide, part).T
        lanes = slice(2 * i * wide, 2 * (i + 1) * wide)
        query_out[0, :, lanes] = block
        sums += jnp.sum(block * query_ref[:, lanes].astype(jnp.float32), axis=1, keepdims=True)
    for start, weight_ref, out in ((wide, key_ref, key_out), (wide + head, value_ref, value_out)):
        block = gathered_ref[:, start : start + head, :].astype(jnp.float32).reshape(count * head, part).T
        out[0] = block
        sums += jnp.sum(block * weight_ref[...].astype(jnp.float32), axis=1, keepdims=True)
    sum_ref[...] = sums
    total = gathered_ref[0, deep : deep + small, :].astype(jnp.float32)
    for c in range(1, count):
        total += gathered_ref[c, deep : deep + small, :].astype(jnp.float32)
    small_out[...] = total
    rows = part // count
    for c in range(count):
        for j in range(out_out.shape[2] // part):
            piece = gathered_ref[c, deep + small + j * rows : deep + small + (j + 1) * rows, :]
            out_out[0, c * rows : (c + 1) * rows, j * part : (j + 1) * part] = piece.astype(jnp.float32)


def spread(layer, layers, spots, sources, weights, wide, head, small, before):
    ringed = len(sources) if spots is not None else 0
    part = weights[0].shape[0]
    width = weights[0].shape[1]
    count = width // wide
    shapes = [(layers,) + weight.shape for weight in weights] + [(layers, part, width)]
    aliased = [] if before is None else list(before)
    one = lambda shape: pl.BlockSpec((1,) + shape[1:], lambda i: (layer, 0, 0))
    whole = lambda shape: pl.BlockSpec(shape, lambda i: (0,) * len(shape))
    deep = sources[0].shape[-2]
    lead = [spots] if ringed else []
    return pl.pallas_call(
        functools.partial(spread_kernel, wide, head, ringed),
        grid=(1,),
        out_shape=tuple(jax.ShapeDtypeStruct(shape, jnp.float32) for shape in shapes)
        + (jax.ShapeDtypeStruct((small, part), jnp.float32), jax.ShapeDtypeStruct((part, 1), jnp.float32)),
        in_specs=[pl.BlockSpec(memory_space=pltpu.SMEM)] * len(lead)
        + [whole(source.shape) for source in sources]
        + [whole(weight.shape) for weight in weights]
        + [pl.BlockSpec(memory_space=pl.ANY)] * len(aliased),
        out_specs=tuple(one(shape) for shape in shapes) + (whole((small, part)), whole((part, 1))),
        scratch_shapes=[pltpu.VMEM((count, deep, part), jnp.bfloat16)] if ringed else [],
        input_output_aliases={len(lead) + len(sources) + 3 + i: i for i in range(len(aliased))},
        compiler_params=kernel_params(),
        cost_estimate=cost(2**20, 2**16),
        name="spread",
    )(*lead, *sources, *weights, *aliased)


def finish_kernel(*refs):
    own_ref, near_ref = refs[:2]
    count = own_ref.shape[0]
    for i, (far_ref, out) in enumerate(zip(refs[2 : 2 + count], refs[-count:])):
        total = own_ref[i].astype(jnp.float32) + near_ref[i].astype(jnp.float32) + far_ref[...].astype(jnp.float32)
        out[0, 0] = total


def finish(layer, layers, own, near, far, before):
    count, rows, columns = own.shape
    steps = 2
    block = rows // steps
    aliased = [] if before is None else list(before)
    taken = pl.BlockSpec((count, block, columns), lambda i: (0, i, 0))
    made = pl.BlockSpec((1, 1, block, columns), lambda i: (layer, 0, i, 0))
    return pl.pallas_call(
        finish_kernel,
        grid=(steps,),
        out_shape=tuple(jax.ShapeDtypeStruct((layers, 1, rows, columns), jnp.float32) for _ in range(count)),
        in_specs=[taken] * 2
        + [pl.BlockSpec((block, columns), lambda i: (i, 0))] * count
        + [pl.BlockSpec(memory_space=pl.ANY)] * len(aliased),
        out_specs=(made,) * count,
        input_output_aliases={2 + count + i: i for i in range(len(aliased))},
        compiler_params=kernel_params(),
        cost_estimate=cost(2**20, 2**16),
        name="finish",
    )(own, near, *far, *aliased)


def head_rows_kernel(wide, head, at_ref, query_ref, key_ref, value_ref, small_ref, out_ref):
    odd = at_ref[0] % 2
    top = 0
    for ref, size in ((query_ref, wide), (key_ref, head), (value_ref, head)):
        turned = ref[0].astype(jnp.float32).T
        out_ref[0, top : top + size, :] = jnp.where(odd == 1, turned[size:], turned[:size]).astype(jnp.bfloat16)
        top += size
    out_ref[0, top:, :] = small_ref[0]


def head_rows(mine, query_weight, key_weight, value_weight, small, wide, head):
    layers, part, _ = query_weight.shape
    rows = wide + 2 * head + small.shape[1]
    taken = lambda size: pl.BlockSpec((1, part, 2 * size), lambda i, at: (i, 0, at[0] // 2))
    return pl.pallas_call(
        functools.partial(head_rows_kernel, wide, head),
        grid_spec=pltpu.PrefetchScalarGridSpec(
            num_scalar_prefetch=1,
            grid=(layers,),
            in_specs=[taken(wide), taken(head), taken(head), pl.BlockSpec((1,) + small.shape[1:], lambda i, at: (i, 0, 0))],
            out_specs=pl.BlockSpec((1, rows, part), lambda i, at: (i, 0, 0)),
        ),
        out_shape=jax.ShapeDtypeStruct((layers, rows, part), jnp.bfloat16),
        compiler_params=kernel_params(),
        cost_estimate=cost(2**20, 2**16),
        name="head_rows",
    )(mine, query_weight, key_weight, value_weight, small)


def middle_forward_kernel(at_ref, attended_ref, state_ref, gain_ref, place_ref, *refs):
    weights, (middle_ref, mixed_ref, out_ref) = refs[:4], refs[4:]
    part = weights[0].shape[0]
    total = state_ref[...]
    for m in range(4):
        rows = attended_ref[pl.ds(pl.multiple_of(at_ref[m] * part, 128), part), :]
        total = total + times(rows, weights[m][...], 0, 0)
    middle_ref[...] = total
    mixed = rms_scale(total, gain_ref[...]).astype(jnp.bfloat16)
    mixed_ref[...] = mixed
    out_ref[...] = times(place_ref[0] + place_ref[1], mixed, 0, 0).astype(jnp.bfloat16)


def middle_forward(at, attended, pieces, state, gain, place):
    rows, width = state.shape
    slots = place.shape[2]
    return pl.pallas_call(
        middle_forward_kernel,
        out_shape=(
            jax.ShapeDtypeStruct((rows, width), jnp.float32),
            jax.ShapeDtypeStruct((rows, width), jnp.bfloat16),
            jax.ShapeDtypeStruct((slots, width), jnp.bfloat16),
        ),
        in_specs=[pl.BlockSpec(memory_space=pltpu.SMEM)] + vmem(4) + vmem(4),
        out_specs=tuple(vmem(3)),
        compiler_params=kernel_params(),
        cost_estimate=cost(2 * rows * width * (width + slots), 9 * 2**20),
        name="middle_forward",
    )(at, attended, state, gain, place, *pieces)


def middle_back_kernel(experts, at_ref, place_ref, back_ref, upstream_ref, middle_ref, mixed_ref, gain_ref, router_ref, chosen_ref, *refs):
    *results, w0, w1, w2, w3, grad_ref, low_ref, heads_ref, small_ref = refs
    weights = (w0, w1, w2, w3)
    rows, width = upstream_ref.shape
    part = w0.shape[0]
    upstream, mixed, router = upstream_ref[...], mixed_ref[...], router_ref[...]
    logits = times(mixed, router, 1, 1)
    ids = lax.broadcasted_iota(jnp.int32, logits.shape, 1)
    logits = jnp.where(ids < experts, logits, NEG)
    odds = jnp.exp(logits - jnp.max(logits, axis=1, keepdims=True))
    probs = odds / jnp.sum(odds, axis=1, keepdims=True)
    hits = [ids == chosen_ref[:, c : c + 1] for c in range(2)]
    picked = [jnp.sum(jnp.where(hit, probs, 0.0), axis=1, keepdims=True) for hit in hits]
    pair_total = picked[0] + picked[1]
    if results:
        signal = [jnp.sum(upstream * r[...].astype(jnp.float32), axis=1, keepdims=True) for r in results]
    else:
        signal = [jnp.sum(times(place_ref[c], back_ref[:, width:], 1, 0), axis=1, keepdims=True) for c in range(2)]
    mean = (picked[0] * signal[0] + picked[1] * signal[1]) / pair_total
    slopes = [(s - mean) / pair_total for s in signal]
    grad_probs = jnp.where(hits[0], slopes[0], 0.0) + jnp.where(hits[1], slopes[1], 0.0)
    grad_logits = probs * (grad_probs - jnp.sum(probs * grad_probs, axis=1, keepdims=True))
    high = grad_logits.astype(jnp.bfloat16)
    rest = (grad_logits - high.astype(jnp.float32)).astype(jnp.bfloat16)
    small_ref[...] = jnp.zeros_like(small_ref)
    router_part = times(high, mixed, 0, 0) + times(rest, mixed, 0, 0)
    small_ref[:experts, :] = router_part[:experts]
    grad_mixed = times(place_ref[0] + place_ref[1], back_ref[:, :width], 1, 0)
    grad_mixed = grad_mixed + times(high, router, 1, 0) + times(rest, router, 1, 0)
    pulled, gain_rows = rms_back(middle_ref[...], gain_ref[...], grad_mixed)
    small_ref[experts : experts + 1, :] = jnp.sum(gain_rows, axis=0, keepdims=True)
    grad = upstream + pulled
    grad_ref[...] = grad
    low = grad.astype(jnp.bfloat16)
    low_ref[...] = low
    for m in range(4):
        lanes = pl.ds(pl.multiple_of(at_ref[m] * part, 128), part)
        heads_ref[lanes, :] = times(weights[m][...], low, 1, 1).astype(jnp.bfloat16)


def middle_back(experts, at, place, back, upstream, middle, mixed, gain, router, chosen, results, pieces):
    rows, width = upstream.shape
    slots = place.shape[2]
    return pl.pallas_call(
        functools.partial(middle_back_kernel, experts),
        out_shape=(
            jax.ShapeDtypeStruct((rows, width), jnp.float32),
            jax.ShapeDtypeStruct((rows, width), jnp.bfloat16),
            jax.ShapeDtypeStruct((width, rows), jnp.bfloat16),
            jax.ShapeDtypeStruct((experts + 8, width), jnp.float32),
        ),
        in_specs=[pl.BlockSpec(memory_space=pltpu.SMEM)] + vmem(8 + len(results)) + vmem(4),
        out_specs=tuple(vmem(4)),
        compiler_params=kernel_params(),
        cost_estimate=cost(2 * rows * width * (width + slots), 10 * 2**20),
        name="middle_back",
    )(at, place, back, upstream, middle, mixed, gain, router, chosen, *results, *pieces)


def swap(x, mask):
    return lax.ppermute(x, "wt", [(i, i ^ mask) for i in range(4)])


def near_finish(far, own):
    return (own, swap(own, 1), far, swap(far, 1))


def wt_gather(own):
    return near_finish(swap(own, 2), own)


def wt_exchange(slices, me):
    def cut(m):
        return lax.dynamic_index_in_dim(slices, me ^ m, 0, keepdims=False)

    far = swap(jnp.stack([cut(2), cut(3)]), 2)
    near = swap(jnp.stack([cut(1), far[1]]), 1)
    return (cut(0), near[0], far[0], near[1])


def in_order(pieces, me, axis):
    own, near, far, last = pieces
    odd, high = me % 2 == 1, me >= 2
    low = (jnp.where(odd, near, own), jnp.where(odd, own, near))
    up = (jnp.where(odd, last, far), jnp.where(odd, far, last))
    first = [jnp.where(high, b, a) for a, b in zip(low, up)]
    second = [jnp.where(high, a, b) for a, b in zip(low, up)]
    return jnp.concatenate(first + second, axis=axis)


def tie(*arrays):
    return lax.optimization_barrier(arrays)


def ring_of(count):
    ring = list(range(0, count, 2)) + list(range(count - 1, 0, -2))
    offsets = [0] + [sign * step for step in range(1, count // 2) for sign in (-1, 1)] + [count // 2]
    table = [[ring[(ring.index(i) + k) % count] for k in offsets] for i in range(count)]
    return ring, jnp.asarray(table, jnp.int32)


def ring_start(x, ring):
    right = [(a, b) for a, b in zip(ring, ring[1:] + ring[:1])]
    left = [(b, a) for a, b in right]
    return lax.ppermute(x, "ctx", right), lax.ppermute(x, "ctx", left)


def ring_blocks(x, first, ring, early=None):
    count = len(ring)
    right = [(a, b) for a, b in zip(ring, ring[1:] + ring[:1])]
    left = [(b, a) for a, b in right]
    ahead, behind = first
    blocks = [x, ahead, behind]
    for _ in range(2, count // 2):
        ahead, behind = lax.ppermute(ahead, "ctx", right), lax.ppermute(behind, "ctx", left)
        blocks += [ahead, behind]
    if early is not None:
        ahead, behind, *early = tie(ahead, behind, *early)
    half = x.shape[0] // 2
    blocks += [lax.ppermute(ahead[:half], "ctx", right), lax.ppermute(behind[half:], "ctx", left)]
    return blocks if early is None else (blocks, early)


def all_to_all(x):
    return lax.all_to_all(x, "ctx", split_axis=0, concat_axis=0, tiled=True)


def rms_back(rows, gain, grad):
    scale = lax.rsqrt(jnp.mean(rows * rows, axis=-1, keepdims=True) + EPS)
    unit = rows * scale
    pulled = grad * gain
    return scale * (pulled - unit * jnp.mean(pulled * unit, axis=-1, keepdims=True)), grad * unit


def by_heads(mesh, tokens, cotangent, seq_lengths, block_deal, *rest):
    return (
        mesh.shape["ctx"] == KV_HEADS
        and mesh.shape["wt"] == 4
        and seq_lengths.shape[1] == 1
        and block_deal.shape[2] == 1
        and tokens.shape[1] == BLK
    )


def local_heads(
    mesh,
    tokens,
    cotangent,
    seq_lengths,
    block_deal,
    routes,
    attention_gain,
    query_weight,
    key_weight,
    value_weight,
    out_weight,
    mixture_gain,
    router_weight,
    gate_weight,
    up_weight,
    down_weight,
):
    n_ctx = mesh.shape["ctx"]
    rows = tokens.shape[1]
    width = tokens.shape[2]
    layers = query_weight.shape[0]
    experts = router_weight.shape[2]
    capacity = 3 * rows // experts
    slot_count = experts * capacity
    rep = HEADS // KV_HEADS
    wide = rep * HEAD
    lanes = wide + 2 * HEAD
    part = width // 4
    ctx = lax.axis_index("ctx")
    mine = ctx.astype(jnp.int32).reshape(1)
    wt = lax.axis_index("wt").astype(jnp.uint32)
    others = (wt ^ jnp.arange(4, dtype=jnp.uint32)).astype(jnp.int32)
    table = block_deal[0, :, 0]
    devices = jnp.arange(n_ctx, dtype=jnp.int32)
    owner_of = jnp.sum(jnp.where(table[None, :] == devices[:, None], devices[None, :], 0), axis=1)
    ring, ring_table = ring_of(n_ctx)
    ring_owners = lax.dynamic_index_in_dim(ring_table, ctx.astype(jnp.uint32), 0, keepdims=False)
    spots = jnp.sum(jnp.where(ring_owners[:, None] == devices[None, :], table[None, :], 0), axis=1)

    first = ring_start(tokens[0], ring)

    expert_ids = jnp.arange(experts, dtype=jnp.int32)
    chosen = routes[:, 0]
    flat = chosen.reshape(layers, 2 * rows)
    onehot = flat[:, :, None] == expert_ids
    earlier = jnp.tril(jnp.ones((2 * rows, 2 * rows), jnp.bfloat16), -1)
    rank = jnp.einsum("ij,lje->lie", earlier, onehot.astype(jnp.bfloat16), preferred_element_type=jnp.float32)
    rank = jnp.sum(jnp.where(onehot, rank, 0.0), axis=2).astype(jnp.int32)
    slots = (flat * capacity + rank).reshape(layers, rows, 2).transpose(0, 2, 1)
    place = (slots[..., None] == jnp.arange(slot_count, dtype=jnp.int32)).astype(jnp.bfloat16)
    named = (chosen.transpose(0, 2, 1)[..., None] == expert_ids).astype(jnp.float32)

    small_rows = jnp.concatenate(
        [
            router_weight.transpose(0, 2, 1),
            attention_gain[:, None],
            mixture_gain[:, None],
            jnp.zeros((layers, 14 - experts, part), jnp.bfloat16),
        ],
        axis=1,
    )
    deep = lanes + 16
    head_own = head_rows(mine, query_weight, key_weight, value_weight, small_rows, wide, HEAD)
    head_own = head_own.reshape(layers * deep, part)
    head_far = swap(head_own, 2)

    out_own = list(out_weight)
    gate_own = [gate_weight[layer, 0] for layer in range(layers)]
    up_own = [up_weight[layer, 0] for layer in range(layers)]
    down_own = [down_weight[layer, 0] for layer in range(layers)]
    query_own = list(query_weight)
    pair_own_weights = [jnp.concatenate([key_weight[layer], value_weight[layer]], axis=1) for layer in range(layers)]
    out_far, gate_far, up_far, down_far, query_far, key_far = [
        [swap(own, 2) for own in group]
        for group in (out_own, gate_own, up_own, down_own, query_own, pair_own_weights)
    ]

    last = layers - 1
    other = chosen[last].transpose(1, 0)[::-1, :, None].astype(jnp.bfloat16)
    cot_rows = jnp.concatenate(
        [jnp.broadcast_to(cotangent[0][None], (2, rows, width)), jnp.broadcast_to(other, (2, rows, 128))], axis=2
    ).reshape(2 * rows, width + 128)
    cot_out = times(place[last].reshape(2 * rows, slot_count), cot_rows, 0, 0).astype(jnp.bfloat16)

    state = tokens[0].astype(jnp.float32)
    saved = []
    for layer in range(layers):
        if layer == 0:
            blocks, head_pieces = ring_blocks(tokens[0], first, ring, near_finish(head_far, head_own))
            small_all = [
                in_order([piece[i * deep + lanes : (i + 1) * deep] for piece in head_pieces], wt, 1)
                for i in range(layers)
            ]
            cot_out = tie(cot_out, *blocks[-2:])[0]
            cot_slots = all_to_all(cot_out.reshape(experts, capacity, width + 128)).reshape(slot_count, width + 128)
        router = jnp.concatenate([small_all[layer][:experts], jnp.zeros((128 - experts, width), jnp.bfloat16)])
        gain_one = small_all[layer][experts : experts + 1].astype(jnp.float32)
        gain_two = small_all[layer][experts + 1 : experts + 2].astype(jnp.float32)
        if layer > 0:
            normed = rms_scale(state, gain_one).astype(jnp.bfloat16)
            blocks = ring_blocks(normed, ring_start(normed, ring), ring)
        normed_all, qkv, sent, exact, log_total = front(
            layer == 0, spots, owner_of, others, blocks, gain_one, head_pieces, layer * deep, rep, HEAD
        )
        if layer == 0:
            sent, cot_slots = tie(sent, cot_slots)
        else:
            sent, out_far[layer], up_far[layer] = tie(sent, out_far[layer], up_far[layer])
        attended = all_to_all(sent).reshape(width, rows)
        if layer == 0:
            attended, out_far[layer] = tie(attended, out_far[layer])
        out_pieces = near_finish(out_far[layer], out_own[layer])
        middle, mixed, outgoing = middle_forward(others, attended, out_pieces, state, gain_two, place[layer])
        outgoing = outgoing.reshape(experts, capacity, width)
        if layer == 0:
            outgoing, gate_far[layer] = tie(outgoing, gate_far[layer])
        else:
            outgoing, down_far[layer], *saved[0]["attended"] = tie(outgoing, down_far[layer], *saved[0]["attended"])
            kept_exchange = wt_exchange(attended.reshape(4, part, rows), wt)
        arrived = all_to_all(outgoing).reshape(slot_count, width)
        if layer == 0:
            kept_exchange = wt_exchange(attended.reshape(4, part, rows), wt)
        else:
            arrived, query_far[layer] = tie(arrived, query_far[layer])
        probs = jax.nn.softmax(times(mixed, router[:experts], 1, 1), axis=-1)
        picked = jnp.sum(named[layer] * probs[None], axis=-1, keepdims=True)
        pair_total = picked[0] + picked[1]
        gates = picked / pair_total
        kept = dict(
            state=state,
            normed_all=normed_all,
            qkv=qkv,
            exact=exact,
            log_total=log_total,
            attended=kept_exchange,
            middle=middle,
            mixed=mixed,
            gates=gates,
            arrived=arrived,
            gain_one=gain_one,
            gain_two=gain_two,
            router=router,
            out_pieces=out_pieces,
        )
        pieces = [near_finish(far[layer], own[layer]) for far, own in ((gate_far, gate_own), (up_far, up_own), (down_far, down_own))]
        kept["pieces"] = pieces
        saved.append(kept)
        if layer == last:
            break
        made, kept["gate_values"], kept["up_values"], kept["inner"] = expert_forward(arrived, *pieces)
        returned = all_to_all(made.reshape(experts, capacity, width)).reshape(slot_count, width)
        returned, gate_far[last] = tie(returned, gate_far[last])
        results = [times(place[layer, choice], returned, 1, 0) for choice in range(2)]
        kept["results"] = [result.astype(jnp.bfloat16) for result in results]
        state = middle + gates[0] * results[0] + gates[1] * results[1]

    upstream = cotangent[0].astype(jnp.float32)
    expert_done, head_done, returned, sources = None, None, None, None
    merge = lambda head, out: jnp.concatenate([head] + [out[:, i * part : (i + 1) * part] for i in range(4)], axis=0)
    smalls, gain_sums = [None] * layers, [None] * layers
    block_output = None
    for layer in reversed(range(layers)):
        k = saved[layer]
        gates, pieces = k["gates"], k["pieces"]
        if layer == last:
            arrived = k["arrived"]
            made, back, arrived_grad, inner, grad_gate, grad_up = expert_both(
                experts, mine, arrived, cot_slots, k["router"], *pieces
            )
            back = all_to_all(back.reshape(experts, capacity, width + 128))
            back = back.reshape(slot_count, width + 128)
            results = []
        else:
            arrived, inner = k["arrived"], k["inner"]
            back_rows = (gates * upstream[None]).astype(jnp.bfloat16).reshape(2 * rows, width)
            outgoing = times(place[layer].reshape(2 * rows, slot_count), back_rows, 0, 0).astype(jnp.bfloat16)
            outgoing, returned, head_sum, key_far[layer] = tie(outgoing, returned, sources[0], key_far[layer])
            sources = [lax.all_gather(merge(head_sum, sources[1]), "ctx", axis=0)]
            arrived_grad = all_to_all(outgoing.reshape(experts, capacity, width)).reshape(slot_count, width)
            state = saved[last]["middle"] + sum(
                saved[last]["gates"][i] * times(place[last, i], returned, 1, 0) for i in range(2)
            )
            block_output = state.astype(jnp.bfloat16)[None]
            back, grad_gate, grad_up = expert_backward(arrived_grad, *pieces, k["gate_values"], k["up_values"])
            back, *last_parts[2:4] = tie(back, *last_parts[2:4])
            back = all_to_all(back.reshape(experts, capacity, width)).reshape(slot_count, width)
            results = k["results"]
        pair_give, far_give, pair_own, pair_far, down_give, down_kept, down_far_part = expert_grads(
            arrived, arrived_grad, inner, grad_gate, grad_up
        )
        pair_near, far_near, down_near = swap(pair_give, 1), swap(far_give, 1), swap(down_give, 1)
        add = lambda a, b: (a.astype(jnp.float32) + b.astype(jnp.float32)).astype(jnp.bfloat16)
        pair_sums = [add(pair_far[i], far_near[i]) for i in range(2)]
        down_sum = add(down_far_part, down_near[1:])
        if layer == last:
            back, key_far[layer] = tie(back, key_far[layer])
        else:
            back, last_parts[6] = tie(back, last_parts[6])
            pair_done, down_done = last_finish(*last_parts)
            expert_done = [*pair_done, *down_done]
        pair_last = [swap(pair_sum, 2) for pair_sum in pair_sums]
        if layer == last:
            down_last = [swap(down_sum[0], 2)]
        grad_middle, middle_low, grad_attended, small = middle_back(
            experts,
            others,
            place[layer],
            back,
            upstream,
            k["middle"],
            k["mixed"],
            k["gain_two"],
            k["router"],
            chosen[layer],
            results,
            k["out_pieces"],
        )
        grad_heads = all_to_all(grad_attended.reshape(n_ctx, wide, rows))
        if layer == last:
            grad_heads, *k["attended"] = tie(grad_heads, *k["attended"])
        grad_whole, grad_sent = attend_back(owner_of, k["qkv"], k["exact"], k["log_total"], grad_heads, rep, HEAD)
        middle_pieces = wt_gather(middle_low)
        out_part = times(jnp.concatenate(k["attended"], axis=1), jnp.concatenate(middle_pieces, axis=0), 1, 0)
        out_part = out_part.astype(jnp.bfloat16)
        if layer == 0:
            out_rows = all_to_all(out_part.reshape(n_ctx, part // n_ctx, width))
            grad_sent, out_rows, *expert_done = tie(grad_sent, out_rows, *expert_done)
        else:
            grad_sent, query_far[0], out_part = tie(grad_sent, query_far[0], out_part)
            out_rows = lax.psum_scatter(out_part, "ctx", scatter_dimension=0, tiled=True)
        grad_own = all_to_all(grad_sent)
        if layer == 0:
            grad_whole, *pair_last = tie(grad_whole, *pair_last)
        head_give, head_kept, head_far = head_grads(others, k["normed_all"], grad_whole, small)
        head_near = swap(head_give, 1)
        head_last = swap(add(head_far[0], head_near[1]), 2)
        head_sum = (
            head_kept[0].astype(jnp.float32) + head_near[0].astype(jnp.float32) + head_last.astype(jnp.float32)
        ).astype(jnp.bfloat16)
        weights = [(query_weight[i], key_weight[i], value_weight[i]) for i in range(layers)]
        columns = lambda at, *rest: spread(at, layers, *rest[:2], weights[at], wide, HEAD, 16, rest[2])
        if layer == last:
            sources = [head_sum, out_rows]
            last_parts = [pair_own, pair_near, *pair_last, down_kept, down_near, *down_last]
            last_finish = lambda *p: (finish(last, layers, *p[:2], p[2:4], None), finish(last, layers, *p[4:6], p[6:], None))
            made = tie(made, grad_own)[0]
            returned = all_to_all(made.reshape(experts, capacity, width)).reshape(slot_count, width)
        else:
            *head_done, smalls[last], gain_sums[last] = columns(last, None, sources, None)
            out_rows = jnp.sum(out_rows.astype(jnp.float32), axis=0).astype(jnp.bfloat16)
            merged = merge(head_sum, out_rows)
            merged, *head_done = tie(merged, *head_done)
            down_last = [swap(tie(down_sum, head_last)[0][0], 2)]
            sources, down_last = ring_blocks(merged, ring_start(merged, ring), ring, down_last)
            pair_done = finish(layer, layers, pair_own, pair_near, pair_last, expert_done[:2])
            down_done = finish(layer, layers, down_kept, down_near, down_last, expert_done[2:])
            expert_done = [*pair_done, *down_done]
            sources[-1], *expert_done = tie(sources[-1], *expert_done)
            *head_done, smalls[layer], gain_sums[layer] = columns(layer, ring_owners, sources, head_done)
        own_query = grad_own[:, :wide].reshape(width, rows)
        own_pair = jnp.concatenate(
            [
                grad_own[:, wide : wide + HEAD].reshape(n_ctx * HEAD, rows),
                grad_own[:, wide + HEAD :].reshape(n_ctx * HEAD, rows),
            ],
            axis=0,
        )
        query_pieces = near_finish(query_far[layer], query_own[layer])
        key_pieces = near_finish(key_far[layer], pair_own_weights[layer])
        grad_normed = jnp.zeros((rows, width), jnp.float32)
        for m in range(4):
            grad_normed = lax.dynamic_update_slice_in_dim(
                grad_normed,
                times(own_query, query_pieces[m], 0, 1) + times(own_pair, key_pieces[m], 0, 1),
                (wt ^ m) * part,
                1,
            )
        pulled, _ = rms_back(k["state"], k["gain_one"], grad_normed)
        upstream = grad_middle + pulled
    gain_one_grad = jnp.stack([s[:, 0] for s in gain_sums]) / attention_gain.astype(jnp.float32)
    small_grads = jnp.stack(smalls)
    query_grad, key_grad, value_grad, out_grad = head_done
    return (
        block_output,
        upstream[None],
        gain_one_grad,
        query_grad,
        key_grad,
        value_grad,
        out_grad,
        small_grads[:, experts],
        small_grads[:, :experts].transpose(0, 2, 1),
        *expert_done,
    )


def local_rows(
    tokens,
    cotangent,
    seq_lengths,
    block_deal,
    routes,
    attention_gain,
    query_weight,
    key_weight,
    value_weight,
    out_weight,
    mixture_gain,
    router_weight,
    gate_weight,
    up_weight,
    down_weight,
):
    rows_here = tokens.shape[1]
    width = tokens.shape[2]
    layers = query_weight.shape[0]
    experts = router_weight.shape[2]
    capacity = 3 * rows_here // experts
    kv_groups = KV_HEADS
    per_group = HEADS // KV_HEADS
    head_size = HEAD
    kv_width = kv_groups * head_size
    scale = head_size ** (-0.5)
    device = lax.axis_index("ctx")
    everywhere = stream_positions(block_deal[0], BLK)
    every_seq = sequence_ids(everywhere, seq_lengths[0])
    own_pos = lax.dynamic_slice_in_dim(everywhere, device * rows_here, rows_here, 0)
    own_seq = lax.dynamic_slice_in_dim(every_seq, device * rows_here, rows_here, 0)
    choice_rows = jnp.arange(2 * rows_here, dtype=jnp.int32) // 2
    expert_ids = jnp.arange(experts, dtype=jnp.int32)

    def block_mask(start, count):
        key_pos = lax.dynamic_slice_in_dim(everywhere, start, count, 0)
        key_seq = lax.dynamic_slice_in_dim(every_seq, start, count, 0)
        return (own_seq[:, None] == key_seq[None, :]) & (key_pos[None, :] <= own_pos[:, None])

    hidden_state = tokens[0].astype(jnp.float32)
    saved = []
    for layer in range(layers):
        shared = (
            lax.all_gather(attention_gain[layer], "wt", axis=0, tiled=True),
            lax.all_gather(query_weight[layer], "wt", axis=0, tiled=True),
            lax.all_gather(key_weight[layer], "wt", axis=0, tiled=True),
            lax.all_gather(value_weight[layer], "wt", axis=0, tiled=True),
            lax.all_gather(out_weight[layer], "wt", axis=0, tiled=True),
            lax.all_gather(mixture_gain[layer], "wt", axis=0, tiled=True),
            lax.all_gather(router_weight[layer], "wt", axis=0, tiled=True),
        )
        gain_one, full_query, full_key, full_value, full_out, gain_two, full_router = shared
        normed = rms_scale(hidden_state, gain_one.astype(jnp.float32)).astype(jnp.bfloat16)
        queries = jnp.dot(normed, full_query, preferred_element_type=jnp.float32).astype(
            jnp.bfloat16
        )
        keys = jnp.dot(normed, full_key, preferred_element_type=jnp.float32).astype(jnp.bfloat16)
        values = jnp.dot(normed, full_value, preferred_element_type=jnp.float32).astype(
            jnp.bfloat16
        )
        query_heads = queries.reshape(rows_here, kv_groups, per_group, head_size)
        start_state = (
            jnp.full((kv_groups, per_group, rows_here), NEG, jnp.float32),
            jnp.zeros((kv_groups, per_group, rows_here), jnp.float32),
            jnp.zeros((kv_groups, per_group, rows_here, head_size), jnp.float32),
        )
        gathered = None
        key_piece = lax.all_gather(keys, "ctx", axis=0, tiled=True)
        value_piece = lax.all_gather(values, "ctx", axis=0, tiled=True)
        absorb_count = key_piece.shape[0]
        absorb_span = 512

        def turn(index, state):
            first = index * absorb_span
            key_block = lax.dynamic_slice_in_dim(key_piece, first, absorb_span, 0).reshape(
                absorb_span, kv_groups, head_size
            )
            value_block = lax.dynamic_slice_in_dim(value_piece, first, absorb_span, 0).reshape(
                absorb_span, kv_groups, head_size
            )
            allowed = block_mask(first, absorb_span)

            def work(state):
                top, total, summed = state
                scores = (
                    jnp.einsum(
                        "tgrd,kgd->grtk", query_heads, key_block, preferred_element_type=jnp.float32
                    )
                    * scale
                )
                scores = jnp.where(allowed[None, None], scores, NEG)
                top_new = jnp.maximum(top, jnp.max(scores, axis=-1))
                fade = jnp.exp(top - top_new)
                weights = jnp.where(allowed[None, None], jnp.exp(scores - top_new[..., None]), 0.0)
                total = total * fade + jnp.sum(weights, axis=-1)
                summed = summed * fade[..., None] + jnp.einsum(
                    "grtk,kgd->grtd",
                    weights.astype(jnp.bfloat16),
                    value_block,
                    preferred_element_type=jnp.float32,
                )
                return (top_new, total, summed)

            return lax.cond(jnp.any(allowed), work, unchanged, state)

        top, total, summed = lax.fori_loop(0, absorb_count // absorb_span, turn, start_state)
        attended = (summed / total[..., None]).transpose(2, 0, 1, 3).reshape(rows_here, width)
        log_total = top + jnp.log(total)
        attended_low = attended.astype(jnp.bfloat16)
        middle = hidden_state + jnp.dot(attended_low, full_out, preferred_element_type=jnp.float32)
        mixed_low = rms_scale(middle, gain_two.astype(jnp.float32)).astype(jnp.bfloat16)
        probs = jax.nn.softmax(
            jnp.dot(mixed_low, full_router, preferred_element_type=jnp.float32), axis=-1
        )
        chosen = routes[layer, 0]
        picked = jnp.take_along_axis(probs, chosen, axis=1)
        gates = picked / jnp.sum(picked, axis=1, keepdims=True)
        flat_choice = chosen.reshape(-1)
        onehot = (flat_choice[:, None] == expert_ids[None, :]).astype(jnp.int32)
        rank = jnp.sum((jnp.cumsum(onehot, axis=0) - onehot) * onehot, axis=1)
        slots = flat_choice * capacity + rank
        outgoing = (
            jnp.zeros((experts * capacity, width), jnp.bfloat16)
            .at[slots]
            .set(mixed_low[choice_rows])
            .reshape(experts, capacity, width)
        )
        arrived = lax.all_to_all(outgoing, "ctx", split_axis=0, concat_axis=0, tiled=True)
        expert_full = (
            lax.all_gather(gate_weight[layer, 0], "wt", axis=1, tiled=True),
            lax.all_gather(up_weight[layer, 0], "wt", axis=1, tiled=True),
            lax.all_gather(down_weight[layer, 0], "wt", axis=0, tiled=True),
        )
        gate_full, up_full, down_full = expert_full
        expert_rows = arrived.reshape(-1, width)
        gate_value = jnp.dot(expert_rows, gate_full, preferred_element_type=jnp.float32)
        up_value = jnp.dot(expert_rows, up_full, preferred_element_type=jnp.float32)
        inner = (jax.nn.silu(gate_value) * up_value).astype(jnp.bfloat16)
        produced = (
            jnp.dot(inner, down_full, preferred_element_type=jnp.float32)
            .astype(jnp.bfloat16)
            .reshape(experts, capacity, width)
        )
        returned = lax.all_to_all(produced, "ctx", split_axis=0, concat_axis=0, tiled=True)
        expert_out = (
            returned.reshape(-1, width)[slots].reshape(rows_here, 2, width).astype(jnp.float32)
        )
        saved.append(
            (
                hidden_state,
                shared,
                normed,
                query_heads,
                keys,
                values,
                gathered,
                attended,
                attended_low,
                log_total,
                middle,
                mixed_low,
                probs,
                chosen,
                picked,
                gates,
                slots,
                expert_full,
                expert_rows,
                gate_value,
                up_value,
                inner,
                expert_out,
            )
        )
        hidden_state = middle + jnp.sum(gates[:, :, None] * expert_out, axis=1)
    block_output = hidden_state.astype(jnp.bfloat16)[None]
    upstream = cotangent[0].astype(jnp.float32)
    collected = []
    for layer in reversed(range(layers)):
        (
            layer_input,
            shared,
            normed,
            query_heads,
            keys,
            values,
            gathered,
            attended,
            attended_low,
            log_total,
            middle,
            mixed_low,
            probs,
            chosen,
            picked,
            gates,
            slots,
            expert_full,
            expert_rows,
            gate_value,
            up_value,
            inner,
            expert_out,
        ) = saved[layer]
        gain_one, full_query, full_key, full_value, full_out, gain_two, full_router = shared
        gate_full, up_full, down_full = expert_full
        gate_signal = jnp.sum(upstream[:, None, :] * expert_out, axis=-1)
        back_rows = (
            (gates[:, :, None] * upstream[:, None, :]).astype(jnp.bfloat16).reshape(-1, width)
        )
        outgoing_grad = (
            jnp.zeros((experts * capacity, width), jnp.bfloat16)
            .at[slots]
            .set(back_rows)
            .reshape(experts, capacity, width)
        )
        arrived_grad = lax.all_to_all(
            outgoing_grad, "ctx", split_axis=0, concat_axis=0, tiled=True
        ).reshape(-1, width)
        grad_down = outer_rows(inner, arrived_grad)
        grad_inner = times_transposed(arrived_grad, down_full)
        sigma = jax.nn.sigmoid(gate_value)
        grad_gate_value = (
            grad_inner * up_value * sigma * (1.0 + gate_value * (1.0 - sigma))
        ).astype(jnp.bfloat16)
        grad_up_value = (grad_inner * gate_value * sigma).astype(jnp.bfloat16)
        grad_gate = outer_rows(expert_rows, grad_gate_value)
        grad_up = outer_rows(expert_rows, grad_up_value)
        grad_rows = (
            (
                times_transposed(grad_gate_value, gate_full)
                + times_transposed(grad_up_value, up_full)
            )
            .astype(jnp.bfloat16)
            .reshape(experts, capacity, width)
        )
        back_grad = lax.all_to_all(grad_rows, "ctx", split_axis=0, concat_axis=0, tiled=True)
        grad_mixed = jnp.sum(
            back_grad.reshape(-1, width)[slots].reshape(rows_here, 2, width).astype(jnp.float32),
            axis=1,
        )
        pair_total = jnp.sum(picked, axis=1, keepdims=True)
        grad_picked = (
            gate_signal - jnp.sum(gates * gate_signal, axis=1, keepdims=True)
        ) / pair_total
        grad_probs = jnp.sum(
            grad_picked[:, :, None]
            * (chosen[:, :, None] == expert_ids[None, None, :]).astype(jnp.float32),
            axis=1,
        )
        grad_logits = probs * (grad_probs - jnp.sum(probs * grad_probs, axis=1, keepdims=True))
        grad_router = lax.dot_general(
            mixed_low.astype(jnp.float32),
            grad_logits,
            (((0,), (0,)), ((), ())),
            precision=lax.Precision.HIGHEST,
            preferred_element_type=jnp.float32,
        )
        grad_mixed = grad_mixed + lax.dot_general(
            grad_logits,
            full_router.astype(jnp.float32),
            (((1,), (1,)), ((), ())),
            precision=lax.Precision.HIGHEST,
            preferred_element_type=jnp.float32,
        )
        norm_value, pull_two = jax.vjp(rms_scale, middle, gain_two.astype(jnp.float32))
        grad_middle_norm, grad_gain_two = pull_two(grad_mixed)
        grad_middle = upstream + grad_middle_norm
        middle_low = grad_middle.astype(jnp.bfloat16)
        grad_out = outer_rows(attended_low, middle_low)
        grad_attended = times_transposed(middle_low, full_out).astype(jnp.bfloat16)
        grad_heads = grad_attended.reshape(rows_here, kv_groups, per_group, head_size)
        attended_heads = attended.reshape(rows_here, kv_groups, per_group, head_size)
        delta = jnp.sum(grad_heads.astype(jnp.float32) * attended_heads, axis=-1).transpose(1, 2, 0)
        whole = (
            lax.all_gather(keys, "ctx", axis=0, tiled=True),
            lax.all_gather(values, "ctx", axis=0, tiled=True),
        )
        key_all, value_all = whole
        total_rows = key_all.shape[0]
        span = 512

        def score_block(first, count, allowed):
            key_block = lax.dynamic_slice_in_dim(key_all, first, count, 0).reshape(
                count, kv_groups, head_size
            )
            value_block = lax.dynamic_slice_in_dim(value_all, first, count, 0).reshape(
                count, kv_groups, head_size
            )
            scores = (
                jnp.einsum(
                    "tgrd,kgd->grtk", query_heads, key_block, preferred_element_type=jnp.float32
                )
                * scale
            )
            probs_block = jnp.where(
                allowed[None, None], jnp.exp(scores - log_total[..., None]), 0.0
            )
            grad_probs_block = jnp.einsum(
                "tgrd,kgd->grtk", grad_heads, value_block, preferred_element_type=jnp.float32
            )
            grad_scores = (probs_block * (grad_probs_block - delta[..., None])).astype(jnp.bfloat16)
            return (key_block, probs_block, grad_scores)

        def key_terms(probs_block, grad_scores, count):
            key_part = (
                jnp.einsum(
                    "grtk,tgrd->kgd", grad_scores, query_heads, preferred_element_type=jnp.float32
                )
                * scale
            ).reshape(count, kv_width)
            value_part = jnp.einsum(
                "grtk,tgrd->kgd",
                probs_block.astype(jnp.bfloat16),
                grad_heads,
                preferred_element_type=jnp.float32,
            ).reshape(count, kv_width)
            return (key_part, value_part)

        query_start = jnp.zeros((rows_here, kv_groups, per_group, head_size), jnp.float32)

        def turn_back(index, state):
            first = index * span
            allowed = block_mask(first, span)

            def work(state):
                grad_query, grad_keys, grad_values = state
                key_block, probs_block, grad_scores = score_block(first, span, allowed)
                grad_query = (
                    grad_query
                    + jnp.einsum(
                        "grtk,kgd->tgrd", grad_scores, key_block, preferred_element_type=jnp.float32
                    )
                    * scale
                )
                key_part, value_part = key_terms(probs_block, grad_scores, span)
                grad_keys = lax.dynamic_update_slice_in_dim(grad_keys, key_part, first, 0)
                grad_values = lax.dynamic_update_slice_in_dim(grad_values, value_part, first, 0)
                return (grad_query, grad_keys, grad_values)

            return lax.cond(jnp.any(allowed), work, unchanged, state)

        back_start = (
            query_start,
            jnp.zeros((total_rows, kv_width), jnp.float32),
            jnp.zeros((total_rows, kv_width), jnp.float32),
        )
        grad_query, grad_keys, grad_values = lax.fori_loop(
            0, total_rows // span, turn_back, back_start
        )
        grad_keys, grad_values = (
            lax.psum_scatter(
                grad_keys.astype(jnp.bfloat16), "ctx", scatter_dimension=0, tiled=True
            ).astype(jnp.float32),
            lax.psum_scatter(
                grad_values.astype(jnp.bfloat16), "ctx", scatter_dimension=0, tiled=True
            ).astype(jnp.float32),
        )
        query_low = grad_query.reshape(rows_here, width).astype(jnp.bfloat16)
        key_low = grad_keys.astype(jnp.bfloat16)
        value_low = grad_values.astype(jnp.bfloat16)
        grad_query_weight = outer_rows(normed, query_low)
        grad_key_weight = outer_rows(normed, key_low)
        grad_value_weight = outer_rows(normed, value_low)
        grad_normed = (
            times_transposed(query_low, full_query)
            + times_transposed(key_low, full_key)
            + times_transposed(value_low, full_value)
        )
        norm_value, pull_one = jax.vjp(rms_scale, layer_input, gain_one.astype(jnp.float32))
        grad_input_norm, grad_gain_one = pull_one(grad_normed)
        upstream = grad_middle + grad_input_norm
        part_one, part_query, part_key, part_value, part_out, part_two, part_router = (
            lax.psum_scatter(
                grad_gain_one.astype(jnp.bfloat16), "wt", scatter_dimension=0, tiled=True
            ).astype(jnp.float32),
            lax.psum_scatter(
                grad_query_weight.astype(jnp.bfloat16), "wt", scatter_dimension=0, tiled=True
            ).astype(jnp.float32),
            lax.psum_scatter(
                grad_key_weight.astype(jnp.bfloat16), "wt", scatter_dimension=0, tiled=True
            ).astype(jnp.float32),
            lax.psum_scatter(
                grad_value_weight.astype(jnp.bfloat16), "wt", scatter_dimension=0, tiled=True
            ).astype(jnp.float32),
            lax.psum_scatter(
                grad_out.astype(jnp.bfloat16), "wt", scatter_dimension=0, tiled=True
            ).astype(jnp.float32),
            lax.psum_scatter(
                grad_gain_two.astype(jnp.bfloat16), "wt", scatter_dimension=0, tiled=True
            ).astype(jnp.float32),
            lax.psum_scatter(
                grad_router.astype(jnp.bfloat16), "wt", scatter_dimension=0, tiled=True
            ).astype(jnp.float32),
        )
        summed_parts = (
            lax.psum(part_one.astype(jnp.bfloat16), "ctx").astype(jnp.float32),
            lax.psum(part_query.astype(jnp.bfloat16), "ctx").astype(jnp.float32),
            lax.psum(part_key.astype(jnp.bfloat16), "ctx").astype(jnp.float32),
            lax.psum(part_value.astype(jnp.bfloat16), "ctx").astype(jnp.float32),
            lax.psum(part_out.astype(jnp.bfloat16), "ctx").astype(jnp.float32),
            lax.psum(part_two.astype(jnp.bfloat16), "ctx").astype(jnp.float32),
            lax.psum(part_router.astype(jnp.bfloat16), "ctx").astype(jnp.float32),
        )
        expert_parts = (
            lax.psum_scatter(
                grad_gate.astype(jnp.bfloat16), "wt", scatter_dimension=1, tiled=True
            ).astype(jnp.float32),
            lax.psum_scatter(
                grad_up.astype(jnp.bfloat16), "wt", scatter_dimension=1, tiled=True
            ).astype(jnp.float32),
            lax.psum_scatter(
                grad_down.astype(jnp.bfloat16), "wt", scatter_dimension=0, tiled=True
            ).astype(jnp.float32),
        )
        collected.append((summed_parts, expert_parts))
    ordered = collected[::-1]
    attention_gain_grad = jnp.stack([item[0][0] for item in ordered])
    query_grad = jnp.stack([item[0][1] for item in ordered])
    key_grad = jnp.stack([item[0][2] for item in ordered])
    value_grad = jnp.stack([item[0][3] for item in ordered])
    out_grad = jnp.stack([item[0][4] for item in ordered])
    mixture_gain_grad = jnp.stack([item[0][5] for item in ordered])
    router_grad = jnp.stack([item[0][6] for item in ordered])
    gate_grad = jnp.stack([item[1][0] for item in ordered])[:, None]
    up_grad = jnp.stack([item[1][1] for item in ordered])[:, None]
    down_grad = jnp.stack([item[1][2] for item in ordered])[:, None]
    return (
        block_output,
        upstream[None],
        attention_gain_grad,
        query_grad,
        key_grad,
        value_grad,
        out_grad,
        mixture_gain_grad,
        router_grad,
        gate_grad,
        up_grad,
        down_grad,
    )


def solution(mesh):
    placed = (
        P("wt", "ctx", None),
        P("wt", "ctx", None),
        P("wt", None),
        P("wt", None, None),
        P(None, "wt", "ctx", None),
        P(None, "wt"),
        P(None, "wt", None),
        P(None, "wt", None),
        P(None, "wt", None),
        P(None, "wt", None),
        P(None, "wt"),
        P(None, "wt", None),
        P(None, "ctx", None, "wt"),
        P(None, "ctx", None, "wt"),
        P(None, "ctx", "wt", None),
    )
    def local(*arrays):
        if by_heads(mesh, *arrays):
            return local_heads(mesh, *arrays)
        return local_rows(*arrays)

    return jax.shard_map(
        local,
        mesh=mesh,
        in_specs=placed,
        out_specs=(
            P("wt", "ctx", None),
            P("wt", "ctx", None),
            P(None, "wt"),
            P(None, "wt", None),
            P(None, "wt", None),
            P(None, "wt", None),
            P(None, "wt", None),
            P(None, "wt"),
            P(None, "wt", None),
            P(None, "ctx", None, "wt"),
            P(None, "ctx", None, "wt"),
            P(None, "ctx", "wt", None),
        ),
        check_vma=False,
    )
```

```python
import functools

import jax
import jax.numpy as jnp
from jax import lax
from jax.experimental import pallas as pl
from jax.experimental.pallas import tpu as pltpu
from jax.sharding import PartitionSpec as P

HEADS = 24
KV_HEADS = 8
HEAD = 64
BLK = 128


EPS = 1e-05
NEG = -1e30


def rms_scale(rows, gain):
    return rows * lax.rsqrt(jnp.mean(rows * rows, axis=-1, keepdims=True) + EPS) * gain


def stream_positions(table, width):
    offsets = jnp.arange(width, dtype=jnp.int32)
    return (table[:, :, None] * width + offsets[None, None, :]).reshape(-1)


def sequence_ids(positions, seq_row):
    ends = jnp.cumsum(seq_row)
    return jnp.sum((positions[:, None] >= ends[None, :]).astype(jnp.int32), axis=1)


def outer_rows(left, right):
    return lax.dot_general(
        left, right, (((0,), (0,)), ((), ())), preferred_element_type=jnp.float32
    )


def times_transposed(left, right):
    return lax.dot_general(
        left, right, (((1,), (1,)), ((), ())), preferred_element_type=jnp.float32
    )


def unchanged(state):
    return state


def times(left, right, a, b):
    return lax.dot_general(left, right, (((a,), (b,)), ((), ())), preferred_element_type=jnp.float32)


def vmem(count):
    return [pl.BlockSpec(memory_space=pltpu.VMEM)] * count


def kernel_params():
    return pltpu.CompilerParams(vmem_limit_bytes=56 * 2**20)


def cost(flops, nbytes, transcendentals=0):
    return pl.CostEstimate(flops=int(flops), bytes_accessed=int(nbytes), transcendentals=int(transcendentals))


def causal_mask(span):
    key_at = lax.broadcasted_iota(jnp.int32, (span, span), 0)
    query_at = lax.broadcasted_iota(jnp.int32, (span, span), 1)
    return key_at <= query_at


def front_kernel(raw, rep, head, span, base, spot_ref, owner_ref, at_ref, *refs):
    *blocks, gain_ref, w0, w1, w2, w3, normed_ref, qkv_ref, sent_ref, exact_ref, log_ref = refs
    rows = blocks[0].shape[0]
    count = len(blocks) - 1
    tokens = count * rows
    width = rep * head
    scale = head ** (-0.5)
    gain = gain_ref[...]
    for k in range(count):
        low, high = (blocks[k],) * 2 if k < count - 1 else blocks[k:]
        half = low.shape[0] if k == count - 1 else rows
        for start, ref in ((0, low), (half, high)) if k == count - 1 else ((0, low),):
            block = ref[...]
            if raw:
                block = rms_scale(block.astype(jnp.float32), gain).astype(jnp.bfloat16)
            normed_ref[spot_ref[k], start : start + ref.shape[0], :] = block
    lanes_all = qkv_ref.shape[0]
    slice_width = w0.shape[1]
    for part in range(tokens // span):
        take = span // rows
        total = 0.0
        for m, weight_ref in enumerate((w0, w1, w2, w3)):
            lanes = pl.ds(pl.multiple_of(at_ref[m] * slice_width, 128), slice_width)
            piece = normed_ref[part * take : (part + 1) * take, :, lanes].reshape(span, slice_width)
            total = total + times(weight_ref[base : base + lanes_all, :], piece, 1, 1)
        qkv_ref[:, part * span : (part + 1) * span] = total.astype(jnp.bfloat16)
    mask = causal_mask(span)
    per = span // rows
    for part in range(tokens // span):
        lanes = pl.ds(part * span, span)
        seen = (part + 1) * span
        keys = qkv_ref[width : width + head, :seen]
        values = qkv_ref[width + head : lanes_all, :seen]
        for h in range(rep):
            at = slice(h * head, (h + 1) * head)
            scores = times(keys, qkv_ref[at, lanes], 0, 0) * scale
            last = jnp.where(mask, scores[seen - span :], NEG)
            top = jnp.max(last, axis=0, keepdims=True)
            if part:
                top = jnp.maximum(top, jnp.max(scores[: seen - span], axis=0, keepdims=True))
            weights = jnp.exp(last - top)
            if part:
                weights = jnp.concatenate([jnp.exp(scores[: seen - span] - top), weights], axis=0)
            total = jnp.sum(weights, axis=0, keepdims=True)
            result = times(values, weights.astype(jnp.bfloat16), 1, 0) / total
            exact_ref[at, lanes] = result
            log_ref[h : h + 1, lanes] = top + jnp.log(total)
            for b in range(per):
                sent_ref[owner_ref[part * per + b], at, :] = result[:, b * rows : (b + 1) * rows].astype(jnp.bfloat16)


def front(raw, spots, owner_of, at, blocks, gain, pieces, base, rep, head):
    rows, width = blocks[0].shape
    count = len(blocks) - 1
    tokens = count * rows
    span = min(256, tokens)
    deep = (rep + 2) * head
    pairs = rep * tokens * (tokens + span) // 2
    return pl.pallas_call(
        functools.partial(front_kernel, raw, rep, head, span, base),
        out_shape=(
            jax.ShapeDtypeStruct((count, rows, width), jnp.bfloat16),
            jax.ShapeDtypeStruct((deep, tokens), jnp.bfloat16),
            jax.ShapeDtypeStruct((count, rep * head, rows), jnp.bfloat16),
            jax.ShapeDtypeStruct((rep * head, tokens), jnp.float32),
            jax.ShapeDtypeStruct((rep, tokens), jnp.float32),
        ),
        in_specs=[pl.BlockSpec(memory_space=pltpu.SMEM)] * 3 + vmem(len(blocks) + 5),
        out_specs=tuple(vmem(5)),
        compiler_params=kernel_params(),
        cost_estimate=cost(4 * head * pairs + 2 * deep * width * tokens, 9 * 2**20, pairs),
        name="front",
    )(spots, owner_of, at, *blocks, gain, *pieces)


def attend_back_kernel(rep, head, span, owner_ref, qkv_ref, exact_ref, log_ref, grad_ref, whole_ref, sent_ref, grad_all, keys_sum, values_sum):
    tokens = qkv_ref.shape[1]
    rows = grad_ref.shape[2]
    width = rep * head
    per = span // rows
    scale = head ** (-0.5)
    mask = causal_mask(span)
    for block in range(tokens // rows):
        grad_all[:, block * rows : (block + 1) * rows] = grad_ref[owner_ref[block]]
    keys_sum[...] = jnp.zeros_like(keys_sum)
    values_sum[...] = jnp.zeros_like(values_sum)
    for part in range(tokens // span):
        lanes = pl.ds(part * span, span)
        seen = (part + 1) * span
        keys = qkv_ref[width : width + head, :seen]
        values = qkv_ref[width + head :, :seen]
        for h in range(rep):
            at = slice(h * head, (h + 1) * head)
            queries = qkv_ref[at, lanes]
            grads = grad_all[at, lanes]
            delta = jnp.sum(grads.astype(jnp.float32) * exact_ref[at, lanes], axis=0, keepdims=True)
            scores = times(keys, queries, 0, 0) * scale
            probs = jnp.exp(scores - log_ref[h : h + 1, lanes])
            last = jnp.where(mask, probs[seen - span :], 0.0)
            probs = last if part == 0 else jnp.concatenate([probs[: seen - span], last], axis=0)
            pulled = times(values, grads, 0, 0)
            slopes = (probs * (pulled - delta)).astype(jnp.bfloat16)
            back = (times(keys, slopes, 1, 0) * scale).astype(jnp.bfloat16)
            whole_ref[at, lanes] = back
            for b in range(per):
                sent_ref[owner_ref[part * per + b], at, :] = back[:, b * rows : (b + 1) * rows]
            keys_sum[:, :seen] += times(queries, slopes, 1, 1)
            values_sum[:, :seen] += times(grads, probs.astype(jnp.bfloat16), 1, 1)
    keys_low = (keys_sum[...] * scale).astype(jnp.bfloat16)
    values_low = values_sum[...].astype(jnp.bfloat16)
    whole_ref[width : width + head, :] = keys_low
    whole_ref[width + head :, :] = values_low
    for block in range(tokens // rows):
        cut = slice(block * rows, (block + 1) * rows)
        sent_ref[owner_ref[block], width : width + head, :] = keys_low[:, cut]
        sent_ref[owner_ref[block], width + head :, :] = values_low[:, cut]


def attend_back(owner_of, qkv, exact, log_total, grads, rep, head):
    deep, tokens = qkv.shape
    count, _, rows = grads.shape
    span = min(256, tokens)
    pairs = rep * tokens * (tokens + span) // 2
    return pl.pallas_call(
        functools.partial(attend_back_kernel, rep, head, span),
        out_shape=(
            jax.ShapeDtypeStruct((deep, tokens), jnp.bfloat16),
            jax.ShapeDtypeStruct((count, deep, rows), jnp.bfloat16),
        ),
        in_specs=[pl.BlockSpec(memory_space=pltpu.SMEM)] + vmem(4),
        out_specs=tuple(vmem(2)),
        scratch_shapes=[
            pltpu.VMEM((rep * head, tokens), jnp.bfloat16),
            pltpu.VMEM((head, tokens), jnp.float32),
            pltpu.VMEM((head, tokens), jnp.float32),
        ],
        compiler_params=kernel_params(),
        cost_estimate=cost(10 * head * pairs, 6 * 2**20, pairs),
        name="attend_back",
    )(owner_of, qkv, exact, log_total, grads)


def silu_pair(gate_value, up_value):
    return (gate_value * jax.nn.sigmoid(gate_value) * up_value).astype(jnp.bfloat16)


def pair_back(grad_inner, gate_value, up_value):
    sigma = jax.nn.sigmoid(gate_value)
    grad_gate = grad_inner * up_value * sigma * (1.0 + gate_value * (1.0 - sigma))
    return grad_gate.astype(jnp.bfloat16), (grad_inner * gate_value * sigma).astype(jnp.bfloat16)


def by_piece(gate, up, down):
    return [piece for pieces in zip(gate, up, down) for piece in pieces]


def expert_forward_kernel(rows_ref, *refs):
    weights, (made_ref, gates_ref, ups_ref, inner_ref, total) = refs[:12], refs[12:]
    rows = rows_ref[...]
    for m in range(4):
        gate_value = times(rows, weights[3 * m][...], 1, 0)
        up_value = times(rows, weights[3 * m + 1][...], 1, 0)
        gates_ref[m] = gate_value
        ups_ref[m] = up_value
        inner = silu_pair(gate_value, up_value)
        inner_ref[m] = inner
        part = times(inner, weights[3 * m + 2][...], 1, 0)
        if m == 0:
            total[...] = part
        elif m < 3:
            total[...] += part
        else:
            made_ref[...] = (total[...] + part).astype(jnp.bfloat16)


def expert_forward(rows, gate, up, down):
    count, width = rows.shape
    hidden = gate[0].shape[1]
    weights = by_piece(gate, up, down)
    return pl.pallas_call(
        expert_forward_kernel,
        out_shape=(
            jax.ShapeDtypeStruct((count, width), jnp.bfloat16),
            jax.ShapeDtypeStruct((4, count, hidden), jnp.float32),
            jax.ShapeDtypeStruct((4, count, hidden), jnp.float32),
            jax.ShapeDtypeStruct((4, count, hidden), jnp.bfloat16),
        ),
        in_specs=vmem(1) + vmem(12),
        out_specs=tuple(vmem(4)),
        scratch_shapes=[pltpu.VMEM((count, width), jnp.float32)],
        compiler_params=kernel_params(),
        cost_estimate=cost(24 * count * width * hidden, 16 * 2**20, 4 * count * hidden),
        name="expert_forward",
    )(rows, *weights)


def expert_backward_kernel(grad_ref, *refs):
    weights, (gates, ups, back_ref, grad_gate_ref, grad_up_ref, total) = refs[2:14], refs[:2] + refs[14:]
    grads = grad_ref[...]
    for m in range(4):
        grad_inner = times(grads, weights[3 * m + 2][...], 1, 1)
        grad_gate, grad_up = pair_back(grad_inner, gates[m], ups[m])
        grad_gate_ref[m] = grad_gate
        grad_up_ref[m] = grad_up
        part = times(grad_gate, weights[3 * m][...], 1, 1) + times(grad_up, weights[3 * m + 1][...], 1, 1)
        if m == 0:
            total[...] = part
        elif m < 3:
            total[...] += part
        else:
            back_ref[...] = (total[...] + part).astype(jnp.bfloat16)


def expert_backward(grads, gate, up, down, gates, ups):
    count, width = grads.shape
    hidden = gate[0].shape[1]
    weights = [gates, ups] + by_piece(gate, up, down)
    return pl.pallas_call(
        expert_backward_kernel,
        out_shape=(
            jax.ShapeDtypeStruct((count, width), jnp.bfloat16),
            jax.ShapeDtypeStruct((4, count, hidden), jnp.bfloat16),
            jax.ShapeDtypeStruct((4, count, hidden), jnp.bfloat16),
        ),
        in_specs=vmem(1) + vmem(14),
        out_specs=tuple(vmem(3)),
        scratch_shapes=[pltpu.VMEM((count, width), jnp.float32)],
        compiler_params=kernel_params(),
        cost_estimate=cost(24 * count * width * hidden, 16 * 2**20, 4 * count * hidden),
        name="expert_backward",
    )(grads, *weights)


def expert_both_kernel(experts, mine_ref, rows_ref, cot_ref, router_ref, *refs):
    weights, outs = refs[:12], refs[12:]
    made_ref, back_ref, grad_ref, inner_ref, grad_gate_ref, grad_up_ref, total, total_back = outs
    rows = rows_ref[...]
    count, width = rows.shape
    cot = cot_ref[:, :width].astype(jnp.float32)
    logits = times(rows, router_ref[...], 1, 1)
    ids = lax.broadcasted_iota(jnp.int32, logits.shape, 1)
    logits = jnp.where(ids < experts, logits, NEG)
    odds = jnp.exp(logits - jnp.max(logits, axis=1, keepdims=True))
    other = cot_ref[:, width : width + 1].astype(jnp.float32).astype(jnp.int32)
    own_odds = jnp.sum(jnp.where(ids == mine_ref[0], odds, 0.0), axis=1, keepdims=True)
    other_odds = jnp.sum(jnp.where(ids == other, odds, 0.0), axis=1, keepdims=True)
    grad_ref[...] = (own_odds / (own_odds + other_odds) * cot).astype(jnp.bfloat16)
    grads = grad_ref[...]
    for m in range(4):
        gate, up = weights[3 * m], weights[3 * m + 1]
        gate_value = times(rows, gate[...], 1, 0)
        up_value = times(rows, up[...], 1, 0)
        inner = silu_pair(gate_value, up_value)
        inner_ref[m] = inner
        down = weights[3 * m + 2]
        grad_gate, grad_up = pair_back(times(grads, down[...], 1, 1), gate_value, up_value)
        grad_gate_ref[m] = grad_gate
        grad_up_ref[m] = grad_up
        part = times(inner, down[...], 1, 0)
        part_back = times(grad_gate, gate[...], 1, 1) + times(grad_up, up[...], 1, 1)
        total[...] = part if m == 0 else total[...] + part
        total_back[...] = part_back if m == 0 else total_back[...] + part_back
    made = total[...].astype(jnp.bfloat16)
    made_ref[...] = made
    back_ref[:, :width] = total_back[...].astype(jnp.bfloat16)
    signal = jnp.sum(cot * made.astype(jnp.float32), axis=1, keepdims=True)
    high = signal.astype(jnp.bfloat16)
    low = (signal - high.astype(jnp.float32)).astype(jnp.bfloat16)
    at = lax.broadcasted_iota(jnp.int32, (count, back_ref.shape[1] - width), 1)
    back_ref[:, width:] = jnp.where(
        at == 0, high.astype(jnp.float32), jnp.where(at == 1, low.astype(jnp.float32), 0.0)
    ).astype(jnp.bfloat16)


def expert_both(experts, mine, rows, cot, router, gate, up, down):
    count, width = rows.shape
    hidden = gate[0].shape[1]
    weights = by_piece(gate, up, down)
    return pl.pallas_call(
        functools.partial(expert_both_kernel, experts),
        out_shape=(
            jax.ShapeDtypeStruct((count, width), jnp.bfloat16),
            jax.ShapeDtypeStruct(cot.shape, jnp.bfloat16),
            jax.ShapeDtypeStruct((count, width), jnp.bfloat16),
            jax.ShapeDtypeStruct((4, count, hidden), jnp.bfloat16),
            jax.ShapeDtypeStruct((4, count, hidden), jnp.bfloat16),
            jax.ShapeDtypeStruct((4, count, hidden), jnp.bfloat16),
        ),
        in_specs=[pl.BlockSpec(memory_space=pltpu.SMEM)] + vmem(3) + vmem(12),
        out_specs=tuple(vmem(6)),
        scratch_shapes=[pltpu.VMEM((count, width), jnp.float32)] * 2,
        compiler_params=kernel_params(),
        cost_estimate=cost(48 * count * width * hidden, 18 * 2**20, 8 * count * hidden),
        name="expert_both",
    )(mine, rows, cot, router, *weights)


def expert_grads_kernel(rows_ref, grad_ref, inner_ref, grad_gate_ref, grad_up_ref, pair_give, far_give, pair_own, pair_far, down_give, down_own, down_far):
    for m, (pairs, at, downs, down_at) in enumerate(
        (
            (pair_own, 0, down_own, 0),
            (pair_give, 0, down_give, 0),
            (pair_far, 0, down_far, 0),
            (far_give, 0, down_give, 1),
        )
    ):
        pairs[at] = times(rows_ref[...], grad_gate_ref[m], 0, 0).astype(jnp.bfloat16)
        pairs[at + 1] = times(rows_ref[...], grad_up_ref[m], 0, 0).astype(jnp.bfloat16)
        downs[down_at] = times(inner_ref[m], grad_ref[...], 0, 0).astype(jnp.bfloat16)


def expert_grads(rows, grads, inner, grad_gate, grad_up):
    count, width = rows.shape
    hidden = inner.shape[2]
    shapes = [(2, width, hidden)] * 4
    shapes += [(2, hidden, width), (1, hidden, width), (1, hidden, width)]
    return pl.pallas_call(
        expert_grads_kernel,
        out_shape=tuple(jax.ShapeDtypeStruct(shape, jnp.bfloat16) for shape in shapes),
        in_specs=vmem(5),
        out_specs=tuple(vmem(7)),
        compiler_params=kernel_params(),
        cost_estimate=cost(24 * count * width * hidden, 14 * 2**20),
        name="expert_grads",
    )(rows, grads, inner, grad_gate, grad_up)


def head_grads_kernel(part, at_ref, normed_ref, whole_ref, small_ref, give_ref, own_ref, far_ref):
    tokens = whole_ref.shape[1]
    deep = whole_ref.shape[0]
    for m, (ref, slot) in enumerate(((own_ref, 0), (give_ref, 0), (far_ref, 0), (give_ref, 1))):
        lanes = pl.ds(pl.multiple_of(at_ref[m] * part, 128), part)
        rows = normed_ref[:, :, lanes].reshape(tokens, part)
        ref[slot, :deep, :] = times(whole_ref[...], rows, 1, 0).astype(jnp.bfloat16)
        ref[slot, deep:, :] = small_ref[:, lanes].astype(jnp.bfloat16)


def head_grads(at, normed, whole, small):
    deep, tokens = whole.shape
    width = normed.shape[2]
    part = width // 4
    full = deep + small.shape[0]
    return pl.pallas_call(
        functools.partial(head_grads_kernel, part),
        out_shape=tuple(jax.ShapeDtypeStruct((n, full, part), jnp.bfloat16) for n in (2, 1, 1)),
        in_specs=[pl.BlockSpec(memory_space=pltpu.SMEM)] + vmem(3),
        out_specs=tuple(vmem(3)),
        compiler_params=kernel_params(),
        cost_estimate=cost(2**20, 2**16),
        name="head_grads",
    )(at, normed, whole, small)


def spread_kernel(wide, head, ringed, *refs):
    if ringed:
        spot_ref, *blocks, query_ref, key_ref, value_ref = refs[: ringed + 4]
        gathered_ref = refs[-1]
        outs = refs[-7:-1]
        for k, block in enumerate(blocks[:-2]):
            gathered_ref[spot_ref[k]] = block[...]
        half = blocks[-2].shape[0]
        gathered_ref[spot_ref[ringed - 2], :half, :] = blocks[-2][...]
        gathered_ref[spot_ref[ringed - 2], half:, :] = blocks[-1][...]
    else:
        gathered_ref, query_ref, key_ref, value_ref = refs[:4]
        outs = refs[-6:]
    query_out, key_out, value_out, out_out, small_out, sum_ref = outs
    count, _, part = gathered_ref.shape
    deep = wide + 2 * head
    small = small_out.shape[0]
    sums = jnp.zeros((part, 1), jnp.float32)
    for i in range(count // 2):
        block = gathered_ref[2 * i : 2 * i + 2, :wide, :].astype(jnp.float32).reshape(2 * wide, part).T
        lanes = slice(2 * i * wide, 2 * (i + 1) * wide)
        query_out[0, :, lanes] = block
        sums += jnp.sum(block * query_ref[:, lanes].astype(jnp.float32), axis=1, keepdims=True)
    for start, weight_ref, out in ((wide, key_ref, key_out), (wide + head, value_ref, value_out)):
        block = gathered_ref[:, start : start + head, :].astype(jnp.float32).reshape(count * head, part).T
        out[0] = block
        sums += jnp.sum(block * weight_ref[...].astype(jnp.float32), axis=1, keepdims=True)
    sum_ref[...] = sums
    total = gathered_ref[0, deep : deep + small, :].astype(jnp.float32)
    for c in range(1, count):
        total += gathered_ref[c, deep : deep + small, :].astype(jnp.float32)
    small_out[...] = total
    rows = part // count
    for c in range(count):
        for j in range(out_out.shape[2] // part):
            piece = gathered_ref[c, deep + small + j * rows : deep + small + (j + 1) * rows, :]
            out_out[0, c * rows : (c + 1) * rows, j * part : (j + 1) * part] = piece.astype(jnp.float32)


def spread(layer, layers, spots, sources, weights, wide, head, small, before):
    ringed = len(sources) if spots is not None else 0
    part = weights[0].shape[0]
    width = weights[0].shape[1]
    count = width // wide
    shapes = [(layers,) + weight.shape for weight in weights] + [(layers, part, width)]
    aliased = [] if before is None else list(before)
    one = lambda shape: pl.BlockSpec((1,) + shape[1:], lambda i: (layer, 0, 0))
    whole = lambda shape: pl.BlockSpec(shape, lambda i: (0,) * len(shape))
    deep = sources[0].shape[-2]
    lead = [spots] if ringed else []
    return pl.pallas_call(
        functools.partial(spread_kernel, wide, head, ringed),
        grid=(1,),
        out_shape=tuple(jax.ShapeDtypeStruct(shape, jnp.float32) for shape in shapes)
        + (jax.ShapeDtypeStruct((small, part), jnp.float32), jax.ShapeDtypeStruct((part, 1), jnp.float32)),
        in_specs=[pl.BlockSpec(memory_space=pltpu.SMEM)] * len(lead)
        + [whole(source.shape) for source in sources]
        + [whole(weight.shape) for weight in weights]
        + [pl.BlockSpec(memory_space=pl.ANY)] * len(aliased),
        out_specs=tuple(one(shape) for shape in shapes) + (whole((small, part)), whole((part, 1))),
        scratch_shapes=[pltpu.VMEM((count, deep, part), jnp.bfloat16)] if ringed else [],
        input_output_aliases={len(lead) + len(sources) + 3 + i: i for i in range(len(aliased))},
        compiler_params=kernel_params(),
        cost_estimate=cost(2**20, 2**16),
        name="spread",
    )(*lead, *sources, *weights, *aliased)


def finish_kernel(*refs):
    own_ref, near_ref = refs[:2]
    count = own_ref.shape[0]
    for i, (far_ref, out) in enumerate(zip(refs[2 : 2 + count], refs[-count:])):
        total = own_ref[i].astype(jnp.float32) + near_ref[i].astype(jnp.float32) + far_ref[...].astype(jnp.float32)
        out[0, 0] = total


def finish(layer, layers, own, near, far, before):
    count, rows, columns = own.shape
    steps = 2
    block = rows // steps
    aliased = [] if before is None else list(before)
    taken = pl.BlockSpec((count, block, columns), lambda i: (0, i, 0))
    made = pl.BlockSpec((1, 1, block, columns), lambda i: (layer, 0, i, 0))
    return pl.pallas_call(
        finish_kernel,
        grid=(steps,),
        out_shape=tuple(jax.ShapeDtypeStruct((layers, 1, rows, columns), jnp.float32) for _ in range(count)),
        in_specs=[taken] * 2
        + [pl.BlockSpec((block, columns), lambda i: (i, 0))] * count
        + [pl.BlockSpec(memory_space=pl.ANY)] * len(aliased),
        out_specs=(made,) * count,
        input_output_aliases={2 + count + i: i for i in range(len(aliased))},
        compiler_params=kernel_params(),
        cost_estimate=cost(2**20, 2**16),
        name="finish",
    )(own, near, *far, *aliased)


def head_rows_kernel(wide, head, at_ref, query_ref, key_ref, value_ref, small_ref, out_ref):
    odd = at_ref[0] % 2
    top = 0
    for ref, size in ((query_ref, wide), (key_ref, head), (value_ref, head)):
        turned = ref[0].astype(jnp.float32).T
        out_ref[0, top : top + size, :] = jnp.where(odd == 1, turned[size:], turned[:size]).astype(jnp.bfloat16)
        top += size
    out_ref[0, top:, :] = small_ref[0]


def head_rows(mine, query_weight, key_weight, value_weight, small, wide, head):
    layers, part, _ = query_weight.shape
    rows = wide + 2 * head + small.shape[1]
    taken = lambda size: pl.BlockSpec((1, part, 2 * size), lambda i, at: (i, 0, at[0] // 2))
    return pl.pallas_call(
        functools.partial(head_rows_kernel, wide, head),
        grid_spec=pltpu.PrefetchScalarGridSpec(
            num_scalar_prefetch=1,
            grid=(layers,),
            in_specs=[taken(wide), taken(head), taken(head), pl.BlockSpec((1,) + small.shape[1:], lambda i, at: (i, 0, 0))],
            out_specs=pl.BlockSpec((1, rows, part), lambda i, at: (i, 0, 0)),
        ),
        out_shape=jax.ShapeDtypeStruct((layers, rows, part), jnp.bfloat16),
        compiler_params=kernel_params(),
        cost_estimate=cost(2**20, 2**16),
        name="head_rows",
    )(mine, query_weight, key_weight, value_weight, small)


def middle_forward_kernel(at_ref, attended_ref, state_ref, gain_ref, place_ref, *refs):
    weights, (middle_ref, mixed_ref, out_ref) = refs[:4], refs[4:]
    part = weights[0].shape[0]
    total = state_ref[...]
    for m in range(4):
        rows = attended_ref[pl.ds(pl.multiple_of(at_ref[m] * part, 128), part), :]
        total = total + times(rows, weights[m][...], 0, 0)
    middle_ref[...] = total
    mixed = rms_scale(total, gain_ref[...]).astype(jnp.bfloat16)
    mixed_ref[...] = mixed
    out_ref[...] = times(place_ref[0] + place_ref[1], mixed, 0, 0).astype(jnp.bfloat16)


def middle_forward(at, attended, pieces, state, gain, place):
    rows, width = state.shape
    slots = place.shape[2]
    return pl.pallas_call(
        middle_forward_kernel,
        out_shape=(
            jax.ShapeDtypeStruct((rows, width), jnp.float32),
            jax.ShapeDtypeStruct((rows, width), jnp.bfloat16),
            jax.ShapeDtypeStruct((slots, width), jnp.bfloat16),
        ),
        in_specs=[pl.BlockSpec(memory_space=pltpu.SMEM)] + vmem(4) + vmem(4),
        out_specs=tuple(vmem(3)),
        compiler_params=kernel_params(),
        cost_estimate=cost(2 * rows * width * (width + slots), 9 * 2**20),
        name="middle_forward",
    )(at, attended, state, gain, place, *pieces)


def middle_back_kernel(experts, at_ref, place_ref, back_ref, upstream_ref, middle_ref, mixed_ref, gain_ref, router_ref, chosen_ref, *refs):
    *results, w0, w1, w2, w3, grad_ref, low_ref, heads_ref, small_ref = refs
    weights = (w0, w1, w2, w3)
    rows, width = upstream_ref.shape
    part = w0.shape[0]
    upstream, mixed, router = upstream_ref[...], mixed_ref[...], router_ref[...]
    logits = times(mixed, router, 1, 1)
    ids = lax.broadcasted_iota(jnp.int32, logits.shape, 1)
    logits = jnp.where(ids < experts, logits, NEG)
    odds = jnp.exp(logits - jnp.max(logits, axis=1, keepdims=True))
    probs = odds / jnp.sum(odds, axis=1, keepdims=True)
    hits = [ids == chosen_ref[:, c : c + 1] for c in range(2)]
    picked = [jnp.sum(jnp.where(hit, probs, 0.0), axis=1, keepdims=True) for hit in hits]
    pair_total = picked[0] + picked[1]
    if results:
        signal = [jnp.sum(upstream * r[...].astype(jnp.float32), axis=1, keepdims=True) for r in results]
    else:
        signal = [jnp.sum(times(place_ref[c], back_ref[:, width:], 1, 0), axis=1, keepdims=True) for c in range(2)]
    mean = (picked[0] * signal[0] + picked[1] * signal[1]) / pair_total
    slopes = [(s - mean) / pair_total for s in signal]
    grad_probs = jnp.where(hits[0], slopes[0], 0.0) + jnp.where(hits[1], slopes[1], 0.0)
    grad_logits = probs * (grad_probs - jnp.sum(probs * grad_probs, axis=1, keepdims=True))
    high = grad_logits.astype(jnp.bfloat16)
    rest = (grad_logits - high.astype(jnp.float32)).astype(jnp.bfloat16)
    small_ref[...] = jnp.zeros_like(small_ref)
    router_part = times(high, mixed, 0, 0) + times(rest, mixed, 0, 0)
    small_ref[:experts, :] = router_part[:experts]
    grad_mixed = times(place_ref[0] + place_ref[1], back_ref[:, :width], 1, 0)
    grad_mixed = grad_mixed + times(high, router, 1, 0) + times(rest, router, 1, 0)
    pulled, gain_rows = rms_back(middle_ref[...], gain_ref[...], grad_mixed)
    small_ref[experts : experts + 1, :] = jnp.sum(gain_rows, axis=0, keepdims=True)
    grad = upstream + pulled
    grad_ref[...] = grad
    low = grad.astype(jnp.bfloat16)
    low_ref[...] = low
    for m in range(4):
        lanes = pl.ds(pl.multiple_of(at_ref[m] * part, 128), part)
        heads_ref[lanes, :] = times(weights[m][...], low, 1, 1).astype(jnp.bfloat16)


def middle_back(experts, at, place, back, upstream, middle, mixed, gain, router, chosen, results, pieces):
    rows, width = upstream.shape
    slots = place.shape[2]
    return pl.pallas_call(
        functools.partial(middle_back_kernel, experts),
        out_shape=(
            jax.ShapeDtypeStruct((rows, width), jnp.float32),
            jax.ShapeDtypeStruct((rows, width), jnp.bfloat16),
            jax.ShapeDtypeStruct((width, rows), jnp.bfloat16),
            jax.ShapeDtypeStruct((experts + 8, width), jnp.float32),
        ),
        in_specs=[pl.BlockSpec(memory_space=pltpu.SMEM)] + vmem(8 + len(results)) + vmem(4),
        out_specs=tuple(vmem(4)),
        compiler_params=kernel_params(),
        cost_estimate=cost(2 * rows * width * (width + slots), 10 * 2**20),
        name="middle_back",
    )(at, place, back, upstream, middle, mixed, gain, router, chosen, *results, *pieces)


def swap(x, mask):
    return lax.ppermute(x, "wt", [(i, i ^ mask) for i in range(4)])


def near_finish(far, own):
    return (own, swap(own, 1), far, swap(far, 1))


def wt_gather(own):
    return near_finish(swap(own, 2), own)


def wt_exchange(slices, me):
    def cut(m):
        return lax.dynamic_index_in_dim(slices, me ^ m, 0, keepdims=False)

    far = swap(jnp.stack([cut(2), cut(3)]), 2)
    near = swap(jnp.stack([cut(1), far[1]]), 1)
    return (cut(0), near[0], far[0], near[1])


def in_order(pieces, me, axis):
    own, near, far, last = pieces
    odd, high = me % 2 == 1, me >= 2
    low = (jnp.where(odd, near, own), jnp.where(odd, own, near))
    up = (jnp.where(odd, last, far), jnp.where(odd, far, last))
    first = [jnp.where(high, b, a) for a, b in zip(low, up)]
    second = [jnp.where(high, a, b) for a, b in zip(low, up)]
    return jnp.concatenate(first + second, axis=axis)


def tie(*arrays):
    return lax.optimization_barrier(arrays)


def ring_of(count):
    ring = list(range(0, count, 2)) + list(range(count - 1, 0, -2))
    offsets = [0] + [sign * step for step in range(1, count // 2) for sign in (-1, 1)] + [count // 2]
    table = [[ring[(ring.index(i) + k) % count] for k in offsets] for i in range(count)]
    return ring, jnp.asarray(table, jnp.int32)


def ring_start(x, ring):
    right = [(a, b) for a, b in zip(ring, ring[1:] + ring[:1])]
    left = [(b, a) for a, b in right]
    return lax.ppermute(x, "ctx", right), lax.ppermute(x, "ctx", left)


def ring_blocks(x, first, ring, early=None):
    count = len(ring)
    right = [(a, b) for a, b in zip(ring, ring[1:] + ring[:1])]
    left = [(b, a) for a, b in right]
    ahead, behind = first
    blocks = [x, ahead, behind]
    for _ in range(2, count // 2):
        ahead, behind = lax.ppermute(ahead, "ctx", right), lax.ppermute(behind, "ctx", left)
        blocks += [ahead, behind]
    if early is not None:
        ahead, behind, *early = tie(ahead, behind, *early)
    half = x.shape[0] // 2
    blocks += [lax.ppermute(ahead[:half], "ctx", right), lax.ppermute(behind[half:], "ctx", left)]
    return blocks if early is None else (blocks, early)


def all_to_all(x):
    return lax.all_to_all(x, "ctx", split_axis=0, concat_axis=0, tiled=True)


def rms_back(rows, gain, grad):
    scale = lax.rsqrt(jnp.mean(rows * rows, axis=-1, keepdims=True) + EPS)
    unit = rows * scale
    pulled = grad * gain
    return scale * (pulled - unit * jnp.mean(pulled * unit, axis=-1, keepdims=True)), grad * unit


def by_heads(mesh, tokens, cotangent, seq_lengths, block_deal, *rest):
    return (
        mesh.shape["ctx"] == KV_HEADS
        and mesh.shape["wt"] == 4
        and seq_lengths.shape[1] == 1
        and block_deal.shape[2] == 1
        and tokens.shape[1] == BLK
    )


def local_heads(
    mesh,
    tokens,
    cotangent,
    seq_lengths,
    block_deal,
    routes,
    attention_gain,
    query_weight,
    key_weight,
    value_weight,
    out_weight,
    mixture_gain,
    router_weight,
    gate_weight,
    up_weight,
    down_weight,
):
    n_ctx = mesh.shape["ctx"]
    rows = tokens.shape[1]
    width = tokens.shape[2]
    layers = query_weight.shape[0]
    experts = router_weight.shape[2]
    capacity = 3 * rows // experts
    slot_count = experts * capacity
    rep = HEADS // KV_HEADS
    wide = rep * HEAD
    lanes = wide + 2 * HEAD
    part = width // 4
    ctx = lax.axis_index("ctx")
    mine = ctx.astype(jnp.int32).reshape(1)
    wt = lax.axis_index("wt").astype(jnp.uint32)
    others = (wt ^ jnp.arange(4, dtype=jnp.uint32)).astype(jnp.int32)
    table = block_deal[0, :, 0]
    devices = jnp.arange(n_ctx, dtype=jnp.int32)
    owner_of = jnp.sum(jnp.where(table[None, :] == devices[:, None], devices[None, :], 0), axis=1)
    ring, ring_table = ring_of(n_ctx)
    ring_owners = lax.dynamic_index_in_dim(ring_table, ctx.astype(jnp.uint32), 0, keepdims=False)
    spots = jnp.sum(jnp.where(ring_owners[:, None] == devices[None, :], table[None, :], 0), axis=1)

    first = ring_start(tokens[0], ring)

    expert_ids = jnp.arange(experts, dtype=jnp.int32)
    chosen = routes[:, 0]
    flat = chosen.reshape(layers, 2 * rows)
    onehot = flat[:, :, None] == expert_ids
    earlier = jnp.tril(jnp.ones((2 * rows, 2 * rows), jnp.bfloat16), -1)
    rank = jnp.einsum("ij,lje->lie", earlier, onehot.astype(jnp.bfloat16), preferred_element_type=jnp.float32)
    rank = jnp.sum(jnp.where(onehot, rank, 0.0), axis=2).astype(jnp.int32)
    slots = (flat * capacity + rank).reshape(layers, rows, 2).transpose(0, 2, 1)
    place = (slots[..., None] == jnp.arange(slot_count, dtype=jnp.int32)).astype(jnp.bfloat16)
    named = (chosen.transpose(0, 2, 1)[..., None] == expert_ids).astype(jnp.float32)

    small_rows = jnp.concatenate(
        [
            router_weight.transpose(0, 2, 1),
            attention_gain[:, None],
            mixture_gain[:, None],
            jnp.zeros((layers, 14 - experts, part), jnp.bfloat16),
        ],
        axis=1,
    )
    deep = lanes + 16
    head_own = head_rows(mine, query_weight, key_weight, value_weight, small_rows, wide, HEAD)
    head_own = head_own.reshape(layers * deep, part)
    head_far = swap(head_own, 2)

    out_own = list(out_weight)
    gate_own = [gate_weight[layer, 0] for layer in range(layers)]
    up_own = [up_weight[layer, 0] for layer in range(layers)]
    down_own = [down_weight[layer, 0] for layer in range(layers)]
    query_own = list(query_weight)
    pair_own_weights = [jnp.concatenate([key_weight[layer], value_weight[layer]], axis=1) for layer in range(layers)]
    out_far, gate_far, up_far, down_far, query_far, key_far = [
        [swap(own, 2) for own in group]
        for group in (out_own, gate_own, up_own, down_own, query_own, pair_own_weights)
    ]

    last = layers - 1
    other = chosen[last].transpose(1, 0)[::-1, :, None].astype(jnp.bfloat16)
    cot_rows = jnp.concatenate(
        [jnp.broadcast_to(cotangent[0][None], (2, rows, width)), jnp.broadcast_to(other, (2, rows, 128))], axis=2
    ).reshape(2 * rows, width + 128)
    cot_out = times(place[last].reshape(2 * rows, slot_count), cot_rows, 0, 0).astype(jnp.bfloat16)

    state = tokens[0].astype(jnp.float32)
    saved = []
    for layer in range(layers):
        if layer == 0:
            blocks, head_pieces = ring_blocks(tokens[0], first, ring, near_finish(head_far, head_own))
            small_all = [
                in_order([piece[i * deep + lanes : (i + 1) * deep] for piece in head_pieces], wt, 1)
                for i in range(layers)
            ]
            cot_out = tie(cot_out, *blocks[-2:])[0]
            cot_slots = all_to_all(cot_out.reshape(experts, capacity, width + 128)).reshape(slot_count, width + 128)
        router = jnp.concatenate([small_all[layer][:experts], jnp.zeros((128 - experts, width), jnp.bfloat16)])
        gain_one = small_all[layer][experts : experts + 1].astype(jnp.float32)
        gain_two = small_all[layer][experts + 1 : experts + 2].astype(jnp.float32)
        if layer > 0:
            normed = rms_scale(state, gain_one).astype(jnp.bfloat16)
            blocks = ring_blocks(normed, ring_start(normed, ring), ring)
        normed_all, qkv, sent, exact, log_total = front(
            layer == 0, spots, owner_of, others, blocks, gain_one, head_pieces, layer * deep, rep, HEAD
        )
        if layer == 0:
            sent, cot_slots = tie(sent, cot_slots)
        else:
            sent, out_far[layer], up_far[layer] = tie(sent, out_far[layer], up_far[layer])
        attended = all_to_all(sent).reshape(width, rows)
        if layer == 0:
            attended, out_far[layer] = tie(attended, out_far[layer])
        out_pieces = near_finish(out_far[layer], out_own[layer])
        middle, mixed, outgoing = middle_forward(others, attended, out_pieces, state, gain_two, place[layer])
        outgoing = outgoing.reshape(experts, capacity, width)
        if layer == 0:
            outgoing, gate_far[layer] = tie(outgoing, gate_far[layer])
        else:
            outgoing, down_far[layer], *saved[0]["attended"] = tie(outgoing, down_far[layer], *saved[0]["attended"])
            kept_exchange = wt_exchange(attended.reshape(4, part, rows), wt)
        arrived = all_to_all(outgoing).reshape(slot_count, width)
        if layer == 0:
            kept_exchange = wt_exchange(attended.reshape(4, part, rows), wt)
        else:
            arrived, query_far[layer] = tie(arrived, query_far[layer])
        probs = jax.nn.softmax(times(mixed, router[:experts], 1, 1), axis=-1)
        picked = jnp.sum(named[layer] * probs[None], axis=-1, keepdims=True)
        pair_total = picked[0] + picked[1]
        gates = picked / pair_total
        kept = dict(
            state=state,
            normed_all=normed_all,
            qkv=qkv,
            exact=exact,
            log_total=log_total,
            attended=kept_exchange,
            middle=middle,
            mixed=mixed,
            gates=gates,
            arrived=arrived,
            gain_one=gain_one,
            gain_two=gain_two,
            router=router,
            out_pieces=out_pieces,
        )
        pieces = [near_finish(far[layer], own[layer]) for far, own in ((gate_far, gate_own), (up_far, up_own), (down_far, down_own))]
        kept["pieces"] = pieces
        saved.append(kept)
        if layer == last:
            break
        made, kept["gate_values"], kept["up_values"], kept["inner"] = expert_forward(arrived, *pieces)
        returned = all_to_all(made.reshape(experts, capacity, width)).reshape(slot_count, width)
        returned, gate_far[last] = tie(returned, gate_far[last])
        results = [times(place[layer, choice], returned, 1, 0) for choice in range(2)]
        kept["results"] = [result.astype(jnp.bfloat16) for result in results]
        state = middle + gates[0] * results[0] + gates[1] * results[1]

    upstream = cotangent[0].astype(jnp.float32)
    expert_done, head_done, returned, sources = None, None, None, None
    merge = lambda head, out: jnp.concatenate([head] + [out[:, i * part : (i + 1) * part] for i in range(4)], axis=0)
    smalls, gain_sums = [None] * layers, [None] * layers
    block_output = None
    for layer in reversed(range(layers)):
        k = saved[layer]
        gates, pieces = k["gates"], k["pieces"]
        if layer == last:
            arrived = k["arrived"]
            made, back, arrived_grad, inner, grad_gate, grad_up = expert_both(
                experts, mine, arrived, cot_slots, k["router"], *pieces
            )
            back = all_to_all(back.reshape(experts, capacity, width + 128))
            back = back.reshape(slot_count, width + 128)
            results = []
        else:
            arrived, inner = k["arrived"], k["inner"]
            back_rows = (gates * upstream[None]).astype(jnp.bfloat16).reshape(2 * rows, width)
            outgoing = times(place[layer].reshape(2 * rows, slot_count), back_rows, 0, 0).astype(jnp.bfloat16)
            outgoing, returned, head_sum, key_far[layer] = tie(outgoing, returned, sources[0], key_far[layer])
            sources = [lax.all_gather(merge(head_sum, sources[1]), "ctx", axis=0)]
            arrived_grad = all_to_all(outgoing.reshape(experts, capacity, width)).reshape(slot_count, width)
            state = saved[last]["middle"] + sum(
                saved[last]["gates"][i] * times(place[last, i], returned, 1, 0) for i in range(2)
            )
            block_output = state.astype(jnp.bfloat16)[None]
            back, grad_gate, grad_up = expert_backward(arrived_grad, *pieces, k["gate_values"], k["up_values"])
            back, *last_parts[2:4] = tie(back, *last_parts[2:4])
            back = all_to_all(back.reshape(experts, capacity, width)).reshape(slot_count, width)
            results = k["results"]
        pair_give, far_give, pair_own, pair_far, down_give, down_kept, down_far_part = expert_grads(
            arrived, arrived_grad, inner, grad_gate, grad_up
        )
        pair_near, far_near, down_near = swap(pair_give, 1), swap(far_give, 1), swap(down_give, 1)
        add = lambda a, b: (a.astype(jnp.float32) + b.astype(jnp.float32)).astype(jnp.bfloat16)
        pair_sums = [add(pair_far[i], far_near[i]) for i in range(2)]
        down_sum = add(down_far_part, down_near[1:])
        if layer == last:
            back, key_far[layer] = tie(back, key_far[layer])
        else:
            back, last_parts[6] = tie(back, last_parts[6])
            pair_done, down_done = last_finish(*last_parts)
            expert_done = [*pair_done, *down_done]
        pair_last = [swap(pair_sum, 2) for pair_sum in pair_sums]
        if layer == last:
            down_last = [swap(down_sum[0], 2)]
        grad_middle, middle_low, grad_attended, small = middle_back(
            experts,
            others,
            place[layer],
            back,
            upstream,
            k["middle"],
            k["mixed"],
            k["gain_two"],
            k["router"],
            chosen[layer],
            results,
            k["out_pieces"],
        )
        grad_heads = all_to_all(grad_attended.reshape(n_ctx, wide, rows))
        if layer == last:
            grad_heads, *k["attended"] = tie(grad_heads, *k["attended"])
        grad_whole, grad_sent = attend_back(owner_of, k["qkv"], k["exact"], k["log_total"], grad_heads, rep, HEAD)
        middle_pieces = wt_gather(middle_low)
        out_part = times(jnp.concatenate(k["attended"], axis=1), jnp.concatenate(middle_pieces, axis=0), 1, 0)
        out_part = out_part.astype(jnp.bfloat16)
        if layer == 0:
            out_rows = all_to_all(out_part.reshape(n_ctx, part // n_ctx, width))
            grad_sent, out_rows, *expert_done = tie(grad_sent, out_rows, *expert_done)
        else:
            grad_sent, query_far[0], out_part = tie(grad_sent, query_far[0], out_part)
            out_rows = lax.psum_scatter(out_part, "ctx", scatter_dimension=0, tiled=True)
        grad_own = all_to_all(grad_sent)
        if layer == 0:
            grad_whole, *pair_last = tie(grad_whole, *pair_last)
        head_give, head_kept, head_far = head_grads(others, k["normed_all"], grad_whole, small)
        head_near = swap(head_give, 1)
        head_last = swap(add(head_far[0], head_near[1]), 2)
        head_sum = (
            head_kept[0].astype(jnp.float32) + head_near[0].astype(jnp.float32) + head_last.astype(jnp.float32)
        ).astype(jnp.bfloat16)
        weights = [(query_weight[i], key_weight[i], value_weight[i]) for i in range(layers)]
        columns = lambda at, *rest: spread(at, layers, *rest[:2], weights[at], wide, HEAD, 16, rest[2])
        if layer == last:
            sources = [head_sum, out_rows]
            last_parts = [pair_own, pair_near, *pair_last, down_kept, down_near, *down_last]
            last_finish = lambda *p: (finish(last, layers, *p[:2], p[2:4], None), finish(last, layers, *p[4:6], p[6:], None))
            made = tie(made, grad_own)[0]
            returned = all_to_all(made.reshape(experts, capacity, width)).reshape(slot_count, width)
        else:
            *head_done, smalls[last], gain_sums[last] = columns(last, None, sources, None)
            out_rows = jnp.sum(out_rows.astype(jnp.float32), axis=0).astype(jnp.bfloat16)
            merged = merge(head_sum, out_rows)
            merged, *head_done = tie(merged, *head_done)
            down_last = [swap(tie(down_sum, head_last)[0][0], 2)]
            sources = ring_blocks(merged, ring_start(merged, ring), ring)
            *sources[-2:], down_last[0] = tie(*sources[-2:], down_last[0])
            pair_done = finish(layer, layers, pair_own, pair_near, pair_last, expert_done[:2])
            down_done = finish(layer, layers, down_kept, down_near, down_last, expert_done[2:])
            expert_done = [*pair_done, *down_done]
            sources[-1], *expert_done = tie(sources[-1], *expert_done)
            *head_done, smalls[layer], gain_sums[layer] = columns(layer, ring_owners, sources, head_done)
        own_query = grad_own[:, :wide].reshape(width, rows)
        own_pair = jnp.concatenate(
            [
                grad_own[:, wide : wide + HEAD].reshape(n_ctx * HEAD, rows),
                grad_own[:, wide + HEAD :].reshape(n_ctx * HEAD, rows),
            ],
            axis=0,
        )
        query_pieces = near_finish(query_far[layer], query_own[layer])
        key_pieces = near_finish(key_far[layer], pair_own_weights[layer])
        grad_normed = jnp.zeros((rows, width), jnp.float32)
        for m in range(4):
            grad_normed = lax.dynamic_update_slice_in_dim(
                grad_normed,
                times(own_query, query_pieces[m], 0, 1) + times(own_pair, key_pieces[m], 0, 1),
                (wt ^ m) * part,
                1,
            )
        pulled, _ = rms_back(k["state"], k["gain_one"], grad_normed)
        upstream = grad_middle + pulled
    gain_one_grad = jnp.stack([s[:, 0] for s in gain_sums]) / attention_gain.astype(jnp.float32)
    small_grads = jnp.stack(smalls)
    query_grad, key_grad, value_grad, out_grad = head_done
    return (
        block_output,
        upstream[None],
        gain_one_grad,
        query_grad,
        key_grad,
        value_grad,
        out_grad,
        small_grads[:, experts],
        small_grads[:, :experts].transpose(0, 2, 1),
        *expert_done,
    )


def local_rows(
    tokens,
    cotangent,
    seq_lengths,
    block_deal,
    routes,
    attention_gain,
    query_weight,
    key_weight,
    value_weight,
    out_weight,
    mixture_gain,
    router_weight,
    gate_weight,
    up_weight,
    down_weight,
):
    rows_here = tokens.shape[1]
    width = tokens.shape[2]
    layers = query_weight.shape[0]
    experts = router_weight.shape[2]
    capacity = 3 * rows_here // experts
    kv_groups = KV_HEADS
    per_group = HEADS // KV_HEADS
    head_size = HEAD
    kv_width = kv_groups * head_size
    scale = head_size ** (-0.5)
    device = lax.axis_index("ctx")
    everywhere = stream_positions(block_deal[0], BLK)
    every_seq = sequence_ids(everywhere, seq_lengths[0])
    own_pos = lax.dynamic_slice_in_dim(everywhere, device * rows_here, rows_here, 0)
    own_seq = lax.dynamic_slice_in_dim(every_seq, device * rows_here, rows_here, 0)
    choice_rows = jnp.arange(2 * rows_here, dtype=jnp.int32) // 2
    expert_ids = jnp.arange(experts, dtype=jnp.int32)

    def block_mask(start, count):
        key_pos = lax.dynamic_slice_in_dim(everywhere, start, count, 0)
        key_seq = lax.dynamic_slice_in_dim(every_seq, start, count, 0)
        return (own_seq[:, None] == key_seq[None, :]) & (key_pos[None, :] <= own_pos[:, None])

    hidden_state = tokens[0].astype(jnp.float32)
    saved = []
    for layer in range(layers):
        shared = (
            lax.all_gather(attention_gain[layer], "wt", axis=0, tiled=True),
            lax.all_gather(query_weight[layer], "wt", axis=0, tiled=True),
            lax.all_gather(key_weight[layer], "wt", axis=0, tiled=True),
            lax.all_gather(value_weight[layer], "wt", axis=0, tiled=True),
            lax.all_gather(out_weight[layer], "wt", axis=0, tiled=True),
            lax.all_gather(mixture_gain[layer], "wt", axis=0, tiled=True),
            lax.all_gather(router_weight[layer], "wt", axis=0, tiled=True),
        )
        gain_one, full_query, full_key, full_value, full_out, gain_two, full_router = shared
        normed = rms_scale(hidden_state, gain_one.astype(jnp.float32)).astype(jnp.bfloat16)
        queries = jnp.dot(normed, full_query, preferred_element_type=jnp.float32).astype(
            jnp.bfloat16
        )
        keys = jnp.dot(normed, full_key, preferred_element_type=jnp.float32).astype(jnp.bfloat16)
        values = jnp.dot(normed, full_value, preferred_element_type=jnp.float32).astype(
            jnp.bfloat16
        )
        query_heads = queries.reshape(rows_here, kv_groups, per_group, head_size)
        start_state = (
            jnp.full((kv_groups, per_group, rows_here), NEG, jnp.float32),
            jnp.zeros((kv_groups, per_group, rows_here), jnp.float32),
            jnp.zeros((kv_groups, per_group, rows_here, head_size), jnp.float32),
        )
        gathered = None
        key_piece = lax.all_gather(keys, "ctx", axis=0, tiled=True)
        value_piece = lax.all_gather(values, "ctx", axis=0, tiled=True)
        absorb_count = key_piece.shape[0]
        absorb_span = 512

        def turn(index, state):
            first = index * absorb_span
            key_block = lax.dynamic_slice_in_dim(key_piece, first, absorb_span, 0).reshape(
                absorb_span, kv_groups, head_size
            )
            value_block = lax.dynamic_slice_in_dim(value_piece, first, absorb_span, 0).reshape(
                absorb_span, kv_groups, head_size
            )
            allowed = block_mask(first, absorb_span)

            def work(state):
                top, total, summed = state
                scores = (
                    jnp.einsum(
                        "tgrd,kgd->grtk", query_heads, key_block, preferred_element_type=jnp.float32
                    )
                    * scale
                )
                scores = jnp.where(allowed[None, None], scores, NEG)
                top_new = jnp.maximum(top, jnp.max(scores, axis=-1))
                fade = jnp.exp(top - top_new)
                weights = jnp.where(allowed[None, None], jnp.exp(scores - top_new[..., None]), 0.0)
                total = total * fade + jnp.sum(weights, axis=-1)
                summed = summed * fade[..., None] + jnp.einsum(
                    "grtk,kgd->grtd",
                    weights.astype(jnp.bfloat16),
                    value_block,
                    preferred_element_type=jnp.float32,
                )
                return (top_new, total, summed)

            return lax.cond(jnp.any(allowed), work, unchanged, state)

        top, total, summed = lax.fori_loop(0, absorb_count // absorb_span, turn, start_state)
        attended = (summed / total[..., None]).transpose(2, 0, 1, 3).reshape(rows_here, width)
        log_total = top + jnp.log(total)
        attended_low = attended.astype(jnp.bfloat16)
        middle = hidden_state + jnp.dot(attended_low, full_out, preferred_element_type=jnp.float32)
        mixed_low = rms_scale(middle, gain_two.astype(jnp.float32)).astype(jnp.bfloat16)
        probs = jax.nn.softmax(
            jnp.dot(mixed_low, full_router, preferred_element_type=jnp.float32), axis=-1
        )
        chosen = routes[layer, 0]
        picked = jnp.take_along_axis(probs, chosen, axis=1)
        gates = picked / jnp.sum(picked, axis=1, keepdims=True)
        flat_choice = chosen.reshape(-1)
        onehot = (flat_choice[:, None] == expert_ids[None, :]).astype(jnp.int32)
        rank = jnp.sum((jnp.cumsum(onehot, axis=0) - onehot) * onehot, axis=1)
        slots = flat_choice * capacity + rank
        outgoing = (
            jnp.zeros((experts * capacity, width), jnp.bfloat16)
            .at[slots]
            .set(mixed_low[choice_rows])
            .reshape(experts, capacity, width)
        )
        arrived = lax.all_to_all(outgoing, "ctx", split_axis=0, concat_axis=0, tiled=True)
        expert_full = (
            lax.all_gather(gate_weight[layer, 0], "wt", axis=1, tiled=True),
            lax.all_gather(up_weight[layer, 0], "wt", axis=1, tiled=True),
            lax.all_gather(down_weight[layer, 0], "wt", axis=0, tiled=True),
        )
        gate_full, up_full, down_full = expert_full
        expert_rows = arrived.reshape(-1, width)
        gate_value = jnp.dot(expert_rows, gate_full, preferred_element_type=jnp.float32)
        up_value = jnp.dot(expert_rows, up_full, preferred_element_type=jnp.float32)
        inner = (jax.nn.silu(gate_value) * up_value).astype(jnp.bfloat16)
        produced = (
            jnp.dot(inner, down_full, preferred_element_type=jnp.float32)
            .astype(jnp.bfloat16)
            .reshape(experts, capacity, width)
        )
        returned = lax.all_to_all(produced, "ctx", split_axis=0, concat_axis=0, tiled=True)
        expert_out = (
            returned.reshape(-1, width)[slots].reshape(rows_here, 2, width).astype(jnp.float32)
        )
        saved.append(
            (
                hidden_state,
                shared,
                normed,
                query_heads,
                keys,
                values,
                gathered,
                attended,
                attended_low,
                log_total,
                middle,
                mixed_low,
                probs,
                chosen,
                picked,
                gates,
                slots,
                expert_full,
                expert_rows,
                gate_value,
                up_value,
                inner,
                expert_out,
            )
        )
        hidden_state = middle + jnp.sum(gates[:, :, None] * expert_out, axis=1)
    block_output = hidden_state.astype(jnp.bfloat16)[None]
    upstream = cotangent[0].astype(jnp.float32)
    collected = []
    for layer in reversed(range(layers)):
        (
            layer_input,
            shared,
            normed,
            query_heads,
            keys,
            values,
            gathered,
            attended,
            attended_low,
            log_total,
            middle,
            mixed_low,
            probs,
            chosen,
            picked,
            gates,
            slots,
            expert_full,
            expert_rows,
            gate_value,
            up_value,
            inner,
            expert_out,
        ) = saved[layer]
        gain_one, full_query, full_key, full_value, full_out, gain_two, full_router = shared
        gate_full, up_full, down_full = expert_full
        gate_signal = jnp.sum(upstream[:, None, :] * expert_out, axis=-1)
        back_rows = (
            (gates[:, :, None] * upstream[:, None, :]).astype(jnp.bfloat16).reshape(-1, width)
        )
        outgoing_grad = (
            jnp.zeros((experts * capacity, width), jnp.bfloat16)
            .at[slots]
            .set(back_rows)
            .reshape(experts, capacity, width)
        )
        arrived_grad = lax.all_to_all(
            outgoing_grad, "ctx", split_axis=0, concat_axis=0, tiled=True
        ).reshape(-1, width)
        grad_down = outer_rows(inner, arrived_grad)
        grad_inner = times_transposed(arrived_grad, down_full)
        sigma = jax.nn.sigmoid(gate_value)
        grad_gate_value = (
            grad_inner * up_value * sigma * (1.0 + gate_value * (1.0 - sigma))
        ).astype(jnp.bfloat16)
        grad_up_value = (grad_inner * gate_value * sigma).astype(jnp.bfloat16)
        grad_gate = outer_rows(expert_rows, grad_gate_value)
        grad_up = outer_rows(expert_rows, grad_up_value)
        grad_rows = (
            (
                times_transposed(grad_gate_value, gate_full)
                + times_transposed(grad_up_value, up_full)
            )
            .astype(jnp.bfloat16)
            .reshape(experts, capacity, width)
        )
        back_grad = lax.all_to_all(grad_rows, "ctx", split_axis=0, concat_axis=0, tiled=True)
        grad_mixed = jnp.sum(
            back_grad.reshape(-1, width)[slots].reshape(rows_here, 2, width).astype(jnp.float32),
            axis=1,
        )
        pair_total = jnp.sum(picked, axis=1, keepdims=True)
        grad_picked = (
            gate_signal - jnp.sum(gates * gate_signal, axis=1, keepdims=True)
        ) / pair_total
        grad_probs = jnp.sum(
            grad_picked[:, :, None]
            * (chosen[:, :, None] == expert_ids[None, None, :]).astype(jnp.float32),
            axis=1,
        )
        grad_logits = probs * (grad_probs - jnp.sum(probs * grad_probs, axis=1, keepdims=True))
        grad_router = lax.dot_general(
            mixed_low.astype(jnp.float32),
            grad_logits,
            (((0,), (0,)), ((), ())),
            precision=lax.Precision.HIGHEST,
            preferred_element_type=jnp.float32,
        )
        grad_mixed = grad_mixed + lax.dot_general(
            grad_logits,
            full_router.astype(jnp.float32),
            (((1,), (1,)), ((), ())),
            precision=lax.Precision.HIGHEST,
            preferred_element_type=jnp.float32,
        )
        norm_value, pull_two = jax.vjp(rms_scale, middle, gain_two.astype(jnp.float32))
        grad_middle_norm, grad_gain_two = pull_two(grad_mixed)
        grad_middle = upstream + grad_middle_norm
        middle_low = grad_middle.astype(jnp.bfloat16)
        grad_out = outer_rows(attended_low, middle_low)
        grad_attended = times_transposed(middle_low, full_out).astype(jnp.bfloat16)
        grad_heads = grad_attended.reshape(rows_here, kv_groups, per_group, head_size)
        attended_heads = attended.reshape(rows_here, kv_groups, per_group, head_size)
        delta = jnp.sum(grad_heads.astype(jnp.float32) * attended_heads, axis=-1).transpose(1, 2, 0)
        whole = (
            lax.all_gather(keys, "ctx", axis=0, tiled=True),
            lax.all_gather(values, "ctx", axis=0, tiled=True),
        )
        key_all, value_all = whole
        total_rows = key_all.shape[0]
        span = 512

        def score_block(first, count, allowed):
            key_block = lax.dynamic_slice_in_dim(key_all, first, count, 0).reshape(
                count, kv_groups, head_size
            )
            value_block = lax.dynamic_slice_in_dim(value_all, first, count, 0).reshape(
                count, kv_groups, head_size
            )
            scores = (
                jnp.einsum(
                    "tgrd,kgd->grtk", query_heads, key_block, preferred_element_type=jnp.float32
                )
                * scale
            )
            probs_block = jnp.where(
                allowed[None, None], jnp.exp(scores - log_total[..., None]), 0.0
            )
            grad_probs_block = jnp.einsum(
                "tgrd,kgd->grtk", grad_heads, value_block, preferred_element_type=jnp.float32
            )
            grad_scores = (probs_block * (grad_probs_block - delta[..., None])).astype(jnp.bfloat16)
            return (key_block, probs_block, grad_scores)

        def key_terms(probs_block, grad_scores, count):
            key_part = (
                jnp.einsum(
                    "grtk,tgrd->kgd", grad_scores, query_heads, preferred_element_type=jnp.float32
                )
                * scale
            ).reshape(count, kv_width)
            value_part = jnp.einsum(
                "grtk,tgrd->kgd",
                probs_block.astype(jnp.bfloat16),
                grad_heads,
                preferred_element_type=jnp.float32,
            ).reshape(count, kv_width)
            return (key_part, value_part)

        query_start = jnp.zeros((rows_here, kv_groups, per_group, head_size), jnp.float32)

        def turn_back(index, state):
            first = index * span
            allowed = block_mask(first, span)

            def work(state):
                grad_query, grad_keys, grad_values = state
                key_block, probs_block, grad_scores = score_block(first, span, allowed)
                grad_query = (
                    grad_query
                    + jnp.einsum(
                        "grtk,kgd->tgrd", grad_scores, key_block, preferred_element_type=jnp.float32
                    )
                    * scale
                )
                key_part, value_part = key_terms(probs_block, grad_scores, span)
                grad_keys = lax.dynamic_update_slice_in_dim(grad_keys, key_part, first, 0)
                grad_values = lax.dynamic_update_slice_in_dim(grad_values, value_part, first, 0)
                return (grad_query, grad_keys, grad_values)

            return lax.cond(jnp.any(allowed), work, unchanged, state)

        back_start = (
            query_start,
            jnp.zeros((total_rows, kv_width), jnp.float32),
            jnp.zeros((total_rows, kv_width), jnp.float32),
        )
        grad_query, grad_keys, grad_values = lax.fori_loop(
            0, total_rows // span, turn_back, back_start
        )
        grad_keys, grad_values = (
            lax.psum_scatter(
                grad_keys.astype(jnp.bfloat16), "ctx", scatter_dimension=0, tiled=True
            ).astype(jnp.float32),
            lax.psum_scatter(
                grad_values.astype(jnp.bfloat16), "ctx", scatter_dimension=0, tiled=True
            ).astype(jnp.float32),
        )
        query_low = grad_query.reshape(rows_here, width).astype(jnp.bfloat16)
        key_low = grad_keys.astype(jnp.bfloat16)
        value_low = grad_values.astype(jnp.bfloat16)
        grad_query_weight = outer_rows(normed, query_low)
        grad_key_weight = outer_rows(normed, key_low)
        grad_value_weight = outer_rows(normed, value_low)
        grad_normed = (
            times_transposed(query_low, full_query)
            + times_transposed(key_low, full_key)
            + times_transposed(value_low, full_value)
        )
        norm_value, pull_one = jax.vjp(rms_scale, layer_input, gain_one.astype(jnp.float32))
        grad_input_norm, grad_gain_one = pull_one(grad_normed)
        upstream = grad_middle + grad_input_norm
        part_one, part_query, part_key, part_value, part_out, part_two, part_router = (
            lax.psum_scatter(
                grad_gain_one.astype(jnp.bfloat16), "wt", scatter_dimension=0, tiled=True
            ).astype(jnp.float32),
            lax.psum_scatter(
                grad_query_weight.astype(jnp.bfloat16), "wt", scatter_dimension=0, tiled=True
            ).astype(jnp.float32),
            lax.psum_scatter(
                grad_key_weight.astype(jnp.bfloat16), "wt", scatter_dimension=0, tiled=True
            ).astype(jnp.float32),
            lax.psum_scatter(
                grad_value_weight.astype(jnp.bfloat16), "wt", scatter_dimension=0, tiled=True
            ).astype(jnp.float32),
            lax.psum_scatter(
                grad_out.astype(jnp.bfloat16), "wt", scatter_dimension=0, tiled=True
            ).astype(jnp.float32),
            lax.psum_scatter(
                grad_gain_two.astype(jnp.bfloat16), "wt", scatter_dimension=0, tiled=True
            ).astype(jnp.float32),
            lax.psum_scatter(
                grad_router.astype(jnp.bfloat16), "wt", scatter_dimension=0, tiled=True
            ).astype(jnp.float32),
        )
        summed_parts = (
            lax.psum(part_one.astype(jnp.bfloat16), "ctx").astype(jnp.float32),
            lax.psum(part_query.astype(jnp.bfloat16), "ctx").astype(jnp.float32),
            lax.psum(part_key.astype(jnp.bfloat16), "ctx").astype(jnp.float32),
            lax.psum(part_value.astype(jnp.bfloat16), "ctx").astype(jnp.float32),
            lax.psum(part_out.astype(jnp.bfloat16), "ctx").astype(jnp.float32),
            lax.psum(part_two.astype(jnp.bfloat16), "ctx").astype(jnp.float32),
            lax.psum(part_router.astype(jnp.bfloat16), "ctx").astype(jnp.float32),
        )
        expert_parts = (
            lax.psum_scatter(
                grad_gate.astype(jnp.bfloat16), "wt", scatter_dimension=1, tiled=True
            ).astype(jnp.float32),
            lax.psum_scatter(
                grad_up.astype(jnp.bfloat16), "wt", scatter_dimension=1, tiled=True
            ).astype(jnp.float32),
            lax.psum_scatter(
                grad_down.astype(jnp.bfloat16), "wt", scatter_dimension=0, tiled=True
            ).astype(jnp.float32),
        )
        collected.append((summed_parts, expert_parts))
    ordered = collected[::-1]
    attention_gain_grad = jnp.stack([item[0][0] for item in ordered])
    query_grad = jnp.stack([item[0][1] for item in ordered])
    key_grad = jnp.stack([item[0][2] for item in ordered])
    value_grad = jnp.stack([item[0][3] for item in ordered])
    out_grad = jnp.stack([item[0][4] for item in ordered])
    mixture_gain_grad = jnp.stack([item[0][5] for item in ordered])
    router_grad = jnp.stack([item[0][6] for item in ordered])
    gate_grad = jnp.stack([item[1][0] for item in ordered])[:, None]
    up_grad = jnp.stack([item[1][1] for item in ordered])[:, None]
    down_grad = jnp.stack([item[1][2] for item in ordered])[:, None]
    return (
        block_output,
        upstream[None],
        attention_gain_grad,
        query_grad,
        key_grad,
        value_grad,
        out_grad,
        mixture_gain_grad,
        router_grad,
        gate_grad,
        up_grad,
        down_grad,
    )


def solution(mesh):
    placed = (
        P("wt", "ctx", None),
        P("wt", "ctx", None),
        P("wt", None),
        P("wt", None, None),
        P(None, "wt", "ctx", None),
        P(None, "wt"),
        P(None, "wt", None),
        P(None, "wt", None),
        P(None, "wt", None),
        P(None, "wt", None),
        P(None, "wt"),
        P(None, "wt", None),
        P(None, "ctx", None, "wt"),
        P(None, "ctx", None, "wt"),
        P(None, "ctx", "wt", None),
    )
    def local(*arrays):
        if by_heads(mesh, *arrays):
            return local_heads(mesh, *arrays)
        return local_rows(*arrays)

    return jax.shard_map(
        local,
        mesh=mesh,
        in_specs=placed,
        out_specs=(
            P("wt", "ctx", None),
            P("wt", "ctx", None),
            P(None, "wt"),
            P(None, "wt", None),
            P(None, "wt", None),
            P(None, "wt", None),
            P(None, "wt", None),
            P(None, "wt"),
            P(None, "wt", None),
            P(None, "ctx", None, "wt"),
            P(None, "ctx", None, "wt"),
            P(None, "ctx", "wt", None),
        ),
        check_vma=False,
    )
```

```python
import functools

import jax
import jax.numpy as jnp
from jax import lax
from jax.experimental import pallas as pl
from jax.experimental.pallas import tpu as pltpu
from jax.sharding import PartitionSpec as P

HEADS = 24
KV_HEADS = 8
HEAD = 64
BLK = 128


EPS = 1e-05
NEG = -1e30


def rms_scale(rows, gain):
    return rows * lax.rsqrt(jnp.mean(rows * rows, axis=-1, keepdims=True) + EPS) * gain


def stream_positions(table, width):
    offsets = jnp.arange(width, dtype=jnp.int32)
    return (table[:, :, None] * width + offsets[None, None, :]).reshape(-1)


def sequence_ids(positions, seq_row):
    ends = jnp.cumsum(seq_row)
    return jnp.sum((positions[:, None] >= ends[None, :]).astype(jnp.int32), axis=1)


def outer_rows(left, right):
    return lax.dot_general(
        left, right, (((0,), (0,)), ((), ())), preferred_element_type=jnp.float32
    )


def times_transposed(left, right):
    return lax.dot_general(
        left, right, (((1,), (1,)), ((), ())), preferred_element_type=jnp.float32
    )


def unchanged(state):
    return state


def times(left, right, a, b):
    return lax.dot_general(left, right, (((a,), (b,)), ((), ())), preferred_element_type=jnp.float32)


def vmem(count):
    return [pl.BlockSpec(memory_space=pltpu.VMEM)] * count


def kernel_params():
    return pltpu.CompilerParams(vmem_limit_bytes=56 * 2**20)


def cost(flops, nbytes, transcendentals=0):
    return pl.CostEstimate(flops=int(flops), bytes_accessed=int(nbytes), transcendentals=int(transcendentals))


def causal_mask(span):
    key_at = lax.broadcasted_iota(jnp.int32, (span, span), 0)
    query_at = lax.broadcasted_iota(jnp.int32, (span, span), 1)
    return key_at <= query_at


def front_kernel(raw, rep, head, span, base, spot_ref, owner_ref, at_ref, *refs):
    *blocks, gain_ref, w0, w1, w2, w3, normed_ref, qkv_ref, sent_ref, exact_ref, log_ref = refs
    rows = blocks[0].shape[0]
    count = len(blocks) - 1
    tokens = count * rows
    width = rep * head
    scale = head ** (-0.5)
    gain = gain_ref[...]
    for k in range(count):
        low, high = (blocks[k],) * 2 if k < count - 1 else blocks[k:]
        half = low.shape[0] if k == count - 1 else rows
        for start, ref in ((0, low), (half, high)) if k == count - 1 else ((0, low),):
            block = ref[...]
            if raw:
                block = rms_scale(block.astype(jnp.float32), gain).astype(jnp.bfloat16)
            normed_ref[spot_ref[k], start : start + ref.shape[0], :] = block
    lanes_all = qkv_ref.shape[0]
    slice_width = w0.shape[1]
    for part in range(tokens // span):
        take = span // rows
        total = 0.0
        for m, weight_ref in enumerate((w0, w1, w2, w3)):
            lanes = pl.ds(pl.multiple_of(at_ref[m] * slice_width, 128), slice_width)
            piece = normed_ref[part * take : (part + 1) * take, :, lanes].reshape(span, slice_width)
            total = total + times(weight_ref[base : base + lanes_all, :], piece, 1, 1)
        qkv_ref[:, part * span : (part + 1) * span] = total.astype(jnp.bfloat16)
    mask = causal_mask(span)
    per = span // rows
    for part in range(tokens // span):
        lanes = pl.ds(part * span, span)
        seen = (part + 1) * span
        keys = qkv_ref[width : width + head, :seen]
        values = qkv_ref[width + head : lanes_all, :seen]
        for h in range(rep):
            at = slice(h * head, (h + 1) * head)
            scores = times(keys, qkv_ref[at, lanes], 0, 0) * scale
            last = jnp.where(mask, scores[seen - span :], NEG)
            top = jnp.max(last, axis=0, keepdims=True)
            if part:
                top = jnp.maximum(top, jnp.max(scores[: seen - span], axis=0, keepdims=True))
            weights = jnp.exp(last - top)
            if part:
                weights = jnp.concatenate([jnp.exp(scores[: seen - span] - top), weights], axis=0)
            total = jnp.sum(weights, axis=0, keepdims=True)
            result = times(values, weights.astype(jnp.bfloat16), 1, 0) / total
            exact_ref[at, lanes] = result
            log_ref[h : h + 1, lanes] = top + jnp.log(total)
            for b in range(per):
                sent_ref[owner_ref[part * per + b], at, :] = result[:, b * rows : (b + 1) * rows].astype(jnp.bfloat16)


def front(raw, spots, owner_of, at, blocks, gain, pieces, base, rep, head):
    rows, width = blocks[0].shape
    count = len(blocks) - 1
    tokens = count * rows
    span = min(256, tokens)
    deep = (rep + 2) * head
    pairs = rep * tokens * (tokens + span) // 2
    return pl.pallas_call(
        functools.partial(front_kernel, raw, rep, head, span, base),
        out_shape=(
            jax.ShapeDtypeStruct((count, rows, width), jnp.bfloat16),
            jax.ShapeDtypeStruct((deep, tokens), jnp.bfloat16),
            jax.ShapeDtypeStruct((count, rep * head, rows), jnp.bfloat16),
            jax.ShapeDtypeStruct((rep * head, tokens), jnp.float32),
            jax.ShapeDtypeStruct((rep, tokens), jnp.float32),
        ),
        in_specs=[pl.BlockSpec(memory_space=pltpu.SMEM)] * 3 + vmem(len(blocks) + 5),
        out_specs=tuple(vmem(5)),
        compiler_params=kernel_params(),
        cost_estimate=cost(4 * head * pairs + 2 * deep * width * tokens, 9 * 2**20, pairs),
        name="front",
    )(spots, owner_of, at, *blocks, gain, *pieces)


def attend_back_kernel(rep, head, span, owner_ref, qkv_ref, exact_ref, log_ref, grad_ref, whole_ref, sent_ref, grad_all, keys_sum, values_sum):
    tokens = qkv_ref.shape[1]
    rows = grad_ref.shape[2]
    width = rep * head
    per = span // rows
    scale = head ** (-0.5)
    mask = causal_mask(span)
    for block in range(tokens // rows):
        grad_all[:, block * rows : (block + 1) * rows] = grad_ref[owner_ref[block]]
    keys_sum[...] = jnp.zeros_like(keys_sum)
    values_sum[...] = jnp.zeros_like(values_sum)
    for part in range(tokens // span):
        lanes = pl.ds(part * span, span)
        seen = (part + 1) * span
        keys = qkv_ref[width : width + head, :seen]
        values = qkv_ref[width + head :, :seen]
        for h in range(rep):
            at = slice(h * head, (h + 1) * head)
            queries = qkv_ref[at, lanes]
            grads = grad_all[at, lanes]
            delta = jnp.sum(grads.astype(jnp.float32) * exact_ref[at, lanes], axis=0, keepdims=True)
            scores = times(keys, queries, 0, 0) * scale
            probs = jnp.exp(scores - log_ref[h : h + 1, lanes])
            last = jnp.where(mask, probs[seen - span :], 0.0)
            probs = last if part == 0 else jnp.concatenate([probs[: seen - span], last], axis=0)
            pulled = times(values, grads, 0, 0)
            slopes = (probs * (pulled - delta)).astype(jnp.bfloat16)
            back = (times(keys, slopes, 1, 0) * scale).astype(jnp.bfloat16)
            whole_ref[at, lanes] = back
            for b in range(per):
                sent_ref[owner_ref[part * per + b], at, :] = back[:, b * rows : (b + 1) * rows]
            keys_sum[:, :seen] += times(queries, slopes, 1, 1)
            values_sum[:, :seen] += times(grads, probs.astype(jnp.bfloat16), 1, 1)
    keys_low = (keys_sum[...] * scale).astype(jnp.bfloat16)
    values_low = values_sum[...].astype(jnp.bfloat16)
    whole_ref[width : width + head, :] = keys_low
    whole_ref[width + head :, :] = values_low
    for block in range(tokens // rows):
        cut = slice(block * rows, (block + 1) * rows)
        sent_ref[owner_ref[block], width : width + head, :] = keys_low[:, cut]
        sent_ref[owner_ref[block], width + head :, :] = values_low[:, cut]


def attend_back(owner_of, qkv, exact, log_total, grads, rep, head):
    deep, tokens = qkv.shape
    count, _, rows = grads.shape
    span = min(256, tokens)
    pairs = rep * tokens * (tokens + span) // 2
    return pl.pallas_call(
        functools.partial(attend_back_kernel, rep, head, span),
        out_shape=(
            jax.ShapeDtypeStruct((deep, tokens), jnp.bfloat16),
            jax.ShapeDtypeStruct((count, deep, rows), jnp.bfloat16),
        ),
        in_specs=[pl.BlockSpec(memory_space=pltpu.SMEM)] + vmem(4),
        out_specs=tuple(vmem(2)),
        scratch_shapes=[
            pltpu.VMEM((rep * head, tokens), jnp.bfloat16),
            pltpu.VMEM((head, tokens), jnp.float32),
            pltpu.VMEM((head, tokens), jnp.float32),
        ],
        compiler_params=kernel_params(),
        cost_estimate=cost(10 * head * pairs, 6 * 2**20, pairs),
        name="attend_back",
    )(owner_of, qkv, exact, log_total, grads)


def silu_pair(gate_value, up_value):
    return (gate_value * jax.nn.sigmoid(gate_value) * up_value).astype(jnp.bfloat16)


def pair_back(grad_inner, gate_value, up_value):
    sigma = jax.nn.sigmoid(gate_value)
    grad_gate = grad_inner * up_value * sigma * (1.0 + gate_value * (1.0 - sigma))
    return grad_gate.astype(jnp.bfloat16), (grad_inner * gate_value * sigma).astype(jnp.bfloat16)


def by_piece(gate, up, down):
    return [piece for pieces in zip(gate, up, down) for piece in pieces]


def expert_forward_kernel(rows_ref, *refs):
    weights, (made_ref, gates_ref, ups_ref, inner_ref, total) = refs[:12], refs[12:]
    rows = rows_ref[...]
    for m in range(4):
        gate_value = times(rows, weights[3 * m][...], 1, 0)
        up_value = times(rows, weights[3 * m + 1][...], 1, 0)
        gates_ref[m] = gate_value
        ups_ref[m] = up_value
        inner = silu_pair(gate_value, up_value)
        inner_ref[m] = inner
        part = times(inner, weights[3 * m + 2][...], 1, 0)
        if m == 0:
            total[...] = part
        elif m < 3:
            total[...] += part
        else:
            made_ref[...] = (total[...] + part).astype(jnp.bfloat16)


def expert_forward(rows, gate, up, down):
    count, width = rows.shape
    hidden = gate[0].shape[1]
    weights = by_piece(gate, up, down)
    return pl.pallas_call(
        expert_forward_kernel,
        out_shape=(
            jax.ShapeDtypeStruct((count, width), jnp.bfloat16),
            jax.ShapeDtypeStruct((4, count, hidden), jnp.float32),
            jax.ShapeDtypeStruct((4, count, hidden), jnp.float32),
            jax.ShapeDtypeStruct((4, count, hidden), jnp.bfloat16),
        ),
        in_specs=vmem(1) + vmem(12),
        out_specs=tuple(vmem(4)),
        scratch_shapes=[pltpu.VMEM((count, width), jnp.float32)],
        compiler_params=kernel_params(),
        cost_estimate=cost(24 * count * width * hidden, 16 * 2**20, 4 * count * hidden),
        name="expert_forward",
    )(rows, *weights)


def expert_backward_kernel(grad_ref, *refs):
    weights, (gates, ups, back_ref, grad_gate_ref, grad_up_ref, total) = refs[2:14], refs[:2] + refs[14:]
    grads = grad_ref[...]
    for m in range(4):
        grad_inner = times(grads, weights[3 * m + 2][...], 1, 1)
        grad_gate, grad_up = pair_back(grad_inner, gates[m], ups[m])
        grad_gate_ref[m] = grad_gate
        grad_up_ref[m] = grad_up
        part = times(grad_gate, weights[3 * m][...], 1, 1) + times(grad_up, weights[3 * m + 1][...], 1, 1)
        if m == 0:
            total[...] = part
        elif m < 3:
            total[...] += part
        else:
            back_ref[...] = (total[...] + part).astype(jnp.bfloat16)


def expert_backward(grads, gate, up, down, gates, ups):
    count, width = grads.shape
    hidden = gate[0].shape[1]
    weights = [gates, ups] + by_piece(gate, up, down)
    return pl.pallas_call(
        expert_backward_kernel,
        out_shape=(
            jax.ShapeDtypeStruct((count, width), jnp.bfloat16),
            jax.ShapeDtypeStruct((4, count, hidden), jnp.bfloat16),
            jax.ShapeDtypeStruct((4, count, hidden), jnp.bfloat16),
        ),
        in_specs=vmem(1) + vmem(14),
        out_specs=tuple(vmem(3)),
        scratch_shapes=[pltpu.VMEM((count, width), jnp.float32)],
        compiler_params=kernel_params(),
        cost_estimate=cost(24 * count * width * hidden, 16 * 2**20, 4 * count * hidden),
        name="expert_backward",
    )(grads, *weights)


def expert_both_kernel(experts, mine_ref, rows_ref, cot_ref, router_ref, *refs):
    weights, outs = refs[:12], refs[12:]
    made_ref, back_ref, grad_ref, inner_ref, grad_gate_ref, grad_up_ref, total, total_back = outs
    rows = rows_ref[...]
    count, width = rows.shape
    cot = cot_ref[:, :width].astype(jnp.float32)
    logits = times(rows, router_ref[...], 1, 1)
    ids = lax.broadcasted_iota(jnp.int32, logits.shape, 1)
    logits = jnp.where(ids < experts, logits, NEG)
    odds = jnp.exp(logits - jnp.max(logits, axis=1, keepdims=True))
    other = cot_ref[:, width : width + 1].astype(jnp.float32).astype(jnp.int32)
    own_odds = jnp.sum(jnp.where(ids == mine_ref[0], odds, 0.0), axis=1, keepdims=True)
    other_odds = jnp.sum(jnp.where(ids == other, odds, 0.0), axis=1, keepdims=True)
    grad_ref[...] = (own_odds / (own_odds + other_odds) * cot).astype(jnp.bfloat16)
    grads = grad_ref[...]
    for m in range(4):
        gate, up = weights[3 * m], weights[3 * m + 1]
        gate_value = times(rows, gate[...], 1, 0)
        up_value = times(rows, up[...], 1, 0)
        inner = silu_pair(gate_value, up_value)
        inner_ref[m] = inner
        down = weights[3 * m + 2]
        grad_gate, grad_up = pair_back(times(grads, down[...], 1, 1), gate_value, up_value)
        grad_gate_ref[m] = grad_gate
        grad_up_ref[m] = grad_up
        part = times(inner, down[...], 1, 0)
        part_back = times(grad_gate, gate[...], 1, 1) + times(grad_up, up[...], 1, 1)
        total[...] = part if m == 0 else total[...] + part
        total_back[...] = part_back if m == 0 else total_back[...] + part_back
    made = total[...].astype(jnp.bfloat16)
    made_ref[...] = made
    back_ref[:, :width] = total_back[...].astype(jnp.bfloat16)
    signal = jnp.sum(cot * made.astype(jnp.float32), axis=1, keepdims=True)
    high = signal.astype(jnp.bfloat16)
    low = (signal - high.astype(jnp.float32)).astype(jnp.bfloat16)
    at = lax.broadcasted_iota(jnp.int32, (count, back_ref.shape[1] - width), 1)
    back_ref[:, width:] = jnp.where(
        at == 0, high.astype(jnp.float32), jnp.where(at == 1, low.astype(jnp.float32), 0.0)
    ).astype(jnp.bfloat16)


def expert_both(experts, mine, rows, cot, router, gate, up, down):
    count, width = rows.shape
    hidden = gate[0].shape[1]
    weights = by_piece(gate, up, down)
    return pl.pallas_call(
        functools.partial(expert_both_kernel, experts),
        out_shape=(
            jax.ShapeDtypeStruct((count, width), jnp.bfloat16),
            jax.ShapeDtypeStruct(cot.shape, jnp.bfloat16),
            jax.ShapeDtypeStruct((count, width), jnp.bfloat16),
            jax.ShapeDtypeStruct((4, count, hidden), jnp.bfloat16),
            jax.ShapeDtypeStruct((4, count, hidden), jnp.bfloat16),
            jax.ShapeDtypeStruct((4, count, hidden), jnp.bfloat16),
        ),
        in_specs=[pl.BlockSpec(memory_space=pltpu.SMEM)] + vmem(3) + vmem(12),
        out_specs=tuple(vmem(6)),
        scratch_shapes=[pltpu.VMEM((count, width), jnp.float32)] * 2,
        compiler_params=kernel_params(),
        cost_estimate=cost(48 * count * width * hidden, 18 * 2**20, 8 * count * hidden),
        name="expert_both",
    )(mine, rows, cot, router, *weights)


def expert_grads_kernel(rows_ref, grad_ref, inner_ref, grad_gate_ref, grad_up_ref, pair_give, far_give, pair_own, pair_far, down_give, down_own, down_far):
    for m, (pairs, at, downs, down_at) in enumerate(
        (
            (pair_own, 0, down_own, 0),
            (pair_give, 0, down_give, 0),
            (pair_far, 0, down_far, 0),
            (far_give, 0, down_give, 1),
        )
    ):
        pairs[at] = times(rows_ref[...], grad_gate_ref[m], 0, 0).astype(jnp.bfloat16)
        pairs[at + 1] = times(rows_ref[...], grad_up_ref[m], 0, 0).astype(jnp.bfloat16)
        downs[down_at] = times(inner_ref[m], grad_ref[...], 0, 0).astype(jnp.bfloat16)


def expert_grads(rows, grads, inner, grad_gate, grad_up):
    count, width = rows.shape
    hidden = inner.shape[2]
    shapes = [(2, width, hidden)] * 4
    shapes += [(2, hidden, width), (1, hidden, width), (1, hidden, width)]
    return pl.pallas_call(
        expert_grads_kernel,
        out_shape=tuple(jax.ShapeDtypeStruct(shape, jnp.bfloat16) for shape in shapes),
        in_specs=vmem(5),
        out_specs=tuple(vmem(7)),
        compiler_params=kernel_params(),
        cost_estimate=cost(24 * count * width * hidden, 14 * 2**20),
        name="expert_grads",
    )(rows, grads, inner, grad_gate, grad_up)


def head_grads_kernel(part, at_ref, normed_ref, whole_ref, small_ref, give_ref, own_ref, far_ref):
    tokens = whole_ref.shape[1]
    deep = whole_ref.shape[0]
    for m, (ref, slot) in enumerate(((own_ref, 0), (give_ref, 0), (far_ref, 0), (give_ref, 1))):
        lanes = pl.ds(pl.multiple_of(at_ref[m] * part, 128), part)
        rows = normed_ref[:, :, lanes].reshape(tokens, part)
        ref[slot, :deep, :] = times(whole_ref[...], rows, 1, 0).astype(jnp.bfloat16)
        ref[slot, deep:, :] = small_ref[:, lanes].astype(jnp.bfloat16)


def head_grads(at, normed, whole, small):
    deep, tokens = whole.shape
    width = normed.shape[2]
    part = width // 4
    full = deep + small.shape[0]
    return pl.pallas_call(
        functools.partial(head_grads_kernel, part),
        out_shape=tuple(jax.ShapeDtypeStruct((n, full, part), jnp.bfloat16) for n in (2, 1, 1)),
        in_specs=[pl.BlockSpec(memory_space=pltpu.SMEM)] + vmem(3),
        out_specs=tuple(vmem(3)),
        compiler_params=kernel_params(),
        cost_estimate=cost(2**20, 2**16),
        name="head_grads",
    )(at, normed, whole, small)


def spread_kernel(wide, head, ringed, *refs):
    if ringed:
        spot_ref, *blocks, query_ref, key_ref, value_ref = refs[: ringed + 4]
        gathered_ref = refs[-1]
        outs = refs[-7:-1]
        for k, block in enumerate(blocks[:-2]):
            gathered_ref[spot_ref[k]] = block[...]
        half = blocks[-2].shape[0]
        gathered_ref[spot_ref[ringed - 2], :half, :] = blocks[-2][...]
        gathered_ref[spot_ref[ringed - 2], half:, :] = blocks[-1][...]
    else:
        gathered_ref, query_ref, key_ref, value_ref = refs[:4]
        outs = refs[-6:]
    query_out, key_out, value_out, out_out, small_out, sum_ref = outs
    count, _, part = gathered_ref.shape
    deep = wide + 2 * head
    small = small_out.shape[0]
    sums = jnp.zeros((part, 1), jnp.float32)
    for i in range(count // 2):
        block = gathered_ref[2 * i : 2 * i + 2, :wide, :].astype(jnp.float32).reshape(2 * wide, part).T
        lanes = slice(2 * i * wide, 2 * (i + 1) * wide)
        query_out[0, :, lanes] = block
        sums += jnp.sum(block * query_ref[:, lanes].astype(jnp.float32), axis=1, keepdims=True)
    for start, weight_ref, out in ((wide, key_ref, key_out), (wide + head, value_ref, value_out)):
        block = gathered_ref[:, start : start + head, :].astype(jnp.float32).reshape(count * head, part).T
        out[0] = block
        sums += jnp.sum(block * weight_ref[...].astype(jnp.float32), axis=1, keepdims=True)
    sum_ref[...] = sums
    total = gathered_ref[0, deep : deep + small, :].astype(jnp.float32)
    for c in range(1, count):
        total += gathered_ref[c, deep : deep + small, :].astype(jnp.float32)
    small_out[...] = total
    rows = part // count
    for c in range(count):
        for j in range(out_out.shape[2] // part):
            piece = gathered_ref[c, deep + small + j * rows : deep + small + (j + 1) * rows, :]
            out_out[0, c * rows : (c + 1) * rows, j * part : (j + 1) * part] = piece.astype(jnp.float32)


def spread(layer, layers, spots, sources, weights, wide, head, small, before):
    ringed = len(sources) if spots is not None else 0
    part = weights[0].shape[0]
    width = weights[0].shape[1]
    count = width // wide
    shapes = [(layers,) + weight.shape for weight in weights] + [(layers, part, width)]
    aliased = [] if before is None else list(before)
    one = lambda shape: pl.BlockSpec((1,) + shape[1:], lambda i: (layer, 0, 0))
    whole = lambda shape: pl.BlockSpec(shape, lambda i: (0,) * len(shape))
    deep = sources[0].shape[-2]
    lead = [spots] if ringed else []
    return pl.pallas_call(
        functools.partial(spread_kernel, wide, head, ringed),
        grid=(1,),
        out_shape=tuple(jax.ShapeDtypeStruct(shape, jnp.float32) for shape in shapes)
        + (jax.ShapeDtypeStruct((small, part), jnp.float32), jax.ShapeDtypeStruct((part, 1), jnp.float32)),
        in_specs=[pl.BlockSpec(memory_space=pltpu.SMEM)] * len(lead)
        + [whole(source.shape) for source in sources]
        + [whole(weight.shape) for weight in weights]
        + [pl.BlockSpec(memory_space=pl.ANY)] * len(aliased),
        out_specs=tuple(one(shape) for shape in shapes) + (whole((small, part)), whole((part, 1))),
        scratch_shapes=[pltpu.VMEM((count, deep, part), jnp.bfloat16)] if ringed else [],
        input_output_aliases={len(lead) + len(sources) + 3 + i: i for i in range(len(aliased))},
        compiler_params=kernel_params(),
        cost_estimate=cost(2**20, 2**16),
        name="spread",
    )(*lead, *sources, *weights, *aliased)


def finish_kernel(*refs):
    own_ref, near_ref = refs[:2]
    count = own_ref.shape[0]
    for i, (far_ref, out) in enumerate(zip(refs[2 : 2 + count], refs[-count:])):
        total = own_ref[i].astype(jnp.float32) + near_ref[i].astype(jnp.float32) + far_ref[...].astype(jnp.float32)
        out[0, 0] = total


def finish(layer, layers, own, near, far, before):
    count, rows, columns = own.shape
    steps = 2
    block = rows // steps
    aliased = [] if before is None else list(before)
    taken = pl.BlockSpec((count, block, columns), lambda i: (0, i, 0))
    made = pl.BlockSpec((1, 1, block, columns), lambda i: (layer, 0, i, 0))
    return pl.pallas_call(
        finish_kernel,
        grid=(steps,),
        out_shape=tuple(jax.ShapeDtypeStruct((layers, 1, rows, columns), jnp.float32) for _ in range(count)),
        in_specs=[taken] * 2
        + [pl.BlockSpec((block, columns), lambda i: (i, 0))] * count
        + [pl.BlockSpec(memory_space=pl.ANY)] * len(aliased),
        out_specs=(made,) * count,
        input_output_aliases={2 + count + i: i for i in range(len(aliased))},
        compiler_params=kernel_params(),
        cost_estimate=cost(2**20, 2**16),
        name="finish",
    )(own, near, *far, *aliased)


def head_rows_kernel(wide, head, at_ref, query_ref, key_ref, value_ref, small_ref, out_ref):
    odd = at_ref[0] % 2
    top = 0
    for ref, size in ((query_ref, wide), (key_ref, head), (value_ref, head)):
        turned = ref[0].astype(jnp.float32).T
        out_ref[0, top : top + size, :] = jnp.where(odd == 1, turned[size:], turned[:size]).astype(jnp.bfloat16)
        top += size
    out_ref[0, top:, :] = small_ref[0]


def head_rows(mine, query_weight, key_weight, value_weight, small, wide, head):
    layers, part, _ = query_weight.shape
    rows = wide + 2 * head + small.shape[1]
    taken = lambda size: pl.BlockSpec((1, part, 2 * size), lambda i, at: (i, 0, at[0] // 2))
    return pl.pallas_call(
        functools.partial(head_rows_kernel, wide, head),
        grid_spec=pltpu.PrefetchScalarGridSpec(
            num_scalar_prefetch=1,
            grid=(layers,),
            in_specs=[taken(wide), taken(head), taken(head), pl.BlockSpec((1,) + small.shape[1:], lambda i, at: (i, 0, 0))],
            out_specs=pl.BlockSpec((1, rows, part), lambda i, at: (i, 0, 0)),
        ),
        out_shape=jax.ShapeDtypeStruct((layers, rows, part), jnp.bfloat16),
        compiler_params=kernel_params(),
        cost_estimate=cost(2**20, 2**16),
        name="head_rows",
    )(mine, query_weight, key_weight, value_weight, small)


def middle_forward_kernel(at_ref, attended_ref, state_ref, gain_ref, place_ref, *refs):
    weights, (middle_ref, mixed_ref, out_ref) = refs[:4], refs[4:]
    part = weights[0].shape[0]
    total = state_ref[...]
    for m in range(4):
        rows = attended_ref[pl.ds(pl.multiple_of(at_ref[m] * part, 128), part), :]
        total = total + times(rows, weights[m][...], 0, 0)
    middle_ref[...] = total
    mixed = rms_scale(total, gain_ref[...]).astype(jnp.bfloat16)
    mixed_ref[...] = mixed
    out_ref[...] = times(place_ref[0] + place_ref[1], mixed, 0, 0).astype(jnp.bfloat16)


def middle_forward(at, attended, pieces, state, gain, place):
    rows, width = state.shape
    slots = place.shape[2]
    return pl.pallas_call(
        middle_forward_kernel,
        out_shape=(
            jax.ShapeDtypeStruct((rows, width), jnp.float32),
            jax.ShapeDtypeStruct((rows, width), jnp.bfloat16),
            jax.ShapeDtypeStruct((slots, width), jnp.bfloat16),
        ),
        in_specs=[pl.BlockSpec(memory_space=pltpu.SMEM)] + vmem(4) + vmem(4),
        out_specs=tuple(vmem(3)),
        compiler_params=kernel_params(),
        cost_estimate=cost(2 * rows * width * (width + slots), 9 * 2**20),
        name="middle_forward",
    )(at, attended, state, gain, place, *pieces)


def middle_back_kernel(experts, at_ref, place_ref, back_ref, upstream_ref, middle_ref, mixed_ref, gain_ref, router_ref, chosen_ref, *refs):
    *results, w0, w1, w2, w3, grad_ref, low_ref, heads_ref, small_ref = refs
    weights = (w0, w1, w2, w3)
    rows, width = upstream_ref.shape
    part = w0.shape[0]
    upstream, mixed, router = upstream_ref[...], mixed_ref[...], router_ref[...]
    logits = times(mixed, router, 1, 1)
    ids = lax.broadcasted_iota(jnp.int32, logits.shape, 1)
    logits = jnp.where(ids < experts, logits, NEG)
    odds = jnp.exp(logits - jnp.max(logits, axis=1, keepdims=True))
    probs = odds / jnp.sum(odds, axis=1, keepdims=True)
    hits = [ids == chosen_ref[:, c : c + 1] for c in range(2)]
    picked = [jnp.sum(jnp.where(hit, probs, 0.0), axis=1, keepdims=True) for hit in hits]
    pair_total = picked[0] + picked[1]
    if results:
        signal = [jnp.sum(upstream * r[...].astype(jnp.float32), axis=1, keepdims=True) for r in results]
    else:
        signal = [jnp.sum(times(place_ref[c], back_ref[:, width:], 1, 0), axis=1, keepdims=True) for c in range(2)]
    mean = (picked[0] * signal[0] + picked[1] * signal[1]) / pair_total
    slopes = [(s - mean) / pair_total for s in signal]
    grad_probs = jnp.where(hits[0], slopes[0], 0.0) + jnp.where(hits[1], slopes[1], 0.0)
    grad_logits = probs * (grad_probs - jnp.sum(probs * grad_probs, axis=1, keepdims=True))
    high = grad_logits.astype(jnp.bfloat16)
    rest = (grad_logits - high.astype(jnp.float32)).astype(jnp.bfloat16)
    small_ref[...] = jnp.zeros_like(small_ref)
    router_part = times(high, mixed, 0, 0) + times(rest, mixed, 0, 0)
    small_ref[:experts, :] = router_part[:experts]
    grad_mixed = times(place_ref[0] + place_ref[1], back_ref[:, :width], 1, 0)
    grad_mixed = grad_mixed + times(high, router, 1, 0) + times(rest, router, 1, 0)
    pulled, gain_rows = rms_back(middle_ref[...], gain_ref[...], grad_mixed)
    small_ref[experts : experts + 1, :] = jnp.sum(gain_rows, axis=0, keepdims=True)
    grad = upstream + pulled
    grad_ref[...] = grad
    low = grad.astype(jnp.bfloat16)
    low_ref[...] = low
    for m in range(4):
        lanes = pl.ds(pl.multiple_of(at_ref[m] * part, 128), part)
        heads_ref[lanes, :] = times(weights[m][...], low, 1, 1).astype(jnp.bfloat16)


def middle_back(experts, at, place, back, upstream, middle, mixed, gain, router, chosen, results, pieces):
    rows, width = upstream.shape
    slots = place.shape[2]
    return pl.pallas_call(
        functools.partial(middle_back_kernel, experts),
        out_shape=(
            jax.ShapeDtypeStruct((rows, width), jnp.float32),
            jax.ShapeDtypeStruct((rows, width), jnp.bfloat16),
            jax.ShapeDtypeStruct((width, rows), jnp.bfloat16),
            jax.ShapeDtypeStruct((experts + 8, width), jnp.float32),
        ),
        in_specs=[pl.BlockSpec(memory_space=pltpu.SMEM)] + vmem(8 + len(results)) + vmem(4),
        out_specs=tuple(vmem(4)),
        compiler_params=kernel_params(),
        cost_estimate=cost(2 * rows * width * (width + slots), 10 * 2**20),
        name="middle_back",
    )(at, place, back, upstream, middle, mixed, gain, router, chosen, *results, *pieces)


def swap(x, mask):
    return lax.ppermute(x, "wt", [(i, i ^ mask) for i in range(4)])


def near_finish(far, own):
    return (own, swap(own, 1), far, swap(far, 1))


def wt_gather(own):
    return near_finish(swap(own, 2), own)


def wt_exchange(slices, me):
    def cut(m):
        return lax.dynamic_index_in_dim(slices, me ^ m, 0, keepdims=False)

    far = swap(jnp.stack([cut(2), cut(3)]), 2)
    near = swap(jnp.stack([cut(1), far[1]]), 1)
    return (cut(0), near[0], far[0], near[1])


def in_order(pieces, me, axis):
    own, near, far, last = pieces
    odd, high = me % 2 == 1, me >= 2
    low = (jnp.where(odd, near, own), jnp.where(odd, own, near))
    up = (jnp.where(odd, last, far), jnp.where(odd, far, last))
    first = [jnp.where(high, b, a) for a, b in zip(low, up)]
    second = [jnp.where(high, a, b) for a, b in zip(low, up)]
    return jnp.concatenate(first + second, axis=axis)


def tie(*arrays):
    return lax.optimization_barrier(arrays)


def ring_of(count):
    ring = list(range(0, count, 2)) + list(range(count - 1, 0, -2))
    offsets = [0] + [sign * step for step in range(1, count // 2) for sign in (-1, 1)] + [count // 2]
    table = [[ring[(ring.index(i) + k) % count] for k in offsets] for i in range(count)]
    return ring, jnp.asarray(table, jnp.int32)


def ring_start(x, ring):
    right = [(a, b) for a, b in zip(ring, ring[1:] + ring[:1])]
    left = [(b, a) for a, b in right]
    return lax.ppermute(x, "ctx", right), lax.ppermute(x, "ctx", left)


def ring_blocks(x, first, ring, early=None):
    count = len(ring)
    right = [(a, b) for a, b in zip(ring, ring[1:] + ring[:1])]
    left = [(b, a) for a, b in right]
    ahead, behind = first
    blocks = [x, ahead, behind]
    for _ in range(2, count // 2):
        ahead, behind = lax.ppermute(ahead, "ctx", right), lax.ppermute(behind, "ctx", left)
        blocks += [ahead, behind]
    if early is not None:
        ahead, behind, *early = tie(ahead, behind, *early)
    half = x.shape[0] // 2
    blocks += [lax.ppermute(ahead[:half], "ctx", right), lax.ppermute(behind[half:], "ctx", left)]
    return blocks if early is None else (blocks, early)


def all_to_all(x):
    return lax.all_to_all(x, "ctx", split_axis=0, concat_axis=0, tiled=True)


def rms_back(rows, gain, grad):
    scale = lax.rsqrt(jnp.mean(rows * rows, axis=-1, keepdims=True) + EPS)
    unit = rows * scale
    pulled = grad * gain
    return scale * (pulled - unit * jnp.mean(pulled * unit, axis=-1, keepdims=True)), grad * unit


def by_heads(mesh, tokens, cotangent, seq_lengths, block_deal, *rest):
    return (
        mesh.shape["ctx"] == KV_HEADS
        and mesh.shape["wt"] == 4
        and seq_lengths.shape[1] == 1
        and block_deal.shape[2] == 1
        and tokens.shape[1] == BLK
    )


def local_heads(
    mesh,
    tokens,
    cotangent,
    seq_lengths,
    block_deal,
    routes,
    attention_gain,
    query_weight,
    key_weight,
    value_weight,
    out_weight,
    mixture_gain,
    router_weight,
    gate_weight,
    up_weight,
    down_weight,
):
    n_ctx = mesh.shape["ctx"]
    rows = tokens.shape[1]
    width = tokens.shape[2]
    layers = query_weight.shape[0]
    experts = router_weight.shape[2]
    capacity = 3 * rows // experts
    slot_count = experts * capacity
    rep = HEADS // KV_HEADS
    wide = rep * HEAD
    lanes = wide + 2 * HEAD
    part = width // 4
    ctx = lax.axis_index("ctx")
    mine = ctx.astype(jnp.int32).reshape(1)
    wt = lax.axis_index("wt").astype(jnp.uint32)
    others = (wt ^ jnp.arange(4, dtype=jnp.uint32)).astype(jnp.int32)
    table = block_deal[0, :, 0]
    devices = jnp.arange(n_ctx, dtype=jnp.int32)
    owner_of = jnp.sum(jnp.where(table[None, :] == devices[:, None], devices[None, :], 0), axis=1)
    ring, ring_table = ring_of(n_ctx)
    ring_owners = lax.dynamic_index_in_dim(ring_table, ctx.astype(jnp.uint32), 0, keepdims=False)
    spots = jnp.sum(jnp.where(ring_owners[:, None] == devices[None, :], table[None, :], 0), axis=1)

    first = ring_start(tokens[0], ring)

    expert_ids = jnp.arange(experts, dtype=jnp.int32)
    chosen = routes[:, 0]
    flat = chosen.reshape(layers, 2 * rows)
    onehot = flat[:, :, None] == expert_ids
    earlier = jnp.tril(jnp.ones((2 * rows, 2 * rows), jnp.bfloat16), -1)
    rank = jnp.einsum("ij,lje->lie", earlier, onehot.astype(jnp.bfloat16), preferred_element_type=jnp.float32)
    rank = jnp.sum(jnp.where(onehot, rank, 0.0), axis=2).astype(jnp.int32)
    slots = (flat * capacity + rank).reshape(layers, rows, 2).transpose(0, 2, 1)
    place = (slots[..., None] == jnp.arange(slot_count, dtype=jnp.int32)).astype(jnp.bfloat16)
    named = (chosen.transpose(0, 2, 1)[..., None] == expert_ids).astype(jnp.float32)

    small_rows = jnp.concatenate(
        [
            router_weight.transpose(0, 2, 1),
            attention_gain[:, None],
            mixture_gain[:, None],
            jnp.zeros((layers, 14 - experts, part), jnp.bfloat16),
        ],
        axis=1,
    )
    deep = lanes + 16
    head_own = head_rows(mine, query_weight, key_weight, value_weight, small_rows, wide, HEAD)
    head_own = head_own.reshape(layers * deep, part)
    head_far = swap(head_own, 2)

    out_own = list(out_weight)
    gate_own = [gate_weight[layer, 0] for layer in range(layers)]
    up_own = [up_weight[layer, 0] for layer in range(layers)]
    down_own = [down_weight[layer, 0] for layer in range(layers)]
    query_own = list(query_weight)
    pair_own_weights = [jnp.concatenate([key_weight[layer], value_weight[layer]], axis=1) for layer in range(layers)]
    out_far, gate_far, up_far, down_far, query_far, key_far = [
        [swap(own, 2) for own in group]
        for group in (out_own, gate_own, up_own, down_own, query_own, pair_own_weights)
    ]

    last = layers - 1
    other = chosen[last].transpose(1, 0)[::-1, :, None].astype(jnp.bfloat16)
    cot_rows = jnp.concatenate(
        [jnp.broadcast_to(cotangent[0][None], (2, rows, width)), jnp.broadcast_to(other, (2, rows, 128))], axis=2
    ).reshape(2 * rows, width + 128)
    cot_out = times(place[last].reshape(2 * rows, slot_count), cot_rows, 0, 0).astype(jnp.bfloat16)

    state = tokens[0].astype(jnp.float32)
    saved = []
    for layer in range(layers):
        if layer == 0:
            blocks, head_pieces = ring_blocks(tokens[0], first, ring, near_finish(head_far, head_own))
            small_all = [
                in_order([piece[i * deep + lanes : (i + 1) * deep] for piece in head_pieces], wt, 1)
                for i in range(layers)
            ]
            cot_out = tie(cot_out, *blocks[-2:])[0]
            cot_slots = all_to_all(cot_out.reshape(experts, capacity, width + 128)).reshape(slot_count, width + 128)
        router = jnp.concatenate([small_all[layer][:experts], jnp.zeros((128 - experts, width), jnp.bfloat16)])
        gain_one = small_all[layer][experts : experts + 1].astype(jnp.float32)
        gain_two = small_all[layer][experts + 1 : experts + 2].astype(jnp.float32)
        if layer > 0:
            normed = rms_scale(state, gain_one).astype(jnp.bfloat16)
            blocks = ring_blocks(normed, ring_start(normed, ring), ring)
        normed_all, qkv, sent, exact, log_total = front(
            layer == 0, spots, owner_of, others, blocks, gain_one, head_pieces, layer * deep, rep, HEAD
        )
        if layer == 0:
            sent, cot_slots = tie(sent, cot_slots)
        else:
            sent, out_far[layer], up_far[layer] = tie(sent, out_far[layer], up_far[layer])
        attended = all_to_all(sent).reshape(width, rows)
        if layer == 0:
            attended, out_far[layer] = tie(attended, out_far[layer])
        out_pieces = near_finish(out_far[layer], out_own[layer])
        middle, mixed, outgoing = middle_forward(others, attended, out_pieces, state, gain_two, place[layer])
        outgoing = outgoing.reshape(experts, capacity, width)
        if layer == 0:
            outgoing, gate_far[layer] = tie(outgoing, gate_far[layer])
        else:
            outgoing, down_far[layer], *saved[0]["attended"] = tie(outgoing, down_far[layer], *saved[0]["attended"])
            kept_exchange = wt_exchange(attended.reshape(4, part, rows), wt)
        arrived = all_to_all(outgoing).reshape(slot_count, width)
        if layer == 0:
            kept_exchange = wt_exchange(attended.reshape(4, part, rows), wt)
        else:
            arrived, query_far[layer] = tie(arrived, query_far[layer])
        probs = jax.nn.softmax(times(mixed, router[:experts], 1, 1), axis=-1)
        picked = jnp.sum(named[layer] * probs[None], axis=-1, keepdims=True)
        pair_total = picked[0] + picked[1]
        gates = picked / pair_total
        kept = dict(
            state=state,
            normed_all=normed_all,
            qkv=qkv,
            exact=exact,
            log_total=log_total,
            attended=kept_exchange,
            middle=middle,
            mixed=mixed,
            gates=gates,
            arrived=arrived,
            gain_one=gain_one,
            gain_two=gain_two,
            router=router,
            out_pieces=out_pieces,
        )
        pieces = [near_finish(far[layer], own[layer]) for far, own in ((gate_far, gate_own), (up_far, up_own), (down_far, down_own))]
        kept["pieces"] = pieces
        saved.append(kept)
        if layer == last:
            break
        made, kept["gate_values"], kept["up_values"], kept["inner"] = expert_forward(arrived, *pieces)
        returned = all_to_all(made.reshape(experts, capacity, width)).reshape(slot_count, width)
        returned, gate_far[last] = tie(returned, gate_far[last])
        results = [times(place[layer, choice], returned, 1, 0) for choice in range(2)]
        kept["results"] = [result.astype(jnp.bfloat16) for result in results]
        state = middle + gates[0] * results[0] + gates[1] * results[1]

    upstream = cotangent[0].astype(jnp.float32)
    expert_done, head_done, returned, sources = None, None, None, None
    merge = lambda head, out: jnp.concatenate([head] + [out[:, i * part : (i + 1) * part] for i in range(4)], axis=0)
    smalls, gain_sums = [None] * layers, [None] * layers
    block_output = None
    for layer in reversed(range(layers)):
        k = saved[layer]
        gates, pieces = k["gates"], k["pieces"]
        if layer == last:
            arrived = k["arrived"]
            made, back, arrived_grad, inner, grad_gate, grad_up = expert_both(
                experts, mine, arrived, cot_slots, k["router"], *pieces
            )
            back = all_to_all(back.reshape(experts, capacity, width + 128))
            back = back.reshape(slot_count, width + 128)
            results = []
        else:
            arrived, inner = k["arrived"], k["inner"]
            back_rows = (gates * upstream[None]).astype(jnp.bfloat16).reshape(2 * rows, width)
            outgoing = times(place[layer].reshape(2 * rows, slot_count), back_rows, 0, 0).astype(jnp.bfloat16)
            outgoing, returned, head_sum, query_far[layer] = tie(outgoing, returned, sources[0], query_far[layer])
            sources = [lax.all_gather(merge(head_sum, sources[1]), "ctx", axis=0)]
            arrived_grad = all_to_all(outgoing.reshape(experts, capacity, width)).reshape(slot_count, width)
            state = saved[last]["middle"] + sum(
                saved[last]["gates"][i] * times(place[last, i], returned, 1, 0) for i in range(2)
            )
            block_output = state.astype(jnp.bfloat16)[None]
            back, grad_gate, grad_up = expert_backward(arrived_grad, *pieces, k["gate_values"], k["up_values"])
            back, *last_parts[2:4] = tie(back, *last_parts[2:4])
            back = all_to_all(back.reshape(experts, capacity, width)).reshape(slot_count, width)
            results = k["results"]
        pair_give, far_give, pair_own, pair_far, down_give, down_kept, down_far_part = expert_grads(
            arrived, arrived_grad, inner, grad_gate, grad_up
        )
        pair_near, far_near, down_near = swap(pair_give, 1), swap(far_give, 1), swap(down_give, 1)
        add = lambda a, b: (a.astype(jnp.float32) + b.astype(jnp.float32)).astype(jnp.bfloat16)
        pair_sums = [add(pair_far[i], far_near[i]) for i in range(2)]
        down_sum = add(down_far_part, down_near[1:])
        if layer == last:
            back, key_far[layer] = tie(back, key_far[layer])
        else:
            back, last_parts[6] = tie(back, last_parts[6])
            pair_done, down_done = last_finish(*last_parts)
            expert_done = [*pair_done, *down_done]
        pair_last = [swap(pair_sum, 2) for pair_sum in pair_sums]
        if layer == last:
            down_last = [swap(down_sum[0], 2)]
        grad_middle, middle_low, grad_attended, small = middle_back(
            experts,
            others,
            place[layer],
            back,
            upstream,
            k["middle"],
            k["mixed"],
            k["gain_two"],
            k["router"],
            chosen[layer],
            results,
            k["out_pieces"],
        )
        grad_heads = all_to_all(grad_attended.reshape(n_ctx, wide, rows))
        if layer == last:
            grad_heads, *k["attended"] = tie(grad_heads, *k["attended"])
        grad_whole, grad_sent = attend_back(owner_of, k["qkv"], k["exact"], k["log_total"], grad_heads, rep, HEAD)
        middle_pieces = wt_gather(middle_low)
        out_part = times(jnp.concatenate(k["attended"], axis=1), jnp.concatenate(middle_pieces, axis=0), 1, 0)
        out_part = out_part.astype(jnp.bfloat16)
        if layer == 0:
            out_rows = all_to_all(out_part.reshape(n_ctx, part // n_ctx, width))
            grad_sent, out_rows, *expert_done = tie(grad_sent, out_rows, *expert_done)
        else:
            grad_sent, out_part = tie(grad_sent, out_part)
            out_rows = lax.psum_scatter(out_part, "ctx", scatter_dimension=0, tiled=True)
        grad_own = all_to_all(grad_sent)
        if layer == 0:
            grad_whole, *pair_last = tie(grad_whole, *pair_last)
        head_give, head_kept, head_far = head_grads(others, k["normed_all"], grad_whole, small)
        head_near = swap(head_give, 1)
        head_last = swap(add(head_far[0], head_near[1]), 2)
        head_sum = (
            head_kept[0].astype(jnp.float32) + head_near[0].astype(jnp.float32) + head_last.astype(jnp.float32)
        ).astype(jnp.bfloat16)
        weights = [(query_weight[i], key_weight[i], value_weight[i]) for i in range(layers)]
        columns = lambda at, *rest: spread(at, layers, *rest[:2], weights[at], wide, HEAD, 16, rest[2])
        if layer == last:
            sources = [head_sum, out_rows]
            last_parts = [pair_own, pair_near, *pair_last, down_kept, down_near, *down_last]
            last_finish = lambda *p: (finish(last, layers, *p[:2], p[2:4], None), finish(last, layers, *p[4:6], p[6:], None))
            made = tie(made, grad_own)[0]
            returned = all_to_all(made.reshape(experts, capacity, width)).reshape(slot_count, width)
        else:
            *head_done, smalls[last], gain_sums[last] = columns(last, None, sources, None)
            out_rows = jnp.sum(out_rows.astype(jnp.float32), axis=0).astype(jnp.bfloat16)
            merged = merge(head_sum, out_rows)
            merged, *head_done = tie(merged, *head_done)
            down_last = [swap(tie(down_sum, head_last)[0][0], 2)]
            sources = ring_blocks(merged, ring_start(merged, ring), ring)
            *sources[-2:], down_last[0] = tie(*sources[-2:], down_last[0])
            pair_done = finish(layer, layers, pair_own, pair_near, pair_last, expert_done[:2])
            down_done = finish(layer, layers, down_kept, down_near, down_last, expert_done[2:])
            expert_done = [*pair_done, *down_done]
            sources[-1], *expert_done = tie(sources[-1], *expert_done)
            *head_done, smalls[layer], gain_sums[layer] = columns(layer, ring_owners, sources, head_done)
        own_query = grad_own[:, :wide].reshape(width, rows)
        own_pair = jnp.concatenate(
            [
                grad_own[:, wide : wide + HEAD].reshape(n_ctx * HEAD, rows),
                grad_own[:, wide + HEAD :].reshape(n_ctx * HEAD, rows),
            ],
            axis=0,
        )
        query_pieces = near_finish(query_far[layer], query_own[layer])
        key_pieces = near_finish(key_far[layer], pair_own_weights[layer])
        grad_normed = jnp.zeros((rows, width), jnp.float32)
        for m in range(4):
            grad_normed = lax.dynamic_update_slice_in_dim(
                grad_normed,
                times(own_query, query_pieces[m], 0, 1) + times(own_pair, key_pieces[m], 0, 1),
                (wt ^ m) * part,
                1,
            )
        pulled, _ = rms_back(k["state"], k["gain_one"], grad_normed)
        upstream = grad_middle + pulled
    gain_one_grad = jnp.stack([s[:, 0] for s in gain_sums]) / attention_gain.astype(jnp.float32)
    small_grads = jnp.stack(smalls)
    query_grad, key_grad, value_grad, out_grad = head_done
    return (
        block_output,
        upstream[None],
        gain_one_grad,
        query_grad,
        key_grad,
        value_grad,
        out_grad,
        small_grads[:, experts],
        small_grads[:, :experts].transpose(0, 2, 1),
        *expert_done,
    )


def local_rows(
    tokens,
    cotangent,
    seq_lengths,
    block_deal,
    routes,
    attention_gain,
    query_weight,
    key_weight,
    value_weight,
    out_weight,
    mixture_gain,
    router_weight,
    gate_weight,
    up_weight,
    down_weight,
):
    rows_here = tokens.shape[1]
    width = tokens.shape[2]
    layers = query_weight.shape[0]
    experts = router_weight.shape[2]
    capacity = 3 * rows_here // experts
    kv_groups = KV_HEADS
    per_group = HEADS // KV_HEADS
    head_size = HEAD
    kv_width = kv_groups * head_size
    scale = head_size ** (-0.5)
    device = lax.axis_index("ctx")
    everywhere = stream_positions(block_deal[0], BLK)
    every_seq = sequence_ids(everywhere, seq_lengths[0])
    own_pos = lax.dynamic_slice_in_dim(everywhere, device * rows_here, rows_here, 0)
    own_seq = lax.dynamic_slice_in_dim(every_seq, device * rows_here, rows_here, 0)
    choice_rows = jnp.arange(2 * rows_here, dtype=jnp.int32) // 2
    expert_ids = jnp.arange(experts, dtype=jnp.int32)

    def block_mask(start, count):
        key_pos = lax.dynamic_slice_in_dim(everywhere, start, count, 0)
        key_seq = lax.dynamic_slice_in_dim(every_seq, start, count, 0)
        return (own_seq[:, None] == key_seq[None, :]) & (key_pos[None, :] <= own_pos[:, None])

    hidden_state = tokens[0].astype(jnp.float32)
    saved = []
    for layer in range(layers):
        shared = (
            lax.all_gather(attention_gain[layer], "wt", axis=0, tiled=True),
            lax.all_gather(query_weight[layer], "wt", axis=0, tiled=True),
            lax.all_gather(key_weight[layer], "wt", axis=0, tiled=True),
            lax.all_gather(value_weight[layer], "wt", axis=0, tiled=True),
            lax.all_gather(out_weight[layer], "wt", axis=0, tiled=True),
            lax.all_gather(mixture_gain[layer], "wt", axis=0, tiled=True),
            lax.all_gather(router_weight[layer], "wt", axis=0, tiled=True),
        )
        gain_one, full_query, full_key, full_value, full_out, gain_two, full_router = shared
        normed = rms_scale(hidden_state, gain_one.astype(jnp.float32)).astype(jnp.bfloat16)
        queries = jnp.dot(normed, full_query, preferred_element_type=jnp.float32).astype(
            jnp.bfloat16
        )
        keys = jnp.dot(normed, full_key, preferred_element_type=jnp.float32).astype(jnp.bfloat16)
        values = jnp.dot(normed, full_value, preferred_element_type=jnp.float32).astype(
            jnp.bfloat16
        )
        query_heads = queries.reshape(rows_here, kv_groups, per_group, head_size)
        start_state = (
            jnp.full((kv_groups, per_group, rows_here), NEG, jnp.float32),
            jnp.zeros((kv_groups, per_group, rows_here), jnp.float32),
            jnp.zeros((kv_groups, per_group, rows_here, head_size), jnp.float32),
        )
        gathered = None
        key_piece = lax.all_gather(keys, "ctx", axis=0, tiled=True)
        value_piece = lax.all_gather(values, "ctx", axis=0, tiled=True)
        absorb_count = key_piece.shape[0]
        absorb_span = 512

        def turn(index, state):
            first = index * absorb_span
            key_block = lax.dynamic_slice_in_dim(key_piece, first, absorb_span, 0).reshape(
                absorb_span, kv_groups, head_size
            )
            value_block = lax.dynamic_slice_in_dim(value_piece, first, absorb_span, 0).reshape(
                absorb_span, kv_groups, head_size
            )
            allowed = block_mask(first, absorb_span)

            def work(state):
                top, total, summed = state
                scores = (
                    jnp.einsum(
                        "tgrd,kgd->grtk", query_heads, key_block, preferred_element_type=jnp.float32
                    )
                    * scale
                )
                scores = jnp.where(allowed[None, None], scores, NEG)
                top_new = jnp.maximum(top, jnp.max(scores, axis=-1))
                fade = jnp.exp(top - top_new)
                weights = jnp.where(allowed[None, None], jnp.exp(scores - top_new[..., None]), 0.0)
                total = total * fade + jnp.sum(weights, axis=-1)
                summed = summed * fade[..., None] + jnp.einsum(
                    "grtk,kgd->grtd",
                    weights.astype(jnp.bfloat16),
                    value_block,
                    preferred_element_type=jnp.float32,
                )
                return (top_new, total, summed)

            return lax.cond(jnp.any(allowed), work, unchanged, state)

        top, total, summed = lax.fori_loop(0, absorb_count // absorb_span, turn, start_state)
        attended = (summed / total[..., None]).transpose(2, 0, 1, 3).reshape(rows_here, width)
        log_total = top + jnp.log(total)
        attended_low = attended.astype(jnp.bfloat16)
        middle = hidden_state + jnp.dot(attended_low, full_out, preferred_element_type=jnp.float32)
        mixed_low = rms_scale(middle, gain_two.astype(jnp.float32)).astype(jnp.bfloat16)
        probs = jax.nn.softmax(
            jnp.dot(mixed_low, full_router, preferred_element_type=jnp.float32), axis=-1
        )
        chosen = routes[layer, 0]
        picked = jnp.take_along_axis(probs, chosen, axis=1)
        gates = picked / jnp.sum(picked, axis=1, keepdims=True)
        flat_choice = chosen.reshape(-1)
        onehot = (flat_choice[:, None] == expert_ids[None, :]).astype(jnp.int32)
        rank = jnp.sum((jnp.cumsum(onehot, axis=0) - onehot) * onehot, axis=1)
        slots = flat_choice * capacity + rank
        outgoing = (
            jnp.zeros((experts * capacity, width), jnp.bfloat16)
            .at[slots]
            .set(mixed_low[choice_rows])
            .reshape(experts, capacity, width)
        )
        arrived = lax.all_to_all(outgoing, "ctx", split_axis=0, concat_axis=0, tiled=True)
        expert_full = (
            lax.all_gather(gate_weight[layer, 0], "wt", axis=1, tiled=True),
            lax.all_gather(up_weight[layer, 0], "wt", axis=1, tiled=True),
            lax.all_gather(down_weight[layer, 0], "wt", axis=0, tiled=True),
        )
        gate_full, up_full, down_full = expert_full
        expert_rows = arrived.reshape(-1, width)
        gate_value = jnp.dot(expert_rows, gate_full, preferred_element_type=jnp.float32)
        up_value = jnp.dot(expert_rows, up_full, preferred_element_type=jnp.float32)
        inner = (jax.nn.silu(gate_value) * up_value).astype(jnp.bfloat16)
        produced = (
            jnp.dot(inner, down_full, preferred_element_type=jnp.float32)
            .astype(jnp.bfloat16)
            .reshape(experts, capacity, width)
        )
        returned = lax.all_to_all(produced, "ctx", split_axis=0, concat_axis=0, tiled=True)
        expert_out = (
            returned.reshape(-1, width)[slots].reshape(rows_here, 2, width).astype(jnp.float32)
        )
        saved.append(
            (
                hidden_state,
                shared,
                normed,
                query_heads,
                keys,
                values,
                gathered,
                attended,
                attended_low,
                log_total,
                middle,
                mixed_low,
                probs,
                chosen,
                picked,
                gates,
                slots,
                expert_full,
                expert_rows,
                gate_value,
                up_value,
                inner,
                expert_out,
            )
        )
        hidden_state = middle + jnp.sum(gates[:, :, None] * expert_out, axis=1)
    block_output = hidden_state.astype(jnp.bfloat16)[None]
    upstream = cotangent[0].astype(jnp.float32)
    collected = []
    for layer in reversed(range(layers)):
        (
            layer_input,
            shared,
            normed,
            query_heads,
            keys,
            values,
            gathered,
            attended,
            attended_low,
            log_total,
            middle,
            mixed_low,
            probs,
            chosen,
            picked,
            gates,
            slots,
            expert_full,
            expert_rows,
            gate_value,
            up_value,
            inner,
            expert_out,
        ) = saved[layer]
        gain_one, full_query, full_key, full_value, full_out, gain_two, full_router = shared
        gate_full, up_full, down_full = expert_full
        gate_signal = jnp.sum(upstream[:, None, :] * expert_out, axis=-1)
        back_rows = (
            (gates[:, :, None] * upstream[:, None, :]).astype(jnp.bfloat16).reshape(-1, width)
        )
        outgoing_grad = (
            jnp.zeros((experts * capacity, width), jnp.bfloat16)
            .at[slots]
            .set(back_rows)
            .reshape(experts, capacity, width)
        )
        arrived_grad = lax.all_to_all(
            outgoing_grad, "ctx", split_axis=0, concat_axis=0, tiled=True
        ).reshape(-1, width)
        grad_down = outer_rows(inner, arrived_grad)
        grad_inner = times_transposed(arrived_grad, down_full)
        sigma = jax.nn.sigmoid(gate_value)
        grad_gate_value = (
            grad_inner * up_value * sigma * (1.0 + gate_value * (1.0 - sigma))
        ).astype(jnp.bfloat16)
        grad_up_value = (grad_inner * gate_value * sigma).astype(jnp.bfloat16)
        grad_gate = outer_rows(expert_rows, grad_gate_value)
        grad_up = outer_rows(expert_rows, grad_up_value)
        grad_rows = (
            (
                times_transposed(grad_gate_value, gate_full)
                + times_transposed(grad_up_value, up_full)
            )
            .astype(jnp.bfloat16)
            .reshape(experts, capacity, width)
        )
        back_grad = lax.all_to_all(grad_rows, "ctx", split_axis=0, concat_axis=0, tiled=True)
        grad_mixed = jnp.sum(
            back_grad.reshape(-1, width)[slots].reshape(rows_here, 2, width).astype(jnp.float32),
            axis=1,
        )
        pair_total = jnp.sum(picked, axis=1, keepdims=True)
        grad_picked = (
            gate_signal - jnp.sum(gates * gate_signal, axis=1, keepdims=True)
        ) / pair_total
        grad_probs = jnp.sum(
            grad_picked[:, :, None]
            * (chosen[:, :, None] == expert_ids[None, None, :]).astype(jnp.float32),
            axis=1,
        )
        grad_logits = probs * (grad_probs - jnp.sum(probs * grad_probs, axis=1, keepdims=True))
        grad_router = lax.dot_general(
            mixed_low.astype(jnp.float32),
            grad_logits,
            (((0,), (0,)), ((), ())),
            precision=lax.Precision.HIGHEST,
            preferred_element_type=jnp.float32,
        )
        grad_mixed = grad_mixed + lax.dot_general(
            grad_logits,
            full_router.astype(jnp.float32),
            (((1,), (1,)), ((), ())),
            precision=lax.Precision.HIGHEST,
            preferred_element_type=jnp.float32,
        )
        norm_value, pull_two = jax.vjp(rms_scale, middle, gain_two.astype(jnp.float32))
        grad_middle_norm, grad_gain_two = pull_two(grad_mixed)
        grad_middle = upstream + grad_middle_norm
        middle_low = grad_middle.astype(jnp.bfloat16)
        grad_out = outer_rows(attended_low, middle_low)
        grad_attended = times_transposed(middle_low, full_out).astype(jnp.bfloat16)
        grad_heads = grad_attended.reshape(rows_here, kv_groups, per_group, head_size)
        attended_heads = attended.reshape(rows_here, kv_groups, per_group, head_size)
        delta = jnp.sum(grad_heads.astype(jnp.float32) * attended_heads, axis=-1).transpose(1, 2, 0)
        whole = (
            lax.all_gather(keys, "ctx", axis=0, tiled=True),
            lax.all_gather(values, "ctx", axis=0, tiled=True),
        )
        key_all, value_all = whole
        total_rows = key_all.shape[0]
        span = 512

        def score_block(first, count, allowed):
            key_block = lax.dynamic_slice_in_dim(key_all, first, count, 0).reshape(
                count, kv_groups, head_size
            )
            value_block = lax.dynamic_slice_in_dim(value_all, first, count, 0).reshape(
                count, kv_groups, head_size
            )
            scores = (
                jnp.einsum(
                    "tgrd,kgd->grtk", query_heads, key_block, preferred_element_type=jnp.float32
                )
                * scale
            )
            probs_block = jnp.where(
                allowed[None, None], jnp.exp(scores - log_total[..., None]), 0.0
            )
            grad_probs_block = jnp.einsum(
                "tgrd,kgd->grtk", grad_heads, value_block, preferred_element_type=jnp.float32
            )
            grad_scores = (probs_block * (grad_probs_block - delta[..., None])).astype(jnp.bfloat16)
            return (key_block, probs_block, grad_scores)

        def key_terms(probs_block, grad_scores, count):
            key_part = (
                jnp.einsum(
                    "grtk,tgrd->kgd", grad_scores, query_heads, preferred_element_type=jnp.float32
                )
                * scale
            ).reshape(count, kv_width)
            value_part = jnp.einsum(
                "grtk,tgrd->kgd",
                probs_block.astype(jnp.bfloat16),
                grad_heads,
                preferred_element_type=jnp.float32,
            ).reshape(count, kv_width)
            return (key_part, value_part)

        query_start = jnp.zeros((rows_here, kv_groups, per_group, head_size), jnp.float32)

        def turn_back(index, state):
            first = index * span
            allowed = block_mask(first, span)

            def work(state):
                grad_query, grad_keys, grad_values = state
                key_block, probs_block, grad_scores = score_block(first, span, allowed)
                grad_query = (
                    grad_query
                    + jnp.einsum(
                        "grtk,kgd->tgrd", grad_scores, key_block, preferred_element_type=jnp.float32
                    )
                    * scale
                )
                key_part, value_part = key_terms(probs_block, grad_scores, span)
                grad_keys = lax.dynamic_update_slice_in_dim(grad_keys, key_part, first, 0)
                grad_values = lax.dynamic_update_slice_in_dim(grad_values, value_part, first, 0)
                return (grad_query, grad_keys, grad_values)

            return lax.cond(jnp.any(allowed), work, unchanged, state)

        back_start = (
            query_start,
            jnp.zeros((total_rows, kv_width), jnp.float32),
            jnp.zeros((total_rows, kv_width), jnp.float32),
        )
        grad_query, grad_keys, grad_values = lax.fori_loop(
            0, total_rows // span, turn_back, back_start
        )
        grad_keys, grad_values = (
            lax.psum_scatter(
                grad_keys.astype(jnp.bfloat16), "ctx", scatter_dimension=0, tiled=True
            ).astype(jnp.float32),
            lax.psum_scatter(
                grad_values.astype(jnp.bfloat16), "ctx", scatter_dimension=0, tiled=True
            ).astype(jnp.float32),
        )
        query_low = grad_query.reshape(rows_here, width).astype(jnp.bfloat16)
        key_low = grad_keys.astype(jnp.bfloat16)
        value_low = grad_values.astype(jnp.bfloat16)
        grad_query_weight = outer_rows(normed, query_low)
        grad_key_weight = outer_rows(normed, key_low)
        grad_value_weight = outer_rows(normed, value_low)
        grad_normed = (
            times_transposed(query_low, full_query)
            + times_transposed(key_low, full_key)
            + times_transposed(value_low, full_value)
        )
        norm_value, pull_one = jax.vjp(rms_scale, layer_input, gain_one.astype(jnp.float32))
        grad_input_norm, grad_gain_one = pull_one(grad_normed)
        upstream = grad_middle + grad_input_norm
        part_one, part_query, part_key, part_value, part_out, part_two, part_router = (
            lax.psum_scatter(
                grad_gain_one.astype(jnp.bfloat16), "wt", scatter_dimension=0, tiled=True
            ).astype(jnp.float32),
            lax.psum_scatter(
                grad_query_weight.astype(jnp.bfloat16), "wt", scatter_dimension=0, tiled=True
            ).astype(jnp.float32),
            lax.psum_scatter(
                grad_key_weight.astype(jnp.bfloat16), "wt", scatter_dimension=0, tiled=True
            ).astype(jnp.float32),
            lax.psum_scatter(
                grad_value_weight.astype(jnp.bfloat16), "wt", scatter_dimension=0, tiled=True
            ).astype(jnp.float32),
            lax.psum_scatter(
                grad_out.astype(jnp.bfloat16), "wt", scatter_dimension=0, tiled=True
            ).astype(jnp.float32),
            lax.psum_scatter(
                grad_gain_two.astype(jnp.bfloat16), "wt", scatter_dimension=0, tiled=True
            ).astype(jnp.float32),
            lax.psum_scatter(
                grad_router.astype(jnp.bfloat16), "wt", scatter_dimension=0, tiled=True
            ).astype(jnp.float32),
        )
        summed_parts = (
            lax.psum(part_one.astype(jnp.bfloat16), "ctx").astype(jnp.float32),
            lax.psum(part_query.astype(jnp.bfloat16), "ctx").astype(jnp.float32),
            lax.psum(part_key.astype(jnp.bfloat16), "ctx").astype(jnp.float32),
            lax.psum(part_value.astype(jnp.bfloat16), "ctx").astype(jnp.float32),
            lax.psum(part_out.astype(jnp.bfloat16), "ctx").astype(jnp.float32),
            lax.psum(part_two.astype(jnp.bfloat16), "ctx").astype(jnp.float32),
            lax.psum(part_router.astype(jnp.bfloat16), "ctx").astype(jnp.float32),
        )
        expert_parts = (
            lax.psum_scatter(
                grad_gate.astype(jnp.bfloat16), "wt", scatter_dimension=1, tiled=True
            ).astype(jnp.float32),
            lax.psum_scatter(
                grad_up.astype(jnp.bfloat16), "wt", scatter_dimension=1, tiled=True
            ).astype(jnp.float32),
            lax.psum_scatter(
                grad_down.astype(jnp.bfloat16), "wt", scatter_dimension=0, tiled=True
            ).astype(jnp.float32),
        )
        collected.append((summed_parts, expert_parts))
    ordered = collected[::-1]
    attention_gain_grad = jnp.stack([item[0][0] for item in ordered])
    query_grad = jnp.stack([item[0][1] for item in ordered])
    key_grad = jnp.stack([item[0][2] for item in ordered])
    value_grad = jnp.stack([item[0][3] for item in ordered])
    out_grad = jnp.stack([item[0][4] for item in ordered])
    mixture_gain_grad = jnp.stack([item[0][5] for item in ordered])
    router_grad = jnp.stack([item[0][6] for item in ordered])
    gate_grad = jnp.stack([item[1][0] for item in ordered])[:, None]
    up_grad = jnp.stack([item[1][1] for item in ordered])[:, None]
    down_grad = jnp.stack([item[1][2] for item in ordered])[:, None]
    return (
        block_output,
        upstream[None],
        attention_gain_grad,
        query_grad,
        key_grad,
        value_grad,
        out_grad,
        mixture_gain_grad,
        router_grad,
        gate_grad,
        up_grad,
        down_grad,
    )


def solution(mesh):
    placed = (
        P("wt", "ctx", None),
        P("wt", "ctx", None),
        P("wt", None),
        P("wt", None, None),
        P(None, "wt", "ctx", None),
        P(None, "wt"),
        P(None, "wt", None),
        P(None, "wt", None),
        P(None, "wt", None),
        P(None, "wt", None),
        P(None, "wt"),
        P(None, "wt", None),
        P(None, "ctx", None, "wt"),
        P(None, "ctx", None, "wt"),
        P(None, "ctx", "wt", None),
    )
    def local(*arrays):
        if by_heads(mesh, *arrays):
            return local_heads(mesh, *arrays)
        return local_rows(*arrays)

    return jax.shard_map(
        local,
        mesh=mesh,
        in_specs=placed,
        out_specs=(
            P("wt", "ctx", None),
            P("wt", "ctx", None),
            P(None, "wt"),
            P(None, "wt", None),
            P(None, "wt", None),
            P(None, "wt", None),
            P(None, "wt", None),
            P(None, "wt"),
            P(None, "wt", None),
            P(None, "ctx", None, "wt"),
            P(None, "ctx", None, "wt"),
            P(None, "ctx", "wt", None),
        ),
        check_vma=False,
    )
```

```python
import functools

import jax
import jax.numpy as jnp
from jax import lax
from jax.experimental import pallas as pl
from jax.experimental.pallas import tpu as pltpu
from jax.sharding import PartitionSpec as P

HEADS = 24
KV_HEADS = 8
HEAD = 64
BLK = 128


EPS = 1e-05
NEG = -1e30


def rms_scale(rows, gain):
    return rows * lax.rsqrt(jnp.mean(rows * rows, axis=-1, keepdims=True) + EPS) * gain


def stream_positions(table, width):
    offsets = jnp.arange(width, dtype=jnp.int32)
    return (table[:, :, None] * width + offsets[None, None, :]).reshape(-1)


def sequence_ids(positions, seq_row):
    ends = jnp.cumsum(seq_row)
    return jnp.sum((positions[:, None] >= ends[None, :]).astype(jnp.int32), axis=1)


def outer_rows(left, right):
    return lax.dot_general(
        left, right, (((0,), (0,)), ((), ())), preferred_element_type=jnp.float32
    )


def times_transposed(left, right):
    return lax.dot_general(
        left, right, (((1,), (1,)), ((), ())), preferred_element_type=jnp.float32
    )


def unchanged(state):
    return state


def times(left, right, a, b):
    return lax.dot_general(left, right, (((a,), (b,)), ((), ())), preferred_element_type=jnp.float32)


def vmem(count):
    return [pl.BlockSpec(memory_space=pltpu.VMEM)] * count


def kernel_params():
    return pltpu.CompilerParams(vmem_limit_bytes=56 * 2**20)


def cost(flops, nbytes, transcendentals=0):
    return pl.CostEstimate(flops=int(flops), bytes_accessed=int(nbytes), transcendentals=int(transcendentals))


def causal_mask(span):
    key_at = lax.broadcasted_iota(jnp.int32, (span, span), 0)
    query_at = lax.broadcasted_iota(jnp.int32, (span, span), 1)
    return key_at <= query_at


def front_kernel(raw, rep, head, span, base, spot_ref, owner_ref, at_ref, *refs):
    *blocks, gain_ref, w0, w1, w2, w3, normed_ref, qkv_ref, sent_ref, exact_ref, log_ref = refs
    rows = blocks[0].shape[0]
    count = len(blocks) - 1
    tokens = count * rows
    width = rep * head
    scale = head ** (-0.5)
    gain = gain_ref[...]
    for k in range(count):
        low, high = (blocks[k],) * 2 if k < count - 1 else blocks[k:]
        half = low.shape[0] if k == count - 1 else rows
        for start, ref in ((0, low), (half, high)) if k == count - 1 else ((0, low),):
            block = ref[...]
            if raw:
                block = rms_scale(block.astype(jnp.float32), gain).astype(jnp.bfloat16)
            normed_ref[spot_ref[k], start : start + ref.shape[0], :] = block
    lanes_all = qkv_ref.shape[0]
    slice_width = w0.shape[1]
    for part in range(tokens // span):
        take = span // rows
        total = 0.0
        for m, weight_ref in enumerate((w0, w1, w2, w3)):
            lanes = pl.ds(pl.multiple_of(at_ref[m] * slice_width, 128), slice_width)
            piece = normed_ref[part * take : (part + 1) * take, :, lanes].reshape(span, slice_width)
            total = total + times(weight_ref[base : base + lanes_all, :], piece, 1, 1)
        qkv_ref[:, part * span : (part + 1) * span] = total.astype(jnp.bfloat16)
    mask = causal_mask(span)
    per = span // rows
    for part in range(tokens // span):
        lanes = pl.ds(part * span, span)
        seen = (part + 1) * span
        keys = qkv_ref[width : width + head, :seen]
        values = qkv_ref[width + head : lanes_all, :seen]
        for h in range(rep):
            at = slice(h * head, (h + 1) * head)
            scores = times(keys, qkv_ref[at, lanes], 0, 0) * scale
            last = jnp.where(mask, scores[seen - span :], NEG)
            top = jnp.max(last, axis=0, keepdims=True)
            if part:
                top = jnp.maximum(top, jnp.max(scores[: seen - span], axis=0, keepdims=True))
            weights = jnp.exp(last - top)
            if part:
                weights = jnp.concatenate([jnp.exp(scores[: seen - span] - top), weights], axis=0)
            total = jnp.sum(weights, axis=0, keepdims=True)
            result = times(values, weights.astype(jnp.bfloat16), 1, 0) / total
            exact_ref[at, lanes] = result
            log_ref[h : h + 1, lanes] = top + jnp.log(total)
            for b in range(per):
                sent_ref[owner_ref[part * per + b], at, :] = result[:, b * rows : (b + 1) * rows].astype(jnp.bfloat16)


def front(raw, spots, owner_of, at, blocks, gain, pieces, base, rep, head):
    rows, width = blocks[0].shape
    count = len(blocks) - 1
    tokens = count * rows
    span = min(256, tokens)
    deep = (rep + 2) * head
    pairs = rep * tokens * (tokens + span) // 2
    return pl.pallas_call(
        functools.partial(front_kernel, raw, rep, head, span, base),
        out_shape=(
            jax.ShapeDtypeStruct((count, rows, width), jnp.bfloat16),
            jax.ShapeDtypeStruct((deep, tokens), jnp.bfloat16),
            jax.ShapeDtypeStruct((count, rep * head, rows), jnp.bfloat16),
            jax.ShapeDtypeStruct((rep * head, tokens), jnp.float32),
            jax.ShapeDtypeStruct((rep, tokens), jnp.float32),
        ),
        in_specs=[pl.BlockSpec(memory_space=pltpu.SMEM)] * 3 + vmem(len(blocks) + 5),
        out_specs=tuple(vmem(5)),
        compiler_params=kernel_params(),
        cost_estimate=cost(4 * head * pairs + 2 * deep * width * tokens, 9 * 2**20, pairs),
        name="front",
    )(spots, owner_of, at, *blocks, gain, *pieces)


def attend_back_kernel(rep, head, span, owner_ref, qkv_ref, exact_ref, log_ref, grad_ref, whole_ref, sent_ref, grad_all, keys_sum, values_sum):
    tokens = qkv_ref.shape[1]
    rows = grad_ref.shape[2]
    width = rep * head
    per = span // rows
    scale = head ** (-0.5)
    mask = causal_mask(span)
    for block in range(tokens // rows):
        grad_all[:, block * rows : (block + 1) * rows] = grad_ref[owner_ref[block]]
    keys_sum[...] = jnp.zeros_like(keys_sum)
    values_sum[...] = jnp.zeros_like(values_sum)
    for part in range(tokens // span):
        lanes = pl.ds(part * span, span)
        seen = (part + 1) * span
        keys = qkv_ref[width : width + head, :seen]
        values = qkv_ref[width + head :, :seen]
        for h in range(rep):
            at = slice(h * head, (h + 1) * head)
            queries = qkv_ref[at, lanes]
            grads = grad_all[at, lanes]
            delta = jnp.sum(grads.astype(jnp.float32) * exact_ref[at, lanes], axis=0, keepdims=True)
            scores = times(keys, queries, 0, 0) * scale
            probs = jnp.exp(scores - log_ref[h : h + 1, lanes])
            last = jnp.where(mask, probs[seen - span :], 0.0)
            probs = last if part == 0 else jnp.concatenate([probs[: seen - span], last], axis=0)
            pulled = times(values, grads, 0, 0)
            slopes = (probs * (pulled - delta)).astype(jnp.bfloat16)
            back = (times(keys, slopes, 1, 0) * scale).astype(jnp.bfloat16)
            whole_ref[at, lanes] = back
            for b in range(per):
                sent_ref[owner_ref[part * per + b], at, :] = back[:, b * rows : (b + 1) * rows]
            keys_sum[:, :seen] += times(queries, slopes, 1, 1)
            values_sum[:, :seen] += times(grads, probs.astype(jnp.bfloat16), 1, 1)
    keys_low = (keys_sum[...] * scale).astype(jnp.bfloat16)
    values_low = values_sum[...].astype(jnp.bfloat16)
    whole_ref[width : width + head, :] = keys_low
    whole_ref[width + head :, :] = values_low
    for block in range(tokens // rows):
        cut = slice(block * rows, (block + 1) * rows)
        sent_ref[owner_ref[block], width : width + head, :] = keys_low[:, cut]
        sent_ref[owner_ref[block], width + head :, :] = values_low[:, cut]


def attend_back(owner_of, qkv, exact, log_total, grads, rep, head):
    deep, tokens = qkv.shape
    count, _, rows = grads.shape
    span = min(256, tokens)
    pairs = rep * tokens * (tokens + span) // 2
    return pl.pallas_call(
        functools.partial(attend_back_kernel, rep, head, span),
        out_shape=(
            jax.ShapeDtypeStruct((deep, tokens), jnp.bfloat16),
            jax.ShapeDtypeStruct((count, deep, rows), jnp.bfloat16),
        ),
        in_specs=[pl.BlockSpec(memory_space=pltpu.SMEM)] + vmem(4),
        out_specs=tuple(vmem(2)),
        scratch_shapes=[
            pltpu.VMEM((rep * head, tokens), jnp.bfloat16),
            pltpu.VMEM((head, tokens), jnp.float32),
            pltpu.VMEM((head, tokens), jnp.float32),
        ],
        compiler_params=kernel_params(),
        cost_estimate=cost(10 * head * pairs, 6 * 2**20, pairs),
        name="attend_back",
    )(owner_of, qkv, exact, log_total, grads)


def silu_pair(gate_value, up_value):
    return (gate_value * jax.nn.sigmoid(gate_value) * up_value).astype(jnp.bfloat16)


def pair_back(grad_inner, gate_value, up_value):
    sigma = jax.nn.sigmoid(gate_value)
    grad_gate = grad_inner * up_value * sigma * (1.0 + gate_value * (1.0 - sigma))
    return grad_gate.astype(jnp.bfloat16), (grad_inner * gate_value * sigma).astype(jnp.bfloat16)


def by_piece(gate, up, down):
    return [piece for pieces in zip(gate, up, down) for piece in pieces]


def expert_forward_kernel(rows_ref, *refs):
    weights, (made_ref, gates_ref, ups_ref, inner_ref, total) = refs[:12], refs[12:]
    rows = rows_ref[...]
    for m in range(4):
        gate_value = times(rows, weights[3 * m][...], 1, 0)
        up_value = times(rows, weights[3 * m + 1][...], 1, 0)
        gates_ref[m] = gate_value
        ups_ref[m] = up_value
        inner = silu_pair(gate_value, up_value)
        inner_ref[m] = inner
        part = times(inner, weights[3 * m + 2][...], 1, 0)
        if m == 0:
            total[...] = part
        elif m < 3:
            total[...] += part
        else:
            made_ref[...] = (total[...] + part).astype(jnp.bfloat16)


def expert_forward(rows, gate, up, down):
    count, width = rows.shape
    hidden = gate[0].shape[1]
    weights = by_piece(gate, up, down)
    return pl.pallas_call(
        expert_forward_kernel,
        out_shape=(
            jax.ShapeDtypeStruct((count, width), jnp.bfloat16),
            jax.ShapeDtypeStruct((4, count, hidden), jnp.float32),
            jax.ShapeDtypeStruct((4, count, hidden), jnp.float32),
            jax.ShapeDtypeStruct((4, count, hidden), jnp.bfloat16),
        ),
        in_specs=vmem(1) + vmem(12),
        out_specs=tuple(vmem(4)),
        scratch_shapes=[pltpu.VMEM((count, width), jnp.float32)],
        compiler_params=kernel_params(),
        cost_estimate=cost(24 * count * width * hidden, 16 * 2**20, 4 * count * hidden),
        name="expert_forward",
    )(rows, *weights)


def expert_backward_kernel(grad_ref, *refs):
    weights, (gates, ups, back_ref, grad_gate_ref, grad_up_ref, total) = refs[2:14], refs[:2] + refs[14:]
    grads = grad_ref[...]
    for m in range(4):
        grad_inner = times(grads, weights[3 * m + 2][...], 1, 1)
        grad_gate, grad_up = pair_back(grad_inner, gates[m], ups[m])
        grad_gate_ref[m] = grad_gate
        grad_up_ref[m] = grad_up
        part = times(grad_gate, weights[3 * m][...], 1, 1) + times(grad_up, weights[3 * m + 1][...], 1, 1)
        if m == 0:
            total[...] = part
        elif m < 3:
            total[...] += part
        else:
            back_ref[...] = (total[...] + part).astype(jnp.bfloat16)


def expert_backward(grads, gate, up, down, gates, ups):
    count, width = grads.shape
    hidden = gate[0].shape[1]
    weights = [gates, ups] + by_piece(gate, up, down)
    return pl.pallas_call(
        expert_backward_kernel,
        out_shape=(
            jax.ShapeDtypeStruct((count, width), jnp.bfloat16),
            jax.ShapeDtypeStruct((4, count, hidden), jnp.bfloat16),
            jax.ShapeDtypeStruct((4, count, hidden), jnp.bfloat16),
        ),
        in_specs=vmem(1) + vmem(14),
        out_specs=tuple(vmem(3)),
        scratch_shapes=[pltpu.VMEM((count, width), jnp.float32)],
        compiler_params=kernel_params(),
        cost_estimate=cost(24 * count * width * hidden, 16 * 2**20, 4 * count * hidden),
        name="expert_backward",
    )(grads, *weights)


def expert_both_kernel(experts, mine_ref, rows_ref, cot_ref, router_ref, *refs):
    weights, outs = refs[:12], refs[12:]
    made_ref, back_ref, grad_ref, inner_ref, grad_gate_ref, grad_up_ref, total, total_back = outs
    rows = rows_ref[...]
    count, width = rows.shape
    cot = cot_ref[:, :width].astype(jnp.float32)
    logits = times(rows, router_ref[...], 1, 1)
    ids = lax.broadcasted_iota(jnp.int32, logits.shape, 1)
    logits = jnp.where(ids < experts, logits, NEG)
    odds = jnp.exp(logits - jnp.max(logits, axis=1, keepdims=True))
    other = cot_ref[:, width : width + 1].astype(jnp.float32).astype(jnp.int32)
    own_odds = jnp.sum(jnp.where(ids == mine_ref[0], odds, 0.0), axis=1, keepdims=True)
    other_odds = jnp.sum(jnp.where(ids == other, odds, 0.0), axis=1, keepdims=True)
    grad_ref[...] = (own_odds / (own_odds + other_odds) * cot).astype(jnp.bfloat16)
    grads = grad_ref[...]
    for m in range(4):
        gate, up = weights[3 * m], weights[3 * m + 1]
        gate_value = times(rows, gate[...], 1, 0)
        up_value = times(rows, up[...], 1, 0)
        inner = silu_pair(gate_value, up_value)
        inner_ref[m] = inner
        down = weights[3 * m + 2]
        grad_gate, grad_up = pair_back(times(grads, down[...], 1, 1), gate_value, up_value)
        grad_gate_ref[m] = grad_gate
        grad_up_ref[m] = grad_up
        part = times(inner, down[...], 1, 0)
        part_back = times(grad_gate, gate[...], 1, 1) + times(grad_up, up[...], 1, 1)
        total[...] = part if m == 0 else total[...] + part
        total_back[...] = part_back if m == 0 else total_back[...] + part_back
    made = total[...].astype(jnp.bfloat16)
    made_ref[...] = made
    back_ref[:, :width] = total_back[...].astype(jnp.bfloat16)
    signal = jnp.sum(cot * made.astype(jnp.float32), axis=1, keepdims=True)
    high = signal.astype(jnp.bfloat16)
    low = (signal - high.astype(jnp.float32)).astype(jnp.bfloat16)
    at = lax.broadcasted_iota(jnp.int32, (count, back_ref.shape[1] - width), 1)
    back_ref[:, width:] = jnp.where(
        at == 0, high.astype(jnp.float32), jnp.where(at == 1, low.astype(jnp.float32), 0.0)
    ).astype(jnp.bfloat16)


def expert_both(experts, mine, rows, cot, router, gate, up, down):
    count, width = rows.shape
    hidden = gate[0].shape[1]
    weights = by_piece(gate, up, down)
    return pl.pallas_call(
        functools.partial(expert_both_kernel, experts),
        out_shape=(
            jax.ShapeDtypeStruct((count, width), jnp.bfloat16),
            jax.ShapeDtypeStruct(cot.shape, jnp.bfloat16),
            jax.ShapeDtypeStruct((count, width), jnp.bfloat16),
            jax.ShapeDtypeStruct((4, count, hidden), jnp.bfloat16),
            jax.ShapeDtypeStruct((4, count, hidden), jnp.bfloat16),
            jax.ShapeDtypeStruct((4, count, hidden), jnp.bfloat16),
        ),
        in_specs=[pl.BlockSpec(memory_space=pltpu.SMEM)] + vmem(3) + vmem(12),
        out_specs=tuple(vmem(6)),
        scratch_shapes=[pltpu.VMEM((count, width), jnp.float32)] * 2,
        compiler_params=kernel_params(),
        cost_estimate=cost(48 * count * width * hidden, 18 * 2**20, 8 * count * hidden),
        name="expert_both",
    )(mine, rows, cot, router, *weights)


def expert_grads_kernel(rows_ref, grad_ref, inner_ref, grad_gate_ref, grad_up_ref, pair_give, far_give, pair_own, pair_far, down_give, down_own, down_far):
    for m, (pairs, at, downs, down_at) in enumerate(
        (
            (pair_own, 0, down_own, 0),
            (pair_give, 0, down_give, 0),
            (pair_far, 0, down_far, 0),
            (far_give, 0, down_give, 1),
        )
    ):
        pairs[at] = times(rows_ref[...], grad_gate_ref[m], 0, 0).astype(jnp.bfloat16)
        pairs[at + 1] = times(rows_ref[...], grad_up_ref[m], 0, 0).astype(jnp.bfloat16)
        downs[down_at] = times(inner_ref[m], grad_ref[...], 0, 0).astype(jnp.bfloat16)


def expert_grads(rows, grads, inner, grad_gate, grad_up):
    count, width = rows.shape
    hidden = inner.shape[2]
    shapes = [(2, width, hidden)] * 4
    shapes += [(2, hidden, width), (1, hidden, width), (1, hidden, width)]
    return pl.pallas_call(
        expert_grads_kernel,
        out_shape=tuple(jax.ShapeDtypeStruct(shape, jnp.bfloat16) for shape in shapes),
        in_specs=vmem(5),
        out_specs=tuple(vmem(7)),
        compiler_params=kernel_params(),
        cost_estimate=cost(24 * count * width * hidden, 14 * 2**20),
        name="expert_grads",
    )(rows, grads, inner, grad_gate, grad_up)


def head_grads_kernel(part, at_ref, normed_ref, whole_ref, small_ref, give_ref, own_ref, far_ref):
    tokens = whole_ref.shape[1]
    deep = whole_ref.shape[0]
    for m, (ref, slot) in enumerate(((own_ref, 0), (give_ref, 0), (far_ref, 0), (give_ref, 1))):
        lanes = pl.ds(pl.multiple_of(at_ref[m] * part, 128), part)
        rows = normed_ref[:, :, lanes].reshape(tokens, part)
        ref[slot, :deep, :] = times(whole_ref[...], rows, 1, 0).astype(jnp.bfloat16)
        ref[slot, deep:, :] = small_ref[:, lanes].astype(jnp.bfloat16)


def head_grads(at, normed, whole, small):
    deep, tokens = whole.shape
    width = normed.shape[2]
    part = width // 4
    full = deep + small.shape[0]
    return pl.pallas_call(
        functools.partial(head_grads_kernel, part),
        out_shape=tuple(jax.ShapeDtypeStruct((n, full, part), jnp.bfloat16) for n in (2, 1, 1)),
        in_specs=[pl.BlockSpec(memory_space=pltpu.SMEM)] + vmem(3),
        out_specs=tuple(vmem(3)),
        compiler_params=kernel_params(),
        cost_estimate=cost(2**20, 2**16),
        name="head_grads",
    )(at, normed, whole, small)


def spread_kernel(wide, head, ringed, *refs):
    if ringed:
        spot_ref, *blocks, query_ref, key_ref, value_ref = refs[: ringed + 4]
        gathered_ref = refs[-1]
        outs = refs[-7:-1]
        for k, block in enumerate(blocks[:-2]):
            gathered_ref[spot_ref[k]] = block[...]
        half = blocks[-2].shape[0]
        gathered_ref[spot_ref[ringed - 2], :half, :] = blocks[-2][...]
        gathered_ref[spot_ref[ringed - 2], half:, :] = blocks[-1][...]
    else:
        gathered_ref, query_ref, key_ref, value_ref = refs[:4]
        outs = refs[-6:]
    query_out, key_out, value_out, out_out, small_out, sum_ref = outs
    count, _, part = gathered_ref.shape
    deep = wide + 2 * head
    small = small_out.shape[0]
    sums = jnp.zeros((part, 1), jnp.float32)
    for i in range(count // 2):
        block = gathered_ref[2 * i : 2 * i + 2, :wide, :].astype(jnp.float32).reshape(2 * wide, part).T
        lanes = slice(2 * i * wide, 2 * (i + 1) * wide)
        query_out[0, :, lanes] = block
        sums += jnp.sum(block * query_ref[:, lanes].astype(jnp.float32), axis=1, keepdims=True)
    for start, weight_ref, out in ((wide, key_ref, key_out), (wide + head, value_ref, value_out)):
        block = gathered_ref[:, start : start + head, :].astype(jnp.float32).reshape(count * head, part).T
        out[0] = block
        sums += jnp.sum(block * weight_ref[...].astype(jnp.float32), axis=1, keepdims=True)
    sum_ref[...] = sums
    total = gathered_ref[0, deep : deep + small, :].astype(jnp.float32)
    for c in range(1, count):
        total += gathered_ref[c, deep : deep + small, :].astype(jnp.float32)
    small_out[...] = total
    rows = part // count
    for c in range(count):
        for j in range(out_out.shape[2] // part):
            piece = gathered_ref[c, deep + small + j * rows : deep + small + (j + 1) * rows, :]
            out_out[0, c * rows : (c + 1) * rows, j * part : (j + 1) * part] = piece.astype(jnp.float32)


def spread(layer, layers, spots, sources, weights, wide, head, small, before):
    ringed = len(sources) if spots is not None else 0
    part = weights[0].shape[0]
    width = weights[0].shape[1]
    count = width // wide
    shapes = [(layers,) + weight.shape for weight in weights] + [(layers, part, width)]
    aliased = [] if before is None else list(before)
    one = lambda shape: pl.BlockSpec((1,) + shape[1:], lambda i: (layer, 0, 0))
    whole = lambda shape: pl.BlockSpec(shape, lambda i: (0,) * len(shape))
    deep = sources[0].shape[-2]
    lead = [spots] if ringed else []
    return pl.pallas_call(
        functools.partial(spread_kernel, wide, head, ringed),
        grid=(1,),
        out_shape=tuple(jax.ShapeDtypeStruct(shape, jnp.float32) for shape in shapes)
        + (jax.ShapeDtypeStruct((small, part), jnp.float32), jax.ShapeDtypeStruct((part, 1), jnp.float32)),
        in_specs=[pl.BlockSpec(memory_space=pltpu.SMEM)] * len(lead)
        + [whole(source.shape) for source in sources]
        + [whole(weight.shape) for weight in weights]
        + [pl.BlockSpec(memory_space=pl.ANY)] * len(aliased),
        out_specs=tuple(one(shape) for shape in shapes) + (whole((small, part)), whole((part, 1))),
        scratch_shapes=[pltpu.VMEM((count, deep, part), jnp.bfloat16)] if ringed else [],
        input_output_aliases={len(lead) + len(sources) + 3 + i: i for i in range(len(aliased))},
        compiler_params=kernel_params(),
        cost_estimate=cost(2**20, 2**16),
        name="spread",
    )(*lead, *sources, *weights, *aliased)


def finish_kernel(*refs):
    own_ref, near_ref = refs[:2]
    count = own_ref.shape[0]
    for i, (far_ref, out) in enumerate(zip(refs[2 : 2 + count], refs[-count:])):
        total = own_ref[i].astype(jnp.float32) + near_ref[i].astype(jnp.float32) + far_ref[...].astype(jnp.float32)
        out[0, 0] = total


def finish(layer, layers, own, near, far, before):
    count, rows, columns = own.shape
    steps = 2
    block = rows // steps
    aliased = [] if before is None else list(before)
    taken = pl.BlockSpec((count, block, columns), lambda i: (0, i, 0))
    made = pl.BlockSpec((1, 1, block, columns), lambda i: (layer, 0, i, 0))
    return pl.pallas_call(
        finish_kernel,
        grid=(steps,),
        out_shape=tuple(jax.ShapeDtypeStruct((layers, 1, rows, columns), jnp.float32) for _ in range(count)),
        in_specs=[taken] * 2
        + [pl.BlockSpec((block, columns), lambda i: (i, 0))] * count
        + [pl.BlockSpec(memory_space=pl.ANY)] * len(aliased),
        out_specs=(made,) * count,
        input_output_aliases={2 + count + i: i for i in range(len(aliased))},
        compiler_params=kernel_params(),
        cost_estimate=cost(2**20, 2**16),
        name="finish",
    )(own, near, *far, *aliased)


def head_rows_kernel(wide, head, at_ref, query_ref, key_ref, value_ref, small_ref, out_ref):
    odd = at_ref[0] % 2
    top = 0
    for ref, size in ((query_ref, wide), (key_ref, head), (value_ref, head)):
        turned = ref[0].astype(jnp.float32).T
        out_ref[0, top : top + size, :] = jnp.where(odd == 1, turned[size:], turned[:size]).astype(jnp.bfloat16)
        top += size
    out_ref[0, top:, :] = small_ref[0]


def head_rows(mine, query_weight, key_weight, value_weight, small, wide, head):
    layers, part, _ = query_weight.shape
    rows = wide + 2 * head + small.shape[1]
    taken = lambda size: pl.BlockSpec((1, part, 2 * size), lambda i, at: (i, 0, at[0] // 2))
    return pl.pallas_call(
        functools.partial(head_rows_kernel, wide, head),
        grid_spec=pltpu.PrefetchScalarGridSpec(
            num_scalar_prefetch=1,
            grid=(layers,),
            in_specs=[taken(wide), taken(head), taken(head), pl.BlockSpec((1,) + small.shape[1:], lambda i, at: (i, 0, 0))],
            out_specs=pl.BlockSpec((1, rows, part), lambda i, at: (i, 0, 0)),
        ),
        out_shape=jax.ShapeDtypeStruct((layers, rows, part), jnp.bfloat16),
        compiler_params=kernel_params(),
        cost_estimate=cost(2**20, 2**16),
        name="head_rows",
    )(mine, query_weight, key_weight, value_weight, small)


def middle_forward_kernel(at_ref, attended_ref, state_ref, gain_ref, place_ref, *refs):
    weights, (middle_ref, mixed_ref, out_ref) = refs[:4], refs[4:]
    part = weights[0].shape[0]
    total = state_ref[...]
    for m in range(4):
        rows = attended_ref[pl.ds(pl.multiple_of(at_ref[m] * part, 128), part), :]
        total = total + times(rows, weights[m][...], 0, 0)
    middle_ref[...] = total
    mixed = rms_scale(total, gain_ref[...]).astype(jnp.bfloat16)
    mixed_ref[...] = mixed
    out_ref[...] = times(place_ref[0] + place_ref[1], mixed, 0, 0).astype(jnp.bfloat16)


def middle_forward(at, attended, pieces, state, gain, place):
    rows, width = state.shape
    slots = place.shape[2]
    return pl.pallas_call(
        middle_forward_kernel,
        out_shape=(
            jax.ShapeDtypeStruct((rows, width), jnp.float32),
            jax.ShapeDtypeStruct((rows, width), jnp.bfloat16),
            jax.ShapeDtypeStruct((slots, width), jnp.bfloat16),
        ),
        in_specs=[pl.BlockSpec(memory_space=pltpu.SMEM)] + vmem(4) + vmem(4),
        out_specs=tuple(vmem(3)),
        compiler_params=kernel_params(),
        cost_estimate=cost(2 * rows * width * (width + slots), 9 * 2**20),
        name="middle_forward",
    )(at, attended, state, gain, place, *pieces)


def middle_back_kernel(experts, at_ref, place_ref, back_ref, upstream_ref, middle_ref, mixed_ref, gain_ref, router_ref, chosen_ref, *refs):
    *results, w0, w1, w2, w3, grad_ref, low_ref, heads_ref, small_ref = refs
    weights = (w0, w1, w2, w3)
    rows, width = upstream_ref.shape
    part = w0.shape[0]
    upstream, mixed, router = upstream_ref[...], mixed_ref[...], router_ref[...]
    logits = times(mixed, router, 1, 1)
    ids = lax.broadcasted_iota(jnp.int32, logits.shape, 1)
    logits = jnp.where(ids < experts, logits, NEG)
    odds = jnp.exp(logits - jnp.max(logits, axis=1, keepdims=True))
    probs = odds / jnp.sum(odds, axis=1, keepdims=True)
    hits = [ids == chosen_ref[:, c : c + 1] for c in range(2)]
    picked = [jnp.sum(jnp.where(hit, probs, 0.0), axis=1, keepdims=True) for hit in hits]
    pair_total = picked[0] + picked[1]
    if results:
        signal = [jnp.sum(upstream * r[...].astype(jnp.float32), axis=1, keepdims=True) for r in results]
    else:
        signal = [jnp.sum(times(place_ref[c], back_ref[:, width:], 1, 0), axis=1, keepdims=True) for c in range(2)]
    mean = (picked[0] * signal[0] + picked[1] * signal[1]) / pair_total
    slopes = [(s - mean) / pair_total for s in signal]
    grad_probs = jnp.where(hits[0], slopes[0], 0.0) + jnp.where(hits[1], slopes[1], 0.0)
    grad_logits = probs * (grad_probs - jnp.sum(probs * grad_probs, axis=1, keepdims=True))
    high = grad_logits.astype(jnp.bfloat16)
    rest = (grad_logits - high.astype(jnp.float32)).astype(jnp.bfloat16)
    small_ref[...] = jnp.zeros_like(small_ref)
    router_part = times(high, mixed, 0, 0) + times(rest, mixed, 0, 0)
    small_ref[:experts, :] = router_part[:experts]
    grad_mixed = times(place_ref[0] + place_ref[1], back_ref[:, :width], 1, 0)
    grad_mixed = grad_mixed + times(high, router, 1, 0) + times(rest, router, 1, 0)
    pulled, gain_rows = rms_back(middle_ref[...], gain_ref[...], grad_mixed)
    small_ref[experts : experts + 1, :] = jnp.sum(gain_rows, axis=0, keepdims=True)
    grad = upstream + pulled
    grad_ref[...] = grad
    low = grad.astype(jnp.bfloat16)
    low_ref[...] = low
    for m in range(4):
        lanes = pl.ds(pl.multiple_of(at_ref[m] * part, 128), part)
        heads_ref[lanes, :] = times(weights[m][...], low, 1, 1).astype(jnp.bfloat16)


def middle_back(experts, at, place, back, upstream, middle, mixed, gain, router, chosen, results, pieces):
    rows, width = upstream.shape
    slots = place.shape[2]
    return pl.pallas_call(
        functools.partial(middle_back_kernel, experts),
        out_shape=(
            jax.ShapeDtypeStruct((rows, width), jnp.float32),
            jax.ShapeDtypeStruct((rows, width), jnp.bfloat16),
            jax.ShapeDtypeStruct((width, rows), jnp.bfloat16),
            jax.ShapeDtypeStruct((experts + 8, width), jnp.float32),
        ),
        in_specs=[pl.BlockSpec(memory_space=pltpu.SMEM)] + vmem(8 + len(results)) + vmem(4),
        out_specs=tuple(vmem(4)),
        compiler_params=kernel_params(),
        cost_estimate=cost(2 * rows * width * (width + slots), 10 * 2**20),
        name="middle_back",
    )(at, place, back, upstream, middle, mixed, gain, router, chosen, *results, *pieces)


def swap(x, mask):
    return lax.ppermute(x, "wt", [(i, i ^ mask) for i in range(4)])


def near_finish(far, own):
    return (own, swap(own, 1), far, swap(far, 1))


def wt_gather(own):
    return near_finish(swap(own, 2), own)


def wt_exchange(slices, me):
    def cut(m):
        return lax.dynamic_index_in_dim(slices, me ^ m, 0, keepdims=False)

    far = swap(jnp.stack([cut(2), cut(3)]), 2)
    near = swap(jnp.stack([cut(1), far[1]]), 1)
    return (cut(0), near[0], far[0], near[1])


def in_order(pieces, me, axis):
    own, near, far, last = pieces
    odd, high = me % 2 == 1, me >= 2
    low = (jnp.where(odd, near, own), jnp.where(odd, own, near))
    up = (jnp.where(odd, last, far), jnp.where(odd, far, last))
    first = [jnp.where(high, b, a) for a, b in zip(low, up)]
    second = [jnp.where(high, a, b) for a, b in zip(low, up)]
    return jnp.concatenate(first + second, axis=axis)


def tie(*arrays):
    return lax.optimization_barrier(arrays)


def ring_of(count):
    ring = list(range(0, count, 2)) + list(range(count - 1, 0, -2))
    offsets = [0] + [sign * step for step in range(1, count // 2) for sign in (-1, 1)] + [count // 2]
    table = [[ring[(ring.index(i) + k) % count] for k in offsets] for i in range(count)]
    return ring, jnp.asarray(table, jnp.int32)


def ring_start(x, ring):
    right = [(a, b) for a, b in zip(ring, ring[1:] + ring[:1])]
    left = [(b, a) for a, b in right]
    return lax.ppermute(x, "ctx", right), lax.ppermute(x, "ctx", left)


def ring_blocks(x, first, ring, early=None):
    count = len(ring)
    right = [(a, b) for a, b in zip(ring, ring[1:] + ring[:1])]
    left = [(b, a) for a, b in right]
    ahead, behind = first
    blocks = [x, ahead, behind]
    for _ in range(2, count // 2):
        ahead, behind = lax.ppermute(ahead, "ctx", right), lax.ppermute(behind, "ctx", left)
        blocks += [ahead, behind]
    if early is not None:
        ahead, behind, *early = tie(ahead, behind, *early)
    half = x.shape[0] // 2
    blocks += [lax.ppermute(ahead[:half], "ctx", right), lax.ppermute(behind[half:], "ctx", left)]
    return blocks if early is None else (blocks, early)


def all_to_all(x):
    return lax.all_to_all(x, "ctx", split_axis=0, concat_axis=0, tiled=True)


def rms_back(rows, gain, grad):
    scale = lax.rsqrt(jnp.mean(rows * rows, axis=-1, keepdims=True) + EPS)
    unit = rows * scale
    pulled = grad * gain
    return scale * (pulled - unit * jnp.mean(pulled * unit, axis=-1, keepdims=True)), grad * unit


def by_heads(mesh, tokens, cotangent, seq_lengths, block_deal, *rest):
    return (
        mesh.shape["ctx"] == KV_HEADS
        and mesh.shape["wt"] == 4
        and seq_lengths.shape[1] == 1
        and block_deal.shape[2] == 1
        and tokens.shape[1] == BLK
    )


def local_heads(
    mesh,
    tokens,
    cotangent,
    seq_lengths,
    block_deal,
    routes,
    attention_gain,
    query_weight,
    key_weight,
    value_weight,
    out_weight,
    mixture_gain,
    router_weight,
    gate_weight,
    up_weight,
    down_weight,
):
    n_ctx = mesh.shape["ctx"]
    rows = tokens.shape[1]
    width = tokens.shape[2]
    layers = query_weight.shape[0]
    experts = router_weight.shape[2]
    capacity = 3 * rows // experts
    slot_count = experts * capacity
    rep = HEADS // KV_HEADS
    wide = rep * HEAD
    lanes = wide + 2 * HEAD
    part = width // 4
    ctx = lax.axis_index("ctx")
    mine = ctx.astype(jnp.int32).reshape(1)
    wt = lax.axis_index("wt").astype(jnp.uint32)
    others = (wt ^ jnp.arange(4, dtype=jnp.uint32)).astype(jnp.int32)
    table = block_deal[0, :, 0]
    devices = jnp.arange(n_ctx, dtype=jnp.int32)
    owner_of = jnp.sum(jnp.where(table[None, :] == devices[:, None], devices[None, :], 0), axis=1)
    ring, ring_table = ring_of(n_ctx)
    ring_owners = lax.dynamic_index_in_dim(ring_table, ctx.astype(jnp.uint32), 0, keepdims=False)
    spots = jnp.sum(jnp.where(ring_owners[:, None] == devices[None, :], table[None, :], 0), axis=1)

    first = ring_start(tokens[0], ring)

    expert_ids = jnp.arange(experts, dtype=jnp.int32)
    chosen = routes[:, 0]
    flat = chosen.reshape(layers, 2 * rows)
    onehot = flat[:, :, None] == expert_ids
    earlier = jnp.tril(jnp.ones((2 * rows, 2 * rows), jnp.bfloat16), -1)
    rank = jnp.einsum("ij,lje->lie", earlier, onehot.astype(jnp.bfloat16), preferred_element_type=jnp.float32)
    rank = jnp.sum(jnp.where(onehot, rank, 0.0), axis=2).astype(jnp.int32)
    slots = (flat * capacity + rank).reshape(layers, rows, 2).transpose(0, 2, 1)
    place = (slots[..., None] == jnp.arange(slot_count, dtype=jnp.int32)).astype(jnp.bfloat16)
    named = (chosen.transpose(0, 2, 1)[..., None] == expert_ids).astype(jnp.float32)

    small_rows = jnp.concatenate(
        [
            router_weight.transpose(0, 2, 1),
            attention_gain[:, None],
            mixture_gain[:, None],
            jnp.zeros((layers, 14 - experts, part), jnp.bfloat16),
        ],
        axis=1,
    )
    deep = lanes + 16
    head_own = head_rows(mine, query_weight, key_weight, value_weight, small_rows, wide, HEAD)
    head_own = head_own.reshape(layers * deep, part)
    head_far = swap(head_own, 2)

    out_own = list(out_weight)
    gate_own = [gate_weight[layer, 0] for layer in range(layers)]
    up_own = [up_weight[layer, 0] for layer in range(layers)]
    down_own = [down_weight[layer, 0] for layer in range(layers)]
    query_own = list(query_weight)
    pair_own_weights = [jnp.concatenate([key_weight[layer], value_weight[layer]], axis=1) for layer in range(layers)]
    out_far, gate_far, up_far, down_far, query_far, key_far = [
        [swap(own, 2) for own in group]
        for group in (out_own, gate_own, up_own, down_own, query_own, pair_own_weights)
    ]

    last = layers - 1
    other = chosen[last].transpose(1, 0)[::-1, :, None].astype(jnp.bfloat16)
    cot_rows = jnp.concatenate(
        [jnp.broadcast_to(cotangent[0][None], (2, rows, width)), jnp.broadcast_to(other, (2, rows, 128))], axis=2
    ).reshape(2 * rows, width + 128)
    cot_out = times(place[last].reshape(2 * rows, slot_count), cot_rows, 0, 0).astype(jnp.bfloat16)

    state = tokens[0].astype(jnp.float32)
    saved = []
    for layer in range(layers):
        if layer == 0:
            blocks, head_pieces = ring_blocks(tokens[0], first, ring, near_finish(head_far, head_own))
            small_all = [
                in_order([piece[i * deep + lanes : (i + 1) * deep] for piece in head_pieces], wt, 1)
                for i in range(layers)
            ]
            cot_out = tie(cot_out, *blocks[-2:])[0]
            cot_slots = all_to_all(cot_out.reshape(experts, capacity, width + 128)).reshape(slot_count, width + 128)
        router = jnp.concatenate([small_all[layer][:experts], jnp.zeros((128 - experts, width), jnp.bfloat16)])
        gain_one = small_all[layer][experts : experts + 1].astype(jnp.float32)
        gain_two = small_all[layer][experts + 1 : experts + 2].astype(jnp.float32)
        if layer > 0:
            normed = rms_scale(state, gain_one).astype(jnp.bfloat16)
            blocks = ring_blocks(normed, ring_start(normed, ring), ring)
        normed_all, qkv, sent, exact, log_total = front(
            layer == 0, spots, owner_of, others, blocks, gain_one, head_pieces, layer * deep, rep, HEAD
        )
        if layer == 0:
            sent, cot_slots = tie(sent, cot_slots)
        else:
            sent, out_far[layer], up_far[layer] = tie(sent, out_far[layer], up_far[layer])
        attended = all_to_all(sent).reshape(width, rows)
        if layer == 0:
            attended, out_far[layer] = tie(attended, out_far[layer])
        out_pieces = near_finish(out_far[layer], out_own[layer])
        middle, mixed, outgoing = middle_forward(others, attended, out_pieces, state, gain_two, place[layer])
        outgoing = outgoing.reshape(experts, capacity, width)
        if layer == 0:
            outgoing, gate_far[layer] = tie(outgoing, gate_far[layer])
        else:
            outgoing, down_far[layer], *saved[0]["attended"] = tie(outgoing, down_far[layer], *saved[0]["attended"])
            kept_exchange = wt_exchange(attended.reshape(4, part, rows), wt)
        arrived = all_to_all(outgoing).reshape(slot_count, width)
        if layer == 0:
            kept_exchange = wt_exchange(attended.reshape(4, part, rows), wt)
        else:
            arrived, query_far[layer] = tie(arrived, query_far[layer])
        probs = jax.nn.softmax(times(mixed, router[:experts], 1, 1), axis=-1)
        picked = jnp.sum(named[layer] * probs[None], axis=-1, keepdims=True)
        pair_total = picked[0] + picked[1]
        gates = picked / pair_total
        kept = dict(
            state=state,
            normed_all=normed_all,
            qkv=qkv,
            exact=exact,
            log_total=log_total,
            attended=kept_exchange,
            middle=middle,
            mixed=mixed,
            gates=gates,
            arrived=arrived,
            gain_one=gain_one,
            gain_two=gain_two,
            router=router,
            out_pieces=out_pieces,
        )
        pieces = [near_finish(far[layer], own[layer]) for far, own in ((gate_far, gate_own), (up_far, up_own), (down_far, down_own))]
        kept["pieces"] = pieces
        saved.append(kept)
        if layer == last:
            break
        made, kept["gate_values"], kept["up_values"], kept["inner"] = expert_forward(arrived, *pieces)
        returned = all_to_all(made.reshape(experts, capacity, width)).reshape(slot_count, width)
        returned, gate_far[last] = tie(returned, gate_far[last])
        results = [times(place[layer, choice], returned, 1, 0) for choice in range(2)]
        kept["results"] = [result.astype(jnp.bfloat16) for result in results]
        state = middle + gates[0] * results[0] + gates[1] * results[1]

    upstream = cotangent[0].astype(jnp.float32)
    expert_done, head_done, returned, sources = None, None, None, None
    merge = lambda head, out: jnp.concatenate([head] + [out[:, i * part : (i + 1) * part] for i in range(4)], axis=0)
    smalls, gain_sums = [None] * layers, [None] * layers
    block_output = None
    for layer in reversed(range(layers)):
        k = saved[layer]
        gates, pieces = k["gates"], k["pieces"]
        if layer == last:
            arrived = k["arrived"]
            made, back, arrived_grad, inner, grad_gate, grad_up = expert_both(
                experts, mine, arrived, cot_slots, k["router"], *pieces
            )
            back = all_to_all(back.reshape(experts, capacity, width + 128))
            back = back.reshape(slot_count, width + 128)
            results = []
        else:
            arrived, inner = k["arrived"], k["inner"]
            back_rows = (gates * upstream[None]).astype(jnp.bfloat16).reshape(2 * rows, width)
            outgoing = times(place[layer].reshape(2 * rows, slot_count), back_rows, 0, 0).astype(jnp.bfloat16)
            outgoing, returned, head_sum, key_far[layer] = tie(outgoing, returned, sources[0], key_far[layer])
            sources = [lax.all_gather(merge(head_sum, sources[1]), "ctx", axis=0)]
            arrived_grad = all_to_all(outgoing.reshape(experts, capacity, width)).reshape(slot_count, width)
            state = saved[last]["middle"] + sum(
                saved[last]["gates"][i] * times(place[last, i], returned, 1, 0) for i in range(2)
            )
            block_output = state.astype(jnp.bfloat16)[None]
            back, grad_gate, grad_up = expert_backward(arrived_grad, *pieces, k["gate_values"], k["up_values"])
            back, *last_parts[2:4] = tie(back, *last_parts[2:4])
            back = all_to_all(back.reshape(experts, capacity, width)).reshape(slot_count, width)
            results = k["results"]
        pair_give, far_give, pair_own, pair_far, down_give, down_kept, down_far_part = expert_grads(
            arrived, arrived_grad, inner, grad_gate, grad_up
        )
        pair_near, far_near, down_near = swap(pair_give, 1), swap(far_give, 1), swap(down_give, 1)
        add = lambda a, b: (a.astype(jnp.float32) + b.astype(jnp.float32)).astype(jnp.bfloat16)
        pair_sums = [add(pair_far[i], far_near[i]) for i in range(2)]
        down_sum = add(down_far_part, down_near[1:])
        if layer == last:
            back, key_far[layer] = tie(back, key_far[layer])
        else:
            back, last_parts[6] = tie(back, last_parts[6])
            pair_done, down_done = last_finish(*last_parts)
            expert_done = [*pair_done, *down_done]
        pair_last = [swap(pair_sum, 2) for pair_sum in pair_sums]
        if layer == last:
            down_last = [swap(down_sum[0], 2)]
        grad_middle, middle_low, grad_attended, small = middle_back(
            experts,
            others,
            place[layer],
            back,
            upstream,
            k["middle"],
            k["mixed"],
            k["gain_two"],
            k["router"],
            chosen[layer],
            results,
            k["out_pieces"],
        )
        grad_heads = all_to_all(grad_attended.reshape(n_ctx, wide, rows))
        if layer == last:
            grad_heads, *k["attended"] = tie(grad_heads, *k["attended"])
        grad_whole, grad_sent = attend_back(owner_of, k["qkv"], k["exact"], k["log_total"], grad_heads, rep, HEAD)
        middle_pieces = wt_gather(middle_low)
        out_part = times(jnp.concatenate(k["attended"], axis=1), jnp.concatenate(middle_pieces, axis=0), 1, 0)
        out_part = out_part.astype(jnp.bfloat16)
        if layer == 0:
            out_rows = all_to_all(out_part.reshape(n_ctx, part // n_ctx, width))
            grad_sent, out_rows, *expert_done = tie(grad_sent, out_rows, *expert_done)
        else:
            grad_sent, query_far[0], out_part = tie(grad_sent, query_far[0], out_part)
            out_rows = lax.psum_scatter(out_part, "ctx", scatter_dimension=0, tiled=True)
        grad_own = all_to_all(grad_sent)
        if layer == 0:
            grad_whole, *pair_last = tie(grad_whole, *pair_last)
        head_give, head_kept, head_far = head_grads(others, k["normed_all"], grad_whole, small)
        head_near = swap(head_give, 1)
        head_last = swap(add(head_far[0], head_near[1]), 2)
        head_sum = (
            head_kept[0].astype(jnp.float32) + head_near[0].astype(jnp.float32) + head_last.astype(jnp.float32)
        ).astype(jnp.bfloat16)
        weights = [(query_weight[i], key_weight[i], value_weight[i]) for i in range(layers)]
        columns = lambda at, *rest: spread(at, layers, *rest[:2], weights[at], wide, HEAD, 16, rest[2])
        if layer == last:
            sources = [head_sum, out_rows]
            last_parts = [pair_own, pair_near, *pair_last, down_kept, down_near, *down_last]
            last_finish = lambda *p: (finish(last, layers, *p[:2], p[2:4], None), finish(last, layers, *p[4:6], p[6:], None))
            made = tie(made, grad_own)[0]
            returned = all_to_all(made.reshape(experts, capacity, width)).reshape(slot_count, width)
        else:
            *head_done, smalls[last], gain_sums[last] = columns(last, None, sources, None)
            out_rows = jnp.sum(out_rows.astype(jnp.float32), axis=0).astype(jnp.bfloat16)
            merged = merge(head_sum, out_rows)
            down_last = [swap(tie(down_sum, head_last)[0][0], 2)]
            sources = ring_blocks(merged, ring_start(merged, ring), ring)
            *tied, down_last[0] = tie(*sources[-2:], *head_done, down_last[0])
            sources[-2:], head_done = tied[:2], tied[2:]
            pair_done = finish(layer, layers, pair_own, pair_near, pair_last, expert_done[:2])
            down_done = finish(layer, layers, down_kept, down_near, down_last, expert_done[2:])
            expert_done = [*pair_done, *down_done]
            sources[-1], *expert_done = tie(sources[-1], *expert_done)
            *head_done, smalls[layer], gain_sums[layer] = columns(layer, ring_owners, sources, head_done)
        own_query = grad_own[:, :wide].reshape(width, rows)
        own_pair = jnp.concatenate(
            [
                grad_own[:, wide : wide + HEAD].reshape(n_ctx * HEAD, rows),
                grad_own[:, wide + HEAD :].reshape(n_ctx * HEAD, rows),
            ],
            axis=0,
        )
        query_pieces = near_finish(query_far[layer], query_own[layer])
        key_pieces = near_finish(key_far[layer], pair_own_weights[layer])
        grad_normed = jnp.zeros((rows, width), jnp.float32)
        for m in range(4):
            grad_normed = lax.dynamic_update_slice_in_dim(
                grad_normed,
                times(own_query, query_pieces[m], 0, 1) + times(own_pair, key_pieces[m], 0, 1),
                (wt ^ m) * part,
                1,
            )
        pulled, _ = rms_back(k["state"], k["gain_one"], grad_normed)
        upstream = grad_middle + pulled
    gain_one_grad = jnp.stack([s[:, 0] for s in gain_sums]) / attention_gain.astype(jnp.float32)
    small_grads = jnp.stack(smalls)
    query_grad, key_grad, value_grad, out_grad = head_done
    return (
        block_output,
        upstream[None],
        gain_one_grad,
        query_grad,
        key_grad,
        value_grad,
        out_grad,
        small_grads[:, experts],
        small_grads[:, :experts].transpose(0, 2, 1),
        *expert_done,
    )


def local_rows(
    tokens,
    cotangent,
    seq_lengths,
    block_deal,
    routes,
    attention_gain,
    query_weight,
    key_weight,
    value_weight,
    out_weight,
    mixture_gain,
    router_weight,
    gate_weight,
    up_weight,
    down_weight,
):
    rows_here = tokens.shape[1]
    width = tokens.shape[2]
    layers = query_weight.shape[0]
    experts = router_weight.shape[2]
    capacity = 3 * rows_here // experts
    kv_groups = KV_HEADS
    per_group = HEADS // KV_HEADS
    head_size = HEAD
    kv_width = kv_groups * head_size
    scale = head_size ** (-0.5)
    device = lax.axis_index("ctx")
    everywhere = stream_positions(block_deal[0], BLK)
    every_seq = sequence_ids(everywhere, seq_lengths[0])
    own_pos = lax.dynamic_slice_in_dim(everywhere, device * rows_here, rows_here, 0)
    own_seq = lax.dynamic_slice_in_dim(every_seq, device * rows_here, rows_here, 0)
    choice_rows = jnp.arange(2 * rows_here, dtype=jnp.int32) // 2
    expert_ids = jnp.arange(experts, dtype=jnp.int32)

    def block_mask(start, count):
        key_pos = lax.dynamic_slice_in_dim(everywhere, start, count, 0)
        key_seq = lax.dynamic_slice_in_dim(every_seq, start, count, 0)
        return (own_seq[:, None] == key_seq[None, :]) & (key_pos[None, :] <= own_pos[:, None])

    hidden_state = tokens[0].astype(jnp.float32)
    saved = []
    for layer in range(layers):
        shared = (
            lax.all_gather(attention_gain[layer], "wt", axis=0, tiled=True),
            lax.all_gather(query_weight[layer], "wt", axis=0, tiled=True),
            lax.all_gather(key_weight[layer], "wt", axis=0, tiled=True),
            lax.all_gather(value_weight[layer], "wt", axis=0, tiled=True),
            lax.all_gather(out_weight[layer], "wt", axis=0, tiled=True),
            lax.all_gather(mixture_gain[layer], "wt", axis=0, tiled=True),
            lax.all_gather(router_weight[layer], "wt", axis=0, tiled=True),
        )
        gain_one, full_query, full_key, full_value, full_out, gain_two, full_router = shared
        normed = rms_scale(hidden_state, gain_one.astype(jnp.float32)).astype(jnp.bfloat16)
        queries = jnp.dot(normed, full_query, preferred_element_type=jnp.float32).astype(
            jnp.bfloat16
        )
        keys = jnp.dot(normed, full_key, preferred_element_type=jnp.float32).astype(jnp.bfloat16)
        values = jnp.dot(normed, full_value, preferred_element_type=jnp.float32).astype(
            jnp.bfloat16
        )
        query_heads = queries.reshape(rows_here, kv_groups, per_group, head_size)
        start_state = (
            jnp.full((kv_groups, per_group, rows_here), NEG, jnp.float32),
            jnp.zeros((kv_groups, per_group, rows_here), jnp.float32),
            jnp.zeros((kv_groups, per_group, rows_here, head_size), jnp.float32),
        )
        gathered = None
        key_piece = lax.all_gather(keys, "ctx", axis=0, tiled=True)
        value_piece = lax.all_gather(values, "ctx", axis=0, tiled=True)
        absorb_count = key_piece.shape[0]
        absorb_span = 512

        def turn(index, state):
            first = index * absorb_span
            key_block = lax.dynamic_slice_in_dim(key_piece, first, absorb_span, 0).reshape(
                absorb_span, kv_groups, head_size
            )
            value_block = lax.dynamic_slice_in_dim(value_piece, first, absorb_span, 0).reshape(
                absorb_span, kv_groups, head_size
            )
            allowed = block_mask(first, absorb_span)

            def work(state):
                top, total, summed = state
                scores = (
                    jnp.einsum(
                        "tgrd,kgd->grtk", query_heads, key_block, preferred_element_type=jnp.float32
                    )
                    * scale
                )
                scores = jnp.where(allowed[None, None], scores, NEG)
                top_new = jnp.maximum(top, jnp.max(scores, axis=-1))
                fade = jnp.exp(top - top_new)
                weights = jnp.where(allowed[None, None], jnp.exp(scores - top_new[..., None]), 0.0)
                total = total * fade + jnp.sum(weights, axis=-1)
                summed = summed * fade[..., None] + jnp.einsum(
                    "grtk,kgd->grtd",
                    weights.astype(jnp.bfloat16),
                    value_block,
                    preferred_element_type=jnp.float32,
                )
                return (top_new, total, summed)

            return lax.cond(jnp.any(allowed), work, unchanged, state)

        top, total, summed = lax.fori_loop(0, absorb_count // absorb_span, turn, start_state)
        attended = (summed / total[..., None]).transpose(2, 0, 1, 3).reshape(rows_here, width)
        log_total = top + jnp.log(total)
        attended_low = attended.astype(jnp.bfloat16)
        middle = hidden_state + jnp.dot(attended_low, full_out, preferred_element_type=jnp.float32)
        mixed_low = rms_scale(middle, gain_two.astype(jnp.float32)).astype(jnp.bfloat16)
        probs = jax.nn.softmax(
            jnp.dot(mixed_low, full_router, preferred_element_type=jnp.float32), axis=-1
        )
        chosen = routes[layer, 0]
        picked = jnp.take_along_axis(probs, chosen, axis=1)
        gates = picked / jnp.sum(picked, axis=1, keepdims=True)
        flat_choice = chosen.reshape(-1)
        onehot = (flat_choice[:, None] == expert_ids[None, :]).astype(jnp.int32)
        rank = jnp.sum((jnp.cumsum(onehot, axis=0) - onehot) * onehot, axis=1)
        slots = flat_choice * capacity + rank
        outgoing = (
            jnp.zeros((experts * capacity, width), jnp.bfloat16)
            .at[slots]
            .set(mixed_low[choice_rows])
            .reshape(experts, capacity, width)
        )
        arrived = lax.all_to_all(outgoing, "ctx", split_axis=0, concat_axis=0, tiled=True)
        expert_full = (
            lax.all_gather(gate_weight[layer, 0], "wt", axis=1, tiled=True),
            lax.all_gather(up_weight[layer, 0], "wt", axis=1, tiled=True),
            lax.all_gather(down_weight[layer, 0], "wt", axis=0, tiled=True),
        )
        gate_full, up_full, down_full = expert_full
        expert_rows = arrived.reshape(-1, width)
        gate_value = jnp.dot(expert_rows, gate_full, preferred_element_type=jnp.float32)
        up_value = jnp.dot(expert_rows, up_full, preferred_element_type=jnp.float32)
        inner = (jax.nn.silu(gate_value) * up_value).astype(jnp.bfloat16)
        produced = (
            jnp.dot(inner, down_full, preferred_element_type=jnp.float32)
            .astype(jnp.bfloat16)
            .reshape(experts, capacity, width)
        )
        returned = lax.all_to_all(produced, "ctx", split_axis=0, concat_axis=0, tiled=True)
        expert_out = (
            returned.reshape(-1, width)[slots].reshape(rows_here, 2, width).astype(jnp.float32)
        )
        saved.append(
            (
                hidden_state,
                shared,
                normed,
                query_heads,
                keys,
                values,
                gathered,
                attended,
                attended_low,
                log_total,
                middle,
                mixed_low,
                probs,
                chosen,
                picked,
                gates,
                slots,
                expert_full,
                expert_rows,
                gate_value,
                up_value,
                inner,
                expert_out,
            )
        )
        hidden_state = middle + jnp.sum(gates[:, :, None] * expert_out, axis=1)
    block_output = hidden_state.astype(jnp.bfloat16)[None]
    upstream = cotangent[0].astype(jnp.float32)
    collected = []
    for layer in reversed(range(layers)):
        (
            layer_input,
            shared,
            normed,
            query_heads,
            keys,
            values,
            gathered,
            attended,
            attended_low,
            log_total,
            middle,
            mixed_low,
            probs,
            chosen,
            picked,
            gates,
            slots,
            expert_full,
            expert_rows,
            gate_value,
            up_value,
            inner,
            expert_out,
        ) = saved[layer]
        gain_one, full_query, full_key, full_value, full_out, gain_two, full_router = shared
        gate_full, up_full, down_full = expert_full
        gate_signal = jnp.sum(upstream[:, None, :] * expert_out, axis=-1)
        back_rows = (
            (gates[:, :, None] * upstream[:, None, :]).astype(jnp.bfloat16).reshape(-1, width)
        )
        outgoing_grad = (
            jnp.zeros((experts * capacity, width), jnp.bfloat16)
            .at[slots]
            .set(back_rows)
            .reshape(experts, capacity, width)
        )
        arrived_grad = lax.all_to_all(
            outgoing_grad, "ctx", split_axis=0, concat_axis=0, tiled=True
        ).reshape(-1, width)
        grad_down = outer_rows(inner, arrived_grad)
        grad_inner = times_transposed(arrived_grad, down_full)
        sigma = jax.nn.sigmoid(gate_value)
        grad_gate_value = (
            grad_inner * up_value * sigma * (1.0 + gate_value * (1.0 - sigma))
        ).astype(jnp.bfloat16)
        grad_up_value = (grad_inner * gate_value * sigma).astype(jnp.bfloat16)
        grad_gate = outer_rows(expert_rows, grad_gate_value)
        grad_up = outer_rows(expert_rows, grad_up_value)
        grad_rows = (
            (
                times_transposed(grad_gate_value, gate_full)
                + times_transposed(grad_up_value, up_full)
            )
            .astype(jnp.bfloat16)
            .reshape(experts, capacity, width)
        )
        back_grad = lax.all_to_all(grad_rows, "ctx", split_axis=0, concat_axis=0, tiled=True)
        grad_mixed = jnp.sum(
            back_grad.reshape(-1, width)[slots].reshape(rows_here, 2, width).astype(jnp.float32),
            axis=1,
        )
        pair_total = jnp.sum(picked, axis=1, keepdims=True)
        grad_picked = (
            gate_signal - jnp.sum(gates * gate_signal, axis=1, keepdims=True)
        ) / pair_total
        grad_probs = jnp.sum(
            grad_picked[:, :, None]
            * (chosen[:, :, None] == expert_ids[None, None, :]).astype(jnp.float32),
            axis=1,
        )
        grad_logits = probs * (grad_probs - jnp.sum(probs * grad_probs, axis=1, keepdims=True))
        grad_router = lax.dot_general(
            mixed_low.astype(jnp.float32),
            grad_logits,
            (((0,), (0,)), ((), ())),
            precision=lax.Precision.HIGHEST,
            preferred_element_type=jnp.float32,
        )
        grad_mixed = grad_mixed + lax.dot_general(
            grad_logits,
            full_router.astype(jnp.float32),
            (((1,), (1,)), ((), ())),
            precision=lax.Precision.HIGHEST,
            preferred_element_type=jnp.float32,
        )
        norm_value, pull_two = jax.vjp(rms_scale, middle, gain_two.astype(jnp.float32))
        grad_middle_norm, grad_gain_two = pull_two(grad_mixed)
        grad_middle = upstream + grad_middle_norm
        middle_low = grad_middle.astype(jnp.bfloat16)
        grad_out = outer_rows(attended_low, middle_low)
        grad_attended = times_transposed(middle_low, full_out).astype(jnp.bfloat16)
        grad_heads = grad_attended.reshape(rows_here, kv_groups, per_group, head_size)
        attended_heads = attended.reshape(rows_here, kv_groups, per_group, head_size)
        delta = jnp.sum(grad_heads.astype(jnp.float32) * attended_heads, axis=-1).transpose(1, 2, 0)
        whole = (
            lax.all_gather(keys, "ctx", axis=0, tiled=True),
            lax.all_gather(values, "ctx", axis=0, tiled=True),
        )
        key_all, value_all = whole
        total_rows = key_all.shape[0]
        span = 512

        def score_block(first, count, allowed):
            key_block = lax.dynamic_slice_in_dim(key_all, first, count, 0).reshape(
                count, kv_groups, head_size
            )
            value_block = lax.dynamic_slice_in_dim(value_all, first, count, 0).reshape(
                count, kv_groups, head_size
            )
            scores = (
                jnp.einsum(
                    "tgrd,kgd->grtk", query_heads, key_block, preferred_element_type=jnp.float32
                )
                * scale
            )
            probs_block = jnp.where(
                allowed[None, None], jnp.exp(scores - log_total[..., None]), 0.0
            )
            grad_probs_block = jnp.einsum(
                "tgrd,kgd->grtk", grad_heads, value_block, preferred_element_type=jnp.float32
            )
            grad_scores = (probs_block * (grad_probs_block - delta[..., None])).astype(jnp.bfloat16)
            return (key_block, probs_block, grad_scores)

        def key_terms(probs_block, grad_scores, count):
            key_part = (
                jnp.einsum(
                    "grtk,tgrd->kgd", grad_scores, query_heads, preferred_element_type=jnp.float32
                )
                * scale
            ).reshape(count, kv_width)
            value_part = jnp.einsum(
                "grtk,tgrd->kgd",
                probs_block.astype(jnp.bfloat16),
                grad_heads,
                preferred_element_type=jnp.float32,
            ).reshape(count, kv_width)
            return (key_part, value_part)

        query_start = jnp.zeros((rows_here, kv_groups, per_group, head_size), jnp.float32)

        def turn_back(index, state):
            first = index * span
            allowed = block_mask(first, span)

            def work(state):
                grad_query, grad_keys, grad_values = state
                key_block, probs_block, grad_scores = score_block(first, span, allowed)
                grad_query = (
                    grad_query
                    + jnp.einsum(
                        "grtk,kgd->tgrd", grad_scores, key_block, preferred_element_type=jnp.float32
                    )
                    * scale
                )
                key_part, value_part = key_terms(probs_block, grad_scores, span)
                grad_keys = lax.dynamic_update_slice_in_dim(grad_keys, key_part, first, 0)
                grad_values = lax.dynamic_update_slice_in_dim(grad_values, value_part, first, 0)
                return (grad_query, grad_keys, grad_values)

            return lax.cond(jnp.any(allowed), work, unchanged, state)

        back_start = (
            query_start,
            jnp.zeros((total_rows, kv_width), jnp.float32),
            jnp.zeros((total_rows, kv_width), jnp.float32),
        )
        grad_query, grad_keys, grad_values = lax.fori_loop(
            0, total_rows // span, turn_back, back_start
        )
        grad_keys, grad_values = (
            lax.psum_scatter(
                grad_keys.astype(jnp.bfloat16), "ctx", scatter_dimension=0, tiled=True
            ).astype(jnp.float32),
            lax.psum_scatter(
                grad_values.astype(jnp.bfloat16), "ctx", scatter_dimension=0, tiled=True
            ).astype(jnp.float32),
        )
        query_low = grad_query.reshape(rows_here, width).astype(jnp.bfloat16)
        key_low = grad_keys.astype(jnp.bfloat16)
        value_low = grad_values.astype(jnp.bfloat16)
        grad_query_weight = outer_rows(normed, query_low)
        grad_key_weight = outer_rows(normed, key_low)
        grad_value_weight = outer_rows(normed, value_low)
        grad_normed = (
            times_transposed(query_low, full_query)
            + times_transposed(key_low, full_key)
            + times_transposed(value_low, full_value)
        )
        norm_value, pull_one = jax.vjp(rms_scale, layer_input, gain_one.astype(jnp.float32))
        grad_input_norm, grad_gain_one = pull_one(grad_normed)
        upstream = grad_middle + grad_input_norm
        part_one, part_query, part_key, part_value, part_out, part_two, part_router = (
            lax.psum_scatter(
                grad_gain_one.astype(jnp.bfloat16), "wt", scatter_dimension=0, tiled=True
            ).astype(jnp.float32),
            lax.psum_scatter(
                grad_query_weight.astype(jnp.bfloat16), "wt", scatter_dimension=0, tiled=True
            ).astype(jnp.float32),
            lax.psum_scatter(
                grad_key_weight.astype(jnp.bfloat16), "wt", scatter_dimension=0, tiled=True
            ).astype(jnp.float32),
            lax.psum_scatter(
                grad_value_weight.astype(jnp.bfloat16), "wt", scatter_dimension=0, tiled=True
            ).astype(jnp.float32),
            lax.psum_scatter(
                grad_out.astype(jnp.bfloat16), "wt", scatter_dimension=0, tiled=True
            ).astype(jnp.float32),
            lax.psum_scatter(
                grad_gain_two.astype(jnp.bfloat16), "wt", scatter_dimension=0, tiled=True
            ).astype(jnp.float32),
            lax.psum_scatter(
                grad_router.astype(jnp.bfloat16), "wt", scatter_dimension=0, tiled=True
            ).astype(jnp.float32),
        )
        summed_parts = (
            lax.psum(part_one.astype(jnp.bfloat16), "ctx").astype(jnp.float32),
            lax.psum(part_query.astype(jnp.bfloat16), "ctx").astype(jnp.float32),
            lax.psum(part_key.astype(jnp.bfloat16), "ctx").astype(jnp.float32),
            lax.psum(part_value.astype(jnp.bfloat16), "ctx").astype(jnp.float32),
            lax.psum(part_out.astype(jnp.bfloat16), "ctx").astype(jnp.float32),
            lax.psum(part_two.astype(jnp.bfloat16), "ctx").astype(jnp.float32),
            lax.psum(part_router.astype(jnp.bfloat16), "ctx").astype(jnp.float32),
        )
        expert_parts = (
            lax.psum_scatter(
                grad_gate.astype(jnp.bfloat16), "wt", scatter_dimension=1, tiled=True
            ).astype(jnp.float32),
            lax.psum_scatter(
                grad_up.astype(jnp.bfloat16), "wt", scatter_dimension=1, tiled=True
            ).astype(jnp.float32),
            lax.psum_scatter(
                grad_down.astype(jnp.bfloat16), "wt", scatter_dimension=0, tiled=True
            ).astype(jnp.float32),
        )
        collected.append((summed_parts, expert_parts))
    ordered = collected[::-1]
    attention_gain_grad = jnp.stack([item[0][0] for item in ordered])
    query_grad = jnp.stack([item[0][1] for item in ordered])
    key_grad = jnp.stack([item[0][2] for item in ordered])
    value_grad = jnp.stack([item[0][3] for item in ordered])
    out_grad = jnp.stack([item[0][4] for item in ordered])
    mixture_gain_grad = jnp.stack([item[0][5] for item in ordered])
    router_grad = jnp.stack([item[0][6] for item in ordered])
    gate_grad = jnp.stack([item[1][0] for item in ordered])[:, None]
    up_grad = jnp.stack([item[1][1] for item in ordered])[:, None]
    down_grad = jnp.stack([item[1][2] for item in ordered])[:, None]
    return (
        block_output,
        upstream[None],
        attention_gain_grad,
        query_grad,
        key_grad,
        value_grad,
        out_grad,
        mixture_gain_grad,
        router_grad,
        gate_grad,
        up_grad,
        down_grad,
    )


def solution(mesh):
    placed = (
        P("wt", "ctx", None),
        P("wt", "ctx", None),
        P("wt", None),
        P("wt", None, None),
        P(None, "wt", "ctx", None),
        P(None, "wt"),
        P(None, "wt", None),
        P(None, "wt", None),
        P(None, "wt", None),
        P(None, "wt", None),
        P(None, "wt"),
        P(None, "wt", None),
        P(None, "ctx", None, "wt"),
        P(None, "ctx", None, "wt"),
        P(None, "ctx", "wt", None),
    )
    def local(*arrays):
        if by_heads(mesh, *arrays):
            return local_heads(mesh, *arrays)
        return local_rows(*arrays)

    return jax.shard_map(
        local,
        mesh=mesh,
        in_specs=placed,
        out_specs=(
            P("wt", "ctx", None),
            P("wt", "ctx", None),
            P(None, "wt"),
            P(None, "wt", None),
            P(None, "wt", None),
            P(None, "wt", None),
            P(None, "wt", None),
            P(None, "wt"),
            P(None, "wt", None),
            P(None, "ctx", None, "wt"),
            P(None, "ctx", None, "wt"),
            P(None, "ctx", "wt", None),
        ),
        check_vma=False,
    )
```
